256 devices in a mesh: seq: 128 (over y, x, z), chan: 2 (over core).
Axes of the slice: x: 4, y: 4, z: 8, core: 2. Of those that a mesh axis runs over, the one named last changes fastest.
Arguments:
- query_proj: float32 [4096, 32768], P('chan', 'seq'), may hold values from -6 to 6
- key_proj: float32 [4096, 32768], P('chan', 'seq'), may hold values from -6 to 6
- value_proj: float32 [4096, 32768], P('chan', 'seq'), may hold values from -6 to 6
- second_query: float32 [4096, 32768], P('chan', 'seq'), may hold values from -6 to 6
- second_key: float32 [4096, 32768], P('chan', 'seq'), may hold values from -6 to 6
- short_filter: float32 [3, 4096, 3], P(None, 'chan'), may hold values from -3 to 3
- second_short: float32 [3, 4096, 3], P(None, 'chan'), may hold values from -3 to 3
- medium_filter: float32 [4096, 128], P('chan'), may hold values from -0.5 to 0.5
- decay_rate: float32 [4096, 8], P('chan'), may hold values from 6.1035156e-06 to 0.0333333333, as said below
- residue: float32 [4096, 8], P('chan'), may hold values from -1.5 to 1.5
- skip_gain: float32 [4096], P('chan'), may hold values from -1 to 1
- norm_gain: float32 [4096], P('chan'), may hold values from 0.1 to 1.9
Outputs:
- normalized: float32 [4096, 32768], P('chan', 'seq')
The draws below stay inside these ranges and needn't reach their ends.
Inputs may be any that keep to these rules, and one draw needn't show every extreme that they name: `decay_rate`: positive decay rates, one for each channel and mode.
All inputs are finite; a program needn't handle non-finite values.
Results may differ from the reference program's by a relative error of at most 0.0003.
Values sent between devices are 32-bit elements; how exact they have to be, the bound alone decides.
No kernel may reach another device: no remote copies, remote signals or barrier semaphores. Data moves between devices by JAX's collectives and lax.ppermute only.
A program may use at most 128 MiB of HBM per device.

```python
import math
import jax
import jax.numpy as jnp
from jax import lax

D = 4096
MTAPS = 128
STAPS = 3
MODES = 8
TOK_DEV = 256
TOKENS = 32768


def draw_decay_rate(key, part):
    key = jax.random.fold_in(key, 11)
    key_pick, key_slow, key_fast = jax.random.split(key, 3)
    share = 0.5
    picked = jax.random.uniform(key_pick, (D, MODES), jnp.float32)
    slow_lo = math.log(0.2 / TOKENS)
    slow_hi = math.log(2.0 / TOKENS)
    fast_lo = math.log(1.0 / (4 * TOK_DEV))
    fast_hi = math.log(1.0 / 30.0)
    slow = jnp.exp(slow_lo + jax.random.uniform(key_slow, (D, MODES), jnp.float32) * (slow_hi - slow_lo))
    fast = jnp.exp(fast_lo + jax.random.uniform(key_fast, (D, MODES), jnp.float32) * (fast_hi - fast_lo))
    return jnp.where(picked < share, slow, fast).astype(jnp.float32)


def steps_of(rng, extent, shards, least, high):
    loudness, own = 1.0, jax.random.fold_in(rng, 6)
    for dim, shards_of in shards:
        draws = jnp.exp(jax.random.uniform(jax.random.fold_in(own, dim), (shards_of,), jnp.float32, least / len(shards), high / len(shards)))
        loudness = loudness * jnp.repeat(draws, extent[dim] // shards_of).reshape([-1 if axis == dim else 1 for axis in range(len(extent))])
    return loudness


def bell_draw(rng, extent, scale, bound, cuts=(), held_as=jnp.bfloat16):
    level = steps_of(rng, extent, cuts, -0.22, 0.18) if cuts else 1.0
    values = jax.random.normal(rng, extent, jnp.float32) * scale * level
    return jnp.minimum(jnp.maximum(values, -bound), bound).astype(held_as)


def setup_inputs(seed: int = 0) -> dict:
    key_list = jax.random.split(jax.random.key(seed), 13)
    query_proj = bell_draw(key_list[0], (D, TOKENS), 1.0, 6.0, ((0, 2), (1, 128)), jnp.float32)
    key_proj = bell_draw(key_list[1], (D, TOKENS), 1.0, 6.0, ((0, 2), (1, 128)), jnp.float32)
    value_proj = bell_draw(key_list[2], (D, TOKENS), 1.0, 6.0, ((0, 2), (1, 128)), jnp.float32)
    second_query = bell_draw(key_list[3], (D, TOKENS), 1.0, 6.0, ((0, 2), (1, 128)), jnp.float32)
    second_key = bell_draw(key_list[4], (D, TOKENS), 1.0, 6.0, ((0, 2), (1, 128)), jnp.float32)
    short_filter = bell_draw(key_list[5], (3, D, STAPS), 0.6, 3.0, ((1, 2),), jnp.float32)
    second_short = bell_draw(key_list[6], (3, D, STAPS), 0.6, 3.0, ((1, 2),), jnp.float32)
    medium_filter = bell_draw(key_list[7], (D, MTAPS), MTAPS ** -0.5, 0.5, ((0, 2),), jnp.float32)
    decay_rate = draw_decay_rate(jax.random.fold_in(key_list[12], 71), 0)
    residue = bell_draw(key_list[9], (D, MODES), 0.25, 1.5, ((0, 2),), jnp.float32)
    skip_gain = jnp.clip(jax.random.uniform(key_list[10], (D,), jnp.float32, -1.0, 1.0) * steps_of(key_list[10], (D,), ((0, 2),), -0.4, 0.0), -1.0, 1.0)
    norm_gain = jnp.clip(1.0 + 0.18 * jax.random.normal(key_list[11], (D,), jnp.float32), 0.1, 1.9)
    return dict(query_proj=query_proj, key_proj=key_proj, value_proj=value_proj, second_query=second_query, second_key=second_key, short_filter=short_filter, second_short=second_short, medium_filter=medium_filter, decay_rate=decay_rate, residue=residue, skip_gain=skip_gain, norm_gain=norm_gain)


norm_eps = 1e-06

def valid_taps(extended, taps):
    span = taps.shape[-1]
    length = extended.shape[-1] - span + 1
    total = taps[..., 0:1] * extended[..., span - 1:span - 1 + length]
    for offset in range(1, span):
        total = total + taps[..., offset:offset + 1] * extended[..., span - 1 - offset:span - 1 - offset + length]
    return total

def depthwise(extended, kernel):
    return lax.conv_general_dilated(extended[None], kernel[:, None, ::-1], (1,), 'VALID', dimension_numbers=('NCH', 'OIH', 'NCH'), feature_group_count=kernel.shape[0], precision=lax.Precision.HIGHEST)[0]

def filtered(items):
    query_grp, key_grp, value_grp, query_two, key_two, short_grp, second_grp, medium_grp, rates, residues, skips = items
    lead = short_grp.shape[-1] - 1
    padding = ((0, 0), (lead, 0))
    query_feat = valid_taps(jnp.pad(query_grp, padding), short_grp[0])
    key_feat = valid_taps(jnp.pad(key_grp, padding), short_grp[1])
    value_feat = valid_taps(jnp.pad(value_grp, padding), short_grp[2])
    gated = key_feat * value_feat
    medium_out = depthwise(jnp.pad(gated, ((0, 0), (MTAPS - 1, 0))), medium_grp)
    first_out = query_feat * medium_out
    query2_feat = valid_taps(jnp.pad(query_two, padding), second_grp[0])
    key2_feat = valid_taps(jnp.pad(key_two, padding), second_grp[1])
    value2_feat = valid_taps(jnp.pad(first_out, padding), second_grp[2])
    second_gated = key2_feat * value2_feat
    amplitude = residues * jnp.sqrt(-jnp.expm1(-2.0 * rates))
    lag_steps = jnp.arange(TOKENS, dtype=jnp.float32)
    response = jnp.zeros((query_grp.shape[0], TOKENS), jnp.float32)
    for mode in range(MODES):
        response = response + amplitude[:, mode:mode + 1] * jnp.exp(-rates[:, mode:mode + 1] * lag_steps)
    size_fft = 2 * TOKENS
    spectrum = jnp.fft.rfft(second_gated, n=size_fft) * jnp.fft.rfft(response, n=size_fft)
    long_out = jnp.fft.irfft(spectrum, n=size_fft)[:, :TOKENS]
    return query2_feat * (long_out + skips[:, None] * second_gated)

def reference(query_proj, key_proj, value_proj, second_query, second_key, short_filter, second_short, medium_filter, decay_rate, residue, skip_gain, norm_gain):
    width = 64
    groups = D // width
    span = short_filter.shape[-1]
    items = (query_proj.reshape(groups, width, TOKENS), key_proj.reshape(groups, width, TOKENS), value_proj.reshape(groups, width, TOKENS), second_query.reshape(groups, width, TOKENS), second_key.reshape(groups, width, TOKENS), jnp.transpose(short_filter.reshape(3, groups, width, span), (1, 0, 2, 3)), jnp.transpose(second_short.reshape(3, groups, width, span), (1, 0, 2, 3)), medium_filter.reshape(groups, width, MTAPS), decay_rate.reshape(groups, width, MODES), residue.reshape(groups, width, MODES), skip_gain.reshape(groups, width))
    mixed = lax.map(filtered, items).reshape(D, TOKENS)
    mean_square = lax.optimization_barrier(jnp.mean(mixed * mixed, axis=0))
    return mixed * lax.rsqrt(mean_square + norm_eps)[None, :] * norm_gain[:, None]
```

```python
import jax
import jax.numpy as jnp
import ml_dtypes
import numpy as np
from jax import lax
from jax.experimental import pallas as pl
from jax.experimental.pallas import tpu as pltpu
from jax.sharding import PartitionSpec as P

norm_eps = 1e-06

T = 256
TAPS = 128
MODES = 8
LANES = 128
SEG = 8
HEAD = 17
MAIN = 15
HEAD_ROWS = HEAD * SEG
MAIN_ROWS = MAIN * SEG
RIMS = 16
LIMIT = 48 * 1024 * 1024

F32 = jnp.float32
BF16 = jnp.bfloat16


def row_times():
    head = [HEAD * i + k for k in range(HEAD) for i in range(SEG)]
    main = [HEAD_ROWS + MAIN * i + k for k in range(MAIN) for i in range(SEG)]
    return np.array(head + main)


def packed_forward(slots):
    k = np.arange(128)[:, None]
    angle = 2.0 * np.pi * k * np.asarray(slots)[None, :] / 256.0
    imag = -np.sin(angle)
    imag[0] = np.cos(np.pi * np.asarray(slots))
    return np.concatenate([np.cos(angle), imag], 0)


def packed_inverse(slots):
    k = np.arange(128)[None, :]
    angle = 2.0 * np.pi * k * np.asarray(slots)[:, None] / 256.0
    real = 2.0 * np.cos(angle)
    real[:, 0] = 1.0
    imag = -2.0 * np.sin(angle)
    imag[:, 0] = np.cos(np.pi * np.asarray(slots))
    return np.concatenate([real, imag], 1) / 256.0


def three_pass(matrix):
    high = matrix.astype(ml_dtypes.bfloat16)
    low = (matrix - high.astype(np.float64)).astype(ml_dtypes.bfloat16)
    return np.concatenate([high, low, high], 1)


def tables():
    times = row_times()
    first = packed_forward(times + 128) * (times < 128)[None, :]
    second = packed_forward(times)
    forward = np.concatenate([first, second], 0)
    taps = packed_forward(np.arange(TAPS))
    real, imag = taps[:128], taps[128:].copy()
    cross = real.copy()
    cross[0] = imag[0]
    imag[0] = 0.0
    spectrum = np.concatenate([real, imag, cross], 0)
    inverse = np.concatenate(
        [
            packed_inverse(times + 128) * (times < 128)[:, None],
            packed_inverse(times) * (times >= 128)[:, None],
        ],
        1,
    )
    halo = packed_forward(np.arange(128))
    halo[:, 0] = 0.0
    head_times = np.concatenate([times[:HEAD_ROWS], np.full(8, 255)])
    halo_back = packed_inverse(head_times + 128) * (head_times < 128)[:, None]
    return [three_pass(m) for m in (forward, spectrum, inverse, halo, halo_back)]


def halves(x):
    high = x.astype(BF16)
    low = (x - high.astype(F32)).astype(BF16)
    return high, low


def matmul3(matrix, x):
    high, low = halves(x)
    stacked = jnp.concatenate([high, high, low], 0)
    return jnp.dot(matrix, stacked, preferred_element_type=F32)


def spectral_product(x, taps):
    real, imag = x[:128], x[128:]
    tap_real, tap_imag, tap_cross = taps[:128], taps[128:256], taps[256:]
    return jnp.concatenate(
        [real * tap_real - imag * tap_imag, real * tap_imag + imag * tap_cross], 0
    )


def sublane(shape):
    return lax.broadcasted_iota(jnp.int32, shape, 0)


def down(x, distance=1):
    return pltpu.roll(x, distance, axis=0)


def fir3(slabs, taps):
    return [
        taps[0] * slabs[k + 2] + taps[1] * slabs[k + 1] + taps[2] * slabs[k]
        for k in range(len(slabs) - 2)
    ]


def with_rims(head, main, rims=None):
    top = sublane(head[0].shape) == 0
    zero = jnp.zeros_like(head[0])
    before = (zero, zero) if rims is None else rims
    ends = [down(head[HEAD - 2]), down(head[HEAD - 1])]
    head_all = [jnp.where(top, before[k], ends[k]) for k in range(2)] + head
    if main is None:
        return head_all, None
    main_all = [jnp.where(top, ends[k], down(main[MAIN - 2 + k])) for k in range(2)] + main
    return head_all, main_all


def rows_of(ref, k, lanes):
    return ref[pl.ds(SEG * k, SEG), lanes]


def spread(row):
    return jnp.broadcast_to(row, (SEG, row.shape[1]))


def recurrence(inputs, decays, gains, skip):
    states = [gains[r] * inputs[0] for r in range(MODES)]
    outs = []
    for k, value in enumerate(inputs):
        if k:
            states = [decays[r] * states[r] + gains[r] * value for r in range(MODES)]
        total = skip * value
        for state in states:
            total = total + state
        outs.append(total)
    return outs, states


def prefix(state, rate, step):
    place = sublane(state.shape)
    total = state
    for distance in (1, 2, 4):
        moved = jnp.where(place >= distance, down(total, distance), 0.0)
        total = total + jnp.exp(-(step * distance) * rate) * moved
    return jnp.where(place >= 1, down(total), 0.0), total[SEG - 1 :]


def tail_kernel(key_ref, value_ref, short_ref, tail_ref, taps_ref):
    taps_ref[...] = jnp.zeros_like(taps_ref)
    taps_ref[0:3, :] = short_ref[1]
    taps_ref[3:6, :] = short_ref[2]
    columns = taps_ref[...].T
    lane = lax.broadcasted_iota(jnp.int32, (key_ref.shape[0], LANES), 1)

    def feature(ref, first):
        here = ref[:, LANES:]
        back_two = jnp.where(lane == LANES - 1, ref[:, :LANES], here)
        return (
            columns[:, first : first + 1] * here
            + columns[:, first + 1 : first + 2] * pltpu.roll(here, 1, axis=1)
            + columns[:, first + 2 : first + 3] * pltpu.roll(back_two, 2, axis=1)
        )

    tail_ref[...] = feature(key_ref, 0) * feature(value_ref, 3)


def local_kernel(
    key_ref,
    value_ref,
    query_ref,
    query2_ref,
    key2_ref,
    short_ref,
    second_ref,
    medium_ref,
    rate_ref,
    amplitude_ref,
    skip_ref,
    forward_ref,
    spectrum_ref,
    inverse_ref,
    taps_out,
    spectrum_out,
    medium_out,
    query_out,
    key2_out,
    query2_out,
    own_out,
    enter_out,
    leave_out,
    first_rows_out,
    rims_out,
    key_t,
    value_t,
    query_t,
    query2_t,
    key2_t,
    taps_t,
    gated_t,
    medium_t,
):
    width = key_ref.shape[0]
    chunks = [pl.ds(LANES * part, LANES) for part in range(width // LANES)]
    first_rows_out[...] = jnp.zeros_like(first_rows_out)
    rims_out[...] = jnp.zeros_like(rims_out)
    for part, lanes in enumerate(chunks):
        for place, (ref, turned) in enumerate(
            (
                (key_ref, key_t),
                (value_ref, value_t),
                (query_ref, query_t),
                (query2_ref, query2_t),
                (key2_ref, key2_t),
            )
        ):
            turned[part] = ref[lanes, :].T
            rims_out[2 * place : 2 * place + 2, lanes] = turned[part, T - 2 : T, :]
            if place < 2:
                first_rows_out[2 * place : 2 * place + 2, lanes] = turned[part, 0:2, :]
        taps_t[part, 0:TAPS, :] = medium_ref[lanes, :].T
        taps_t[part, TAPS:HEAD_ROWS, :] = jnp.zeros((HEAD_ROWS - TAPS, LANES), F32)
        for k in range(HEAD):
            taps_out[pl.ds(SEG * k, SEG), lanes] = taps_t[part, pl.ds(k, SEG, stride=HEAD), :]

    def slabs_of(ref, part):
        head = [ref[part, pl.ds(k, SEG, stride=HEAD), :] for k in range(HEAD)]
        main = [ref[part, pl.ds(HEAD_ROWS + k, SEG, stride=MAIN), :] for k in range(MAIN)]
        return head, main

    def feature(ref, part, taps_of, index, lanes):
        taps = [spread(taps_of[index, j : j + 1, lanes]) for j in range(3)]
        head, main = with_rims(*slabs_of(ref, part))
        return fir3(head, taps) + fir3(main, taps)

    top = sublane((SEG, LANES)) == 0
    for part, lanes in enumerate(chunks):
        keys = feature(key_t, part, short_ref, 1, lanes)
        values = feature(value_t, part, short_ref, 2, lanes)
        for k in range(HEAD + MAIN):
            gated = keys[k] * values[k]
            if k < 2:
                gated = jnp.where(top, 0.0, gated)
            gated_t[pl.ds(SEG * k, SEG), lanes] = gated
        for ref, taps_of, index, out in (
            (query_t, short_ref, 0, query_out),
            (query2_t, second_ref, 0, query2_out),
            (key2_t, second_ref, 1, key2_out),
        ):
            for k, slab in enumerate(feature(ref, part, taps_of, index, lanes)):
                out[pl.ds(SEG * k, SEG), lanes] = slab

    turned = [taps_t[part, 0:TAPS, :] for part in range(len(chunks))]
    spectrum = matmul3(spectrum_ref[...], jnp.concatenate(turned, 1))
    spectrum_out[...] = spectrum
    both = matmul3(forward_ref[...], gated_t[...])
    first = spectral_product(both[:T], spectrum)
    second = spectral_product(both[T:], spectrum)
    medium_t[...] = matmul3(inverse_ref[...], jnp.concatenate([first, second], 0))
    medium_out[...] = medium_t[0:HEAD_ROWS, :]

    for lanes in chunks:
        taps = [spread(second_ref[2, j : j + 1, lanes]) for j in range(3)]
        firsts = [
            rows_of(medium_t, k, lanes) * rows_of(query_out, k, lanes)
            for k in range(HEAD - 2, HEAD + MAIN)
        ]
        ends = [down(firsts[0]), down(firsts[1])]
        main = firsts[2:]
        main_all = [jnp.where(top, ends[k], down(main[MAIN - 2 + k])) for k in range(2)] + main
        rims_out[10:11, lanes] = main[MAIN - 2][SEG - 1 :]
        rims_out[11:12, lanes] = main[MAIN - 1][SEG - 1 :]
        values2 = fir3(main_all, taps)
        inputs = [
            rows_of(key2_out, HEAD + k, lanes) * values2[k] for k in range(MAIN)
        ]
        rates, gains = rate_ref[:, lanes], amplitude_ref[:, lanes]
        decays = jnp.exp(-rates)
        outs, ends = recurrence(
            inputs,
            [spread(decays[r : r + 1]) for r in range(MODES)],
            [spread(gains[r : r + 1]) for r in range(MODES)],
            spread(skip_ref[:, lanes]),
        )
        for k in range(MAIN):
            own_out[pl.ds(SEG * k, SEG), lanes] = outs[k]
        for r in range(MODES):
            enter, leave = prefix(ends[r], spread(rates[r : r + 1]), float(MAIN))
            enter_out[r, :, lanes] = enter
            leave_out[r : r + 1, lanes] = leave


def join_kernel(
    halo_ref,
    rims_ref,
    spectrum_ref,
    medium_ref,
    taps_ref,
    query_ref,
    key2_ref,
    first_rows_ref,
    enter_main_ref,
    leave_main_ref,
    short_ref,
    second_ref,
    rate_ref,
    amplitude_ref,
    skip_ref,
    forward_ref,
    inverse_ref,
    own_out,
    enter_out,
    enter_main_out,
    state_out,
    medium_t,
):
    width = halo_ref.shape[0]
    high, low = halves(halo_ref[...])
    stacked = jnp.concatenate([high, high, low], 1)
    halo = lax.dot_general(
        forward_ref[...], stacked, (((1,), (1,)), ((), ())), preferred_element_type=F32
    )
    product = spectral_product(halo, spectrum_ref[...])
    medium_t[...] = matmul3(inverse_ref[...], product)

    top = sublane((SEG, LANES)) == 0
    for part in range(width // LANES):
        lanes = pl.ds(LANES * part, LANES)

        def rim(k):
            return rims_ref[k : k + 1, lanes]

        def first(k):
            return first_rows_ref[k : k + 1, lanes]

        def taps_of(ref, index):
            return [ref[index, j : j + 1, lanes] for j in range(3)]

        def early(place, index):
            taps = taps_of(short_ref, index)
            zero, one = first(2 * place), first(2 * place + 1)
            older, last = rim(2 * place), rim(2 * place + 1)
            return (
                taps[0] * zero + taps[1] * last + taps[2] * older,
                taps[0] * one + taps[1] * zero + taps[2] * last,
            )

        def mended(ref, place, taps):
            slabs = [rows_of(ref, k, lanes) for k in range(HEAD)]
            older, last = rim(2 * place), rim(2 * place + 1)
            slabs[0] = slabs[0] + jnp.where(top, spread(taps[1] * last + taps[2] * older), 0.0)
            slabs[1] = slabs[1] + jnp.where(top, spread(taps[2] * last), 0.0)
            return slabs

        keys, values = early(0, 1), early(1, 2)
        gated = [spread(keys[k] * values[k]) for k in range(2)]
        taps = [rows_of(taps_ref, k, lanes) for k in range(HEAD)]
        shifted = [jnp.where(top, 0.0, down(taps[HEAD - 1]))] + taps
        query = mended(query_ref, 2, taps_of(short_ref, 0))
        key2 = mended(key2_ref, 4, taps_of(second_ref, 1))
        firsts = [
            query[k]
            * (
                rows_of(medium_ref, k, lanes)
                + rows_of(medium_t, k, lanes)
                + taps[k] * gated[0]
                + shifted[k] * gated[1]
            )
            for k in range(HEAD)
        ]
        firsts_all, _ = with_rims(firsts, None, (spread(rim(10)), spread(rim(11))))
        values2 = fir3(firsts_all, [spread(t) for t in taps_of(second_ref, 2)])
        inputs = [key2[k] * values2[k] for k in range(HEAD)]
        rates, gains = rate_ref[:, lanes], amplitude_ref[:, lanes]
        decays = jnp.exp(-rates)
        outs, ends = recurrence(
            inputs,
            [spread(decays[r : r + 1]) for r in range(MODES)],
            [spread(gains[r : r + 1]) for r in range(MODES)],
            spread(skip_ref[:, lanes]),
        )
        for k in range(HEAD):
            own_out[pl.ds(SEG * k, SEG), lanes] = outs[k]
        segment = sublane((SEG, LANES)).astype(F32)
        for r in range(MODES):
            rate = spread(rates[r : r + 1])
            enter, leave = prefix(ends[r], rate, float(HEAD))
            enter_out[r, :, lanes] = enter
            enter_main_out[r, :, lanes] = enter_main_ref[r, :, lanes] + jnp.exp(
                -(rate * (segment * float(MAIN)))
            ) * spread(leave)
            state_out[part, r : r + 1, :] = leave_main_ref[r : r + 1, lanes] + leave * jnp.exp(
                -float(MAIN_ROWS) * rates[r : r + 1]
            )


def scan_kernel(state_ref, rate_ref, out_ref):
    blocks = state_ref.shape[0]
    place = sublane(state_ref.shape)
    rate = rate_ref[...]
    total = state_ref[...]
    distance = 1
    while distance < blocks:
        moved = jnp.where(place >= distance, down(total, distance), 0.0)
        total = total + jnp.exp(-(float(T) * distance) * rate) * moved
        distance *= 2
    out_ref[...] = jnp.where(place >= 1, down(total), 0.0)


def finish_kernel(
    state_ref,
    own_head_ref,
    own_main_ref,
    enter_head_ref,
    enter_main_ref,
    query2_ref,
    rims_ref,
    second_ref,
    rate_ref,
    gain_ref,
    mixed_out,
    squares_out,
    squares_t,
):
    step = pl.program_id(0)
    width = query2_ref.shape[1]

    @pl.when(step == 0)
    def _():
        squares_t[...] = jnp.zeros_like(squares_t)

    top = sublane((SEG, LANES)) == 0
    segment = sublane((SEG, LANES)).astype(F32)
    for part in range(width // LANES):
        lanes = pl.ds(LANES * part, LANES)
        rates = rate_ref[:, lanes]
        decays = jnp.exp(-rates)
        taps = [second_ref[0, j : j + 1, lanes] for j in range(3)]
        older, last = rims_ref[6:7, lanes], rims_ref[7:8, lanes]
        mends = [spread(taps[1] * last + taps[2] * older), spread(taps[2] * last)]
        gain = spread(gain_ref[:, lanes])
        incoming = [spread(state_ref[part, r : r + 1, :]) for r in range(MODES)]
        rate = [spread(rates[r : r + 1]) for r in range(MODES)]
        decay = [spread(decays[r : r + 1]) for r in range(MODES)]

        def half(count, length, start, enter_ref, own_ref, first_row):
            carry = [
                enter_ref[r, :, lanes]
                + jnp.exp(-(rate[r] * (segment * float(length) + start))) * incoming[r]
                for r in range(MODES)
            ]
            for k in range(count):
                carry = [decay[r] * carry[r] for r in range(MODES)]
                total = rows_of(own_ref, k, lanes)
                for value in carry:
                    total = total + value
                query = query2_ref[pl.ds(first_row + SEG * k, SEG), lanes]
                if first_row == 0 and k < 2:
                    query = query + jnp.where(top, mends[k], 0.0)
                mixed = query * total
                rows = pl.ds(first_row + SEG * k, SEG)
                squares_t[rows, :] = squares_t[rows, :] + mixed * mixed
                mixed_out[part, pl.ds(first_row + k, SEG, stride=length), :] = mixed * gain

        half(HEAD, HEAD, 0.0, enter_head_ref, own_head_ref, 0)
        half(MAIN, MAIN, float(HEAD_ROWS), enter_main_ref, own_main_ref, HEAD_ROWS)

    @pl.when(step == pl.num_programs(0) - 1)
    def _():
        sums = jnp.sum(squares_t[...], axis=1, keepdims=True)
        squares_t[...] = jnp.broadcast_to(sums, squares_t.shape)
        head = [squares_t[pl.ds(i, HEAD, stride=SEG), :] for i in range(SEG)]
        main = [squares_t[pl.ds(HEAD_ROWS + i, MAIN, stride=SEG), :] for i in range(SEG)]
        ordered = jnp.concatenate(head + main, 0)
        squares_out[...] = ordered.T[0:8, :]


def scale_kernel(mixed_ref, scale_ref, out_ref):
    for part in range(mixed_ref.shape[0]):
        out_ref[pl.ds(LANES * part, LANES), :] = mixed_ref[part].T * scale_ref[...]


def from_behind(block):
    count = lax.axis_size("seq")
    return lax.ppermute(block, "seq", [(i, i + 1) for i in range(count - 1)])


def call(kernel, grid, in_specs, out_specs, out_shape, scratch, flops, size, name):
    return pl.pallas_call(
        kernel,
        grid=grid,
        in_specs=in_specs,
        out_specs=out_specs,
        out_shape=out_shape,
        scratch_shapes=scratch,
        compiler_params=pltpu.CompilerParams(vmem_limit_bytes=LIMIT),
        cost_estimate=pl.CostEstimate(flops=flops, bytes_accessed=size, transcendentals=0),
        name=name,
    )


def local(
    query_proj,
    key_proj,
    value_proj,
    second_query,
    second_key,
    short_filter,
    second_short,
    medium_filter,
    decay_rate,
    residue,
    skip_gain,
    norm_gain,
):
    channels = query_proj.shape[0]
    count = lax.axis_size("seq")
    tiles = channels // LANES
    width = min(256, channels)
    steps = channels // width
    per_step = width // LANES
    short_t = jnp.transpose(short_filter, (0, 2, 1))
    second_t = jnp.transpose(second_short, (0, 2, 1))
    rate_t = decay_rate.T
    amplitude = residue.T * jnp.sqrt(-jnp.expm1(-2.0 * rate_t))
    skip = skip_gain[None, :]
    gain = norm_gain[None, :]
    forward, spectrum, inverse, halo_forward, halo_inverse = tables()

    def struct(*shape):
        return jax.ShapeDtypeStruct(shape, F32)

    def by_row(columns):
        return pl.BlockSpec((width, columns), lambda i: (i, 0))

    def by_lane(rows):
        return pl.BlockSpec((rows, width), lambda i: (0, i))

    def by_lane3(planes, rows):
        return pl.BlockSpec((planes, rows, width), lambda i: (0, 0, i))

    def whole(array):
        return pl.BlockSpec(array.shape, lambda i: (0,) * array.ndim)

    state_spec = pl.BlockSpec((per_step, MODES, LANES), lambda i: (i, 0, 0))
    mixed_spec = pl.BlockSpec((per_step, T, LANES), lambda i: (i, 0, 0))

    tail = call(
        tail_kernel,
        (steps,),
        [by_row(T), by_row(T), by_lane3(3, 3)],
        by_row(LANES),
        struct(channels, LANES),
        [pltpu.VMEM((8, width), F32)],
        channels * T * 8,
        channels * T * 10,
        "tail",
    )(key_proj, value_proj, short_t)
    halo = from_behind(tail)

    (
        taps,
        tap_spectrum,
        medium,
        query,
        key2,
        query2,
        own_main,
        enter_main,
        leave_main,
        first_rows,
        rims,
    ) = call(
        local_kernel,
        (steps,),
        [by_row(T)] * 5
        + [by_lane3(3, 3), by_lane3(3, 3), by_row(TAPS), by_lane(MODES), by_lane(MODES), by_lane(1)]
        + [whole(forward), whole(spectrum), whole(inverse)],
        [
            by_lane(HEAD_ROWS),
            by_lane(384),
            by_lane(HEAD_ROWS),
            by_lane(T),
            by_lane(T),
            by_lane(T),
            by_lane(MAIN_ROWS),
            by_lane3(MODES, SEG),
            by_lane(MODES),
            by_lane(8),
            by_lane(RIMS),
        ],
        [
            struct(HEAD_ROWS, channels),
            struct(384, channels),
            struct(HEAD_ROWS, channels),
            struct(T, channels),
            struct(T, channels),
            struct(T, channels),
            struct(MAIN_ROWS, channels),
            struct(MODES, SEG, channels),
            struct(MODES, channels),
            struct(8, channels),
            struct(RIMS, channels),
        ],
        [pltpu.VMEM((per_step, T, LANES), F32)] * 5
        + [pltpu.VMEM((per_step, HEAD_ROWS, LANES), F32)]
        + [pltpu.VMEM((T, width), F32)] * 2,
        channels * T * 8000,
        channels * T * 60,
        "local",
    )(
        key_proj,
        value_proj,
        query_proj,
        second_query,
        second_key,
        short_t,
        second_t,
        medium_filter,
        rate_t,
        amplitude,
        skip,
        forward,
        spectrum,
        inverse,
    )
    border = from_behind(rims)

    own_head, enter_head, enter_main, state = call(
        join_kernel,
        (steps,),
        [
            by_row(LANES),
            by_lane(RIMS),
            by_lane(384),
            by_lane(HEAD_ROWS),
            by_lane(HEAD_ROWS),
            by_lane(HEAD_ROWS),
            by_lane(HEAD_ROWS),
            by_lane(8),
            by_lane3(MODES, SEG),
            by_lane(MODES),
            by_lane3(3, 3),
            by_lane3(3, 3),
            by_lane(MODES),
            by_lane(MODES),
            by_lane(1),
            whole(halo_forward),
            whole(halo_inverse),
        ],
        [by_lane(HEAD_ROWS), by_lane3(MODES, SEG), by_lane3(MODES, SEG), state_spec],
        [
            struct(HEAD_ROWS, channels),
            struct(MODES, SEG, channels),
            struct(MODES, SEG, channels),
            struct(tiles, MODES, LANES),
        ],
        [pltpu.VMEM((HEAD_ROWS + 8, width), F32)],
        channels * T * 2000,
        channels * T * 20,
        "join",
    )(
        halo,
        border,
        tap_spectrum,
        medium,
        taps,
        query,
        key2,
        first_rows,
        enter_main,
        leave_main,
        short_t,
        second_t,
        rate_t,
        amplitude,
        skip,
        halo_forward,
        halo_inverse,
    )

    place = lax.axis_index("seq")
    own_rate = lax.dynamic_slice(
        rate_t, (place % MODES, (place // MODES) * LANES), (1, LANES)
    )
    gathered = lax.all_to_all(
        state.reshape(count, 1, LANES), "seq", split_axis=0, concat_axis=0, tiled=True
    )
    scanned = call(
        scan_kernel,
        (1,),
        [pl.BlockSpec((count, LANES), lambda i: (0, 0)), pl.BlockSpec((1, LANES), lambda i: (0, 0))],
        pl.BlockSpec((count, LANES), lambda i: (0, 0)),
        struct(count, LANES),
        [],
        count * LANES * 30,
        count * LANES * 8,
        "scan",
    )(gathered.reshape(count, LANES), own_rate)
    incoming = lax.all_to_all(
        scanned.reshape(count, 1, LANES), "seq", split_axis=0, concat_axis=0, tiled=True
    ).reshape(tiles, MODES, LANES)

    mixed, squares = call(
        finish_kernel,
        (steps,),
        [
            state_spec,
            by_lane(HEAD_ROWS),
            by_lane(MAIN_ROWS),
            by_lane3(MODES, SEG),
            by_lane3(MODES, SEG),
            by_lane(T),
            by_lane(RIMS),
            by_lane3(3, 3),
            by_lane(MODES),
            by_lane(1),
        ],
        [mixed_spec, pl.BlockSpec((8, T), lambda i: (0, 0))],
        [struct(tiles, T, LANES), struct(8, T)],
        [pltpu.VMEM((T, LANES), F32)],
        channels * T * 40,
        channels * T * 16,
        "finish",
    )(
        incoming,
        own_head,
        own_main,
        enter_head,
        enter_main,
        query2,
        border,
        second_t,
        rate_t,
        gain,
    )
    total = lax.psum(squares[0], "chan")
    scale = lax.rsqrt(total / (channels * lax.axis_size("chan")) + norm_eps)
    return call(
        scale_kernel,
        (steps,),
        [mixed_spec, pl.BlockSpec((1, T), lambda i: (0, 0))],
        by_row(T),
        struct(channels, T),
        [],
        channels * T,
        channels * T * 8,
        "scale",
    )(mixed, scale[None, :])


def solution(mesh):
    return jax.shard_map(
        local,
        mesh=mesh,
        in_specs=(
            P("chan", "seq"),
            P("chan", "seq"),
            P("chan", "seq"),
            P("chan", "seq"),
            P("chan", "seq"),
            P(None, "chan", None),
            P(None, "chan", None),
            P("chan", None),
            P("chan", None),
            P("chan", None),
            P("chan"),
            P("chan"),
        ),
        out_specs=P("chan", "seq"),
        check_vma=False,
    )
```

```python
import functools

import jax
import jax.numpy as jnp
import ml_dtypes
import numpy as np
from jax import lax
from jax.experimental import pallas as pl
from jax.experimental.pallas import tpu as pltpu
from jax.sharding import PartitionSpec as P

norm_eps = 1e-06

T = 256
TAPS = 128
MODES = 8
LANES = 128
SEG = 8
HEAD = 17
MAIN = 15
HEAD_ROWS = HEAD * SEG
MAIN_ROWS = MAIN * SEG
RIMS = 16
LIMIT = 24 * 1024 * 1024

F32 = jnp.float32
BF16 = jnp.bfloat16


def row_times():
    head = [HEAD * i + k for k in range(HEAD) for i in range(SEG)]
    main = [HEAD_ROWS + MAIN * i + k for k in range(MAIN) for i in range(SEG)]
    return np.array(head + main)


def packed_forward(slots):
    k = np.arange(128)[:, None]
    angle = 2.0 * np.pi * k * np.asarray(slots)[None, :] / 256.0
    imag = -np.sin(angle)
    imag[0] = np.cos(np.pi * np.asarray(slots))
    return np.concatenate([np.cos(angle), imag], 0)


def packed_inverse(slots):
    k = np.arange(128)[None, :]
    angle = 2.0 * np.pi * k * np.asarray(slots)[:, None] / 256.0
    real = 2.0 * np.cos(angle)
    real[:, 0] = 1.0
    imag = -2.0 * np.sin(angle)
    imag[:, 0] = np.cos(np.pi * np.asarray(slots))
    return np.concatenate([real, imag], 1) / 256.0


def three_pass(matrix):
    high = matrix.astype(ml_dtypes.bfloat16)
    low = (matrix - high.astype(np.float64)).astype(ml_dtypes.bfloat16)
    return np.concatenate([high, low, high], 1)


def tables():
    times = row_times()
    first = packed_forward(times + 128) * (times < 128)[None, :]
    second = packed_forward(times)
    forward = np.concatenate([first, second], 0)
    taps = packed_forward(np.arange(TAPS))
    real, imag = taps[:128], taps[128:].copy()
    cross = real.copy()
    cross[0] = imag[0]
    imag[0] = 0.0
    spectrum = np.concatenate([real, imag, cross], 0)
    inverse = np.concatenate(
        [
            packed_inverse(times + 128) * (times < 128)[:, None],
            packed_inverse(times) * (times >= 128)[:, None],
        ],
        1,
    )
    halo = packed_forward(np.arange(128))
    halo[:, :2] = 0.0
    head_times = np.concatenate([times[:HEAD_ROWS], [-2, -1], np.full(6, 255)])
    halo_back = packed_inverse(head_times + 128) * (head_times < 128)[:, None]
    return [three_pass(m) for m in (forward, spectrum, inverse, halo, halo_back)]


def halves(x):
    high = x.astype(BF16)
    low = (x - high.astype(F32)).astype(BF16)
    return high, low


def matmul3(matrix, x):
    high, low = halves(x)
    stacked = jnp.concatenate([high, high, low], 0)
    return jnp.dot(matrix, stacked, preferred_element_type=F32)


def spectral_product(x, taps):
    real, imag = x[:128], x[128:]
    tap_real, tap_imag, tap_cross = taps[:128], taps[128:256], taps[256:]
    return jnp.concatenate(
        [real * tap_real - imag * tap_imag, real * tap_imag + imag * tap_cross], 0
    )


def sublane(shape):
    return lax.broadcasted_iota(jnp.int32, shape, 0)


def down(x, distance=1):
    return pltpu.roll(x, distance, axis=0)


def fir3(slabs, taps):
    return [
        taps[0] * slabs[k + 2] + taps[1] * slabs[k + 1] + taps[2] * slabs[k]
        for k in range(len(slabs) - 2)
    ]


def with_rims(head, main, rims=None):
    top = sublane(head[0].shape) == 0
    zero = jnp.zeros_like(head[0])
    before = (zero, zero) if rims is None else rims
    ends = [down(head[HEAD - 2]), down(head[HEAD - 1])]
    head_all = [jnp.where(top, before[k], ends[k]) for k in range(2)] + head
    if main is None:
        return head_all, None
    main_all = [jnp.where(top, ends[k], down(main[MAIN - 2 + k])) for k in range(2)] + main
    return head_all, main_all


def rows_of(ref, k, lanes):
    return ref[pl.ds(SEG * k, SEG), lanes]


def spread(row):
    return jnp.broadcast_to(row, (SEG, row.shape[1]))


def recurrence(inputs, decays, gains, skip):
    states = [gains[r] * inputs[0] for r in range(MODES)]
    outs = []
    for k, value in enumerate(inputs):
        if k:
            states = [decays[r] * states[r] + gains[r] * value for r in range(MODES)]
        total = skip * value
        for state in states:
            total = total + state
        outs.append(total)
    return outs, states


def segment_powers(rates, step):
    return [jnp.exp(-(step * distance) * rates) for distance in (1, 2, 4)]


def prefix(state, powers, mode):
    place = sublane(state.shape)
    total = state
    for power, distance in zip(powers, (1, 2, 4)):
        moved = jnp.where(place >= distance, down(total, distance), 0.0)
        total = total + spread(power[mode : mode + 1]) * moved
    return jnp.where(place >= 1, down(total), 0.0), total[SEG - 1 :]


def turned(block):
    return block.T


def tail_kernel(key_hbm, value_hbm, short_ref, tail_ref, key_in, value_in, key_sem, value_sem):
    chunks = key_sem.shape[0]
    rows = key_hbm.shape[0] // chunks
    copies = []
    for chunk in range(chunks):
        here = pl.ds(chunk * rows, rows)
        for source, target, sem in (
            (key_hbm, key_in, key_sem),
            (value_hbm, value_in, value_sem),
        ):
            copy = pltpu.make_async_copy(
                source.at[here, pl.ds(LANES, LANES)], target.at[here, :], sem.at[chunk]
            )
            copy.start()
            copies.append(copy)
    for chunk in range(chunks):
        copies[2 * chunk].wait()
        copies[2 * chunk + 1].wait()
        for tile in range(chunk * rows // LANES, (chunk + 1) * rows // LANES):
            lanes = pl.ds(tile * LANES, LANES)

            def feature(ref, index):
                here = turned(ref[lanes, :])
                taps = [short_ref[index, j : j + 1, lanes] for j in range(3)]
                return taps[0] * here + taps[1] * down(here) + taps[2] * down(here, 2)

            tail_ref[tile] = feature(key_in, 1) * feature(value_in, 2)


def prep_kernel(
    key_hbm,
    value_hbm,
    query_hbm,
    query2_hbm,
    key2_hbm,
    medium_hbm,
    short_ref,
    key_t,
    value_t,
    query_t,
    query2_t,
    key2_t,
    taps_t,
    rims_out,
    key_in,
    value_in,
    query_in,
    query2_in,
    key2_in,
    medium_in,
    sems,
):
    chunks = sems.shape[1]
    rows = key_hbm.shape[0] // chunks
    fields = (
        (key_hbm, key_in, key_t),
        (value_hbm, value_in, value_t),
        (query_hbm, query_in, query_t),
        (query2_hbm, query2_in, query2_t),
        (key2_hbm, key2_in, key2_t),
        (medium_hbm, medium_in, taps_t),
    )
    copies = []
    for chunk in range(chunks):
        here = pl.ds(chunk * rows, rows)
        for place, (source, target, _) in enumerate(fields):
            copy = pltpu.make_async_copy(
                source.at[here, :], target.at[here, :], sems.at[place, chunk]
            )
            copy.start()
            copies.append(copy)
    for chunk in range(chunks):
        for place in range(len(fields)):
            copies[chunk * len(fields) + place].wait()
        for tile in range(chunk * rows // LANES, (chunk + 1) * rows // LANES):
            lanes = pl.ds(tile * LANES, LANES)
            rims_out[tile] = jnp.zeros((RIMS, LANES), F32)
            for place, (_, source, target) in enumerate(fields):
                if place < 5:
                    target[tile] = turned(source[lanes, :])
                    rims_out[tile, 2 * place : 2 * place + 2, :] = target[tile, T - 2 : T, :]
                else:
                    target[tile, 0:TAPS, :] = turned(source[lanes, :])
                    target[tile, TAPS:HEAD_ROWS, :] = jnp.zeros((HEAD_ROWS - TAPS, LANES), F32)

            def feature(ref, index, time):
                return sum(
                    short_ref[index, j : j + 1, lanes] * ref[tile, time - j : time - j + 1, :]
                    for j in range(3)
                )

            for k in range(2):
                rims_out[tile, 10 + k : 11 + k, :] = feature(query_t, 0, T - 2 + k)
            for k in range(3):
                rims_out[tile, 12 + k : 13 + k, :] = feature(key_t, 1, T // 2 - 1 + k) * feature(
                    value_t, 2, T // 2 - 1 + k
                )


def local_kernel(
    key_t,
    value_t,
    query_t,
    query2_t,
    key2_t,
    taps_t,
    short_ref,
    second_ref,
    rate_ref,
    amplitude_ref,
    skip_ref,
    forward_ref,
    spectrum_ref,
    inverse_ref,
    taps_out,
    spectrum_out,
    medium_out,
    query_out,
    key2_out,
    query2_out,
    own_out,
    enter_out,
    leave_out,
    reach_head_out,
    reach_main_out,
    gated_t,
    medium_t,
    query_all,
    key2_all,
):
    tiles = key_t.shape[0]
    group = gated_t.shape[1] // LANES
    top = sublane((SEG, LANES)) == 0
    segment = sublane((SEG, LANES)).astype(F32)

    def slabs_of(ref, tile):
        head = [ref[tile, pl.ds(k, SEG, stride=HEAD), :] for k in range(HEAD)]
        main = [ref[tile, pl.ds(HEAD_ROWS + k, SEG, stride=MAIN), :] for k in range(MAIN)]
        return head, main

    def feature(ref, tile, taps_of, index, lanes):
        taps = [spread(taps_of[index, j : j + 1, lanes]) for j in range(3)]
        head, main = with_rims(*slabs_of(ref, tile))
        return fir3(head, taps) + fir3(main, taps)

    def body(step, _):
        for part in range(group):
            tile = step * group + part
            lanes = pl.ds(pl.multiple_of(tile * LANES, LANES), LANES)
            local = pl.ds(part * LANES, LANES)
            keys = feature(key_t, tile, short_ref, 1, lanes)
            values = feature(value_t, tile, short_ref, 2, lanes)
            for k in range(HEAD + MAIN):
                gated = keys[k] * values[k]
                if k < 2:
                    gated = jnp.where(top, 0.0, gated)
                gated_t[pl.ds(SEG * k, SEG), local] = gated
            for k, slab in enumerate(feature(query_t, tile, short_ref, 0, lanes)):
                query_all[part, pl.ds(SEG * k, SEG), :] = slab
            query_out[tile] = query_all[part, 0:HEAD_ROWS, :]
            for k, slab in enumerate(feature(key2_t, tile, second_ref, 1, lanes)):
                key2_all[part, pl.ds(SEG * k, SEG), :] = slab
            key2_out[tile] = key2_all[part, 0:HEAD_ROWS, :]
            for k, slab in enumerate(feature(query2_t, tile, second_ref, 0, lanes)):
                query2_out[tile, pl.ds(SEG * k, SEG), :] = slab
            for k in range(HEAD):
                taps_out[tile, pl.ds(SEG * k, SEG), :] = taps_t[
                    tile, pl.ds(k, SEG, stride=HEAD), :
                ]

        filters = [taps_t[step * group + part, 0:TAPS, :] for part in range(group)]
        spectrum = matmul3(spectrum_ref[...], jnp.concatenate(filters, 1))
        both = matmul3(forward_ref[...], gated_t[...])
        first = spectral_product(both[:T], spectrum)
        second = spectral_product(both[T:], spectrum)
        medium_t[...] = matmul3(inverse_ref[...], jnp.concatenate([first, second], 0))

        for part in range(group):
            tile = step * group + part
            lanes = pl.ds(pl.multiple_of(tile * LANES, LANES), LANES)
            local = pl.ds(part * LANES, LANES)
            spectrum_out[tile] = spectrum[:, part * LANES : (part + 1) * LANES]
            medium_out[tile] = medium_t[0:HEAD_ROWS, local]
            taps = [spread(second_ref[2, j : j + 1, lanes]) for j in range(3)]
            firsts = [
                rows_of(medium_t, k, local) * query_all[part, pl.ds(SEG * k, SEG), :]
                for k in range(HEAD - 2, HEAD + MAIN)
            ]
            ends = [down(firsts[0]), down(firsts[1])]
            main = firsts[2:]
            main_all = [jnp.where(top, ends[k], down(main[MAIN - 2 + k])) for k in range(2)] + main
            values2 = fir3(main_all, taps)
            inputs = [
                key2_all[part, pl.ds(SEG * (HEAD + k), SEG), :] * values2[k] for k in range(MAIN)
            ]
            rates, gains = rate_ref[:, lanes], amplitude_ref[:, lanes]
            decays = jnp.exp(-rates)
            outs, ends = recurrence(
                inputs,
                [spread(decays[r : r + 1]) for r in range(MODES)],
                [spread(gains[r : r + 1]) for r in range(MODES)],
                spread(skip_ref[:, lanes]),
            )
            for k in range(MAIN):
                own_out[tile, pl.ds(SEG * k, SEG), :] = outs[k]
            powers = segment_powers(rates, float(MAIN))
            for r in range(MODES):
                enter, leave = prefix(ends[r], powers, r)
                enter_out[tile, r] = enter
                leave_out[tile, r : r + 1, :] = leave
                rate = spread(rates[r : r + 1])
                reach_head_out[tile, r] = jnp.exp(-(rate * (segment * float(HEAD))))
                reach_main_out[tile, r] = jnp.exp(-(rate * (segment * float(MAIN))))
        return _

    lax.fori_loop(0, tiles // group, body, 0)


def join_kernel(
    halo_ref,
    rims_ref,
    spectrum_ref,
    medium_ref,
    taps_ref,
    query_ref,
    key2_ref,
    key_t,
    value_t,
    enter_main_ref,
    leave_main_ref,
    reach_main_ref,
    short_ref,
    second_ref,
    rate_ref,
    amplitude_ref,
    skip_ref,
    forward_ref,
    inverse_ref,
    own_out,
    enter_out,
    enter_main_out,
    state_out,
    medium_t,
):
    tiles = halo_ref.shape[0]
    group = medium_t.shape[1] // LANES
    top = sublane((SEG, LANES)) == 0

    def body(step, _):
        tile_list = [step * group + part for part in range(group)]
        halo = matmul3(
            forward_ref[...], jnp.concatenate([halo_ref[tile] for tile in tile_list], 1)
        )
        filters = jnp.concatenate([spectrum_ref[tile] for tile in tile_list], 1)
        medium_t[...] = matmul3(inverse_ref[...], spectral_product(halo, filters))
        for part, tile in enumerate(tile_list):
            one(tile, pl.ds(part * LANES, LANES))
        return _

    def one(tile, local):
        lanes = pl.ds(pl.multiple_of(tile * LANES, LANES), LANES)

        def rim(k):
            return rims_ref[tile, k : k + 1, :]

        def taps_of(ref, index):
            return [ref[index, j : j + 1, lanes] for j in range(3)]

        def early(ref, place, index):
            taps = taps_of(short_ref, index)
            zero, one = ref[tile, 0:1, :], ref[tile, 1:2, :]
            older, last = rim(2 * place), rim(2 * place + 1)
            return (
                taps[0] * zero + taps[1] * last + taps[2] * older,
                taps[0] * one + taps[1] * zero + taps[2] * last,
            )

        def mended(ref, place, taps):
            slabs = [ref[tile, pl.ds(SEG * k, SEG), :] for k in range(HEAD)]
            older, last = rim(2 * place), rim(2 * place + 1)
            slabs[0] = slabs[0] + jnp.where(top, spread(taps[1] * last + taps[2] * older), 0.0)
            slabs[1] = slabs[1] + jnp.where(top, spread(taps[2] * last), 0.0)
            return slabs

        def tap(j):
            row = SEG * (j % HEAD) + j // HEAD
            return taps_ref[tile, row : row + 1, :]

        keys, values = early(key_t, 0, 1), early(value_t, 1, 2)
        gated = [spread(keys[k] * values[k]) for k in range(2)]
        taps = [taps_ref[tile, pl.ds(SEG * k, SEG), :] for k in range(HEAD)]
        shifted = [jnp.where(top, 0.0, down(taps[HEAD - 1]))] + taps
        query = mended(query_ref, 2, taps_of(short_ref, 0))
        key2 = mended(key2_ref, 4, taps_of(second_ref, 1))
        mediums = [
            medium_ref[tile, pl.ds(SEG * k, SEG), :]
            + rows_of(medium_t, k, local)
            + taps[k] * gated[0]
            + shifted[k] * gated[1]
            for k in range(HEAD)
        ]
        far, farther, farthest = rim(14), rim(13), rim(12)
        mediums[0] = mediums[0] + jnp.where(top, spread(tap(127) * far), 0.0)
        older = medium_t[HEAD_ROWS : HEAD_ROWS + 1, local] + (
            tap(125) * far + tap(126) * farther + tap(127) * farthest
        )
        last = medium_t[HEAD_ROWS + 1 : HEAD_ROWS + 2, local] + (
            tap(126) * far + tap(127) * farther
        )
        firsts = [query[k] * mediums[k] for k in range(HEAD)]
        firsts_all, _ = with_rims(firsts, None, (spread(rim(10) * older), spread(rim(11) * last)))
        values2 = fir3(firsts_all, [spread(t) for t in taps_of(second_ref, 2)])
        inputs = [key2[k] * values2[k] for k in range(HEAD)]
        rates, gains = rate_ref[:, lanes], amplitude_ref[:, lanes]
        decays = jnp.exp(-rates)
        outs, ends = recurrence(
            inputs,
            [spread(decays[r : r + 1]) for r in range(MODES)],
            [spread(gains[r : r + 1]) for r in range(MODES)],
            spread(skip_ref[:, lanes]),
        )
        for k in range(HEAD):
            own_out[tile, pl.ds(SEG * k, SEG), :] = outs[k]
        powers = segment_powers(rates, float(HEAD))
        whole = jnp.exp(-float(MAIN_ROWS) * rates)
        for r in range(MODES):
            enter, leave = prefix(ends[r], powers, r)
            enter_out[tile, r] = enter
            enter_main_out[tile, r] = enter_main_ref[tile, r] + reach_main_ref[tile, r] * spread(
                leave
            )
            state_out[tile, r : r + 1, :] = (
                leave_main_ref[tile, r : r + 1, :] + leave * whole[r : r + 1]
            )

    lax.fori_loop(0, tiles // group, body, 0)


def scan_kernel(place_ref, state_ref, rate_ref, out_ref):
    blocks = state_ref.shape[0]
    position = sublane(state_ref.shape)
    index = place_ref[0]
    lanes = pl.ds(pl.multiple_of((index // MODES) * LANES, LANES), LANES)
    rates = rate_ref[:, lanes]
    mine = sublane(rates.shape) == lax.rem(index, MODES)
    rate = jnp.sum(jnp.where(mine, rates, 0.0), axis=0, keepdims=True)
    total = state_ref[...]
    distance = 1
    while distance < blocks:
        moved = jnp.where(position >= distance, down(total, distance), 0.0)
        total = total + jnp.exp(-(float(T) * distance) * rate) * moved
        distance *= 2
    out_ref[...] = jnp.where(position >= 1, down(total), 0.0)


def finish_kernel(
    state_ref,
    own_head_ref,
    own_main_ref,
    enter_head_ref,
    enter_main_ref,
    reach_head_ref,
    reach_main_ref,
    query2_ref,
    rims_ref,
    second_ref,
    rate_ref,
    gain_ref,
    mixed_out,
    squares_out,
    squares_t,
):
    squares_t[...] = jnp.zeros_like(squares_t)
    top = sublane((SEG, LANES)) == 0

    def body(tile, _):
        lanes = pl.ds(pl.multiple_of(tile * LANES, LANES), LANES)
        rates = rate_ref[:, lanes]
        decays = jnp.exp(-rates)
        start = jnp.exp(-float(HEAD_ROWS) * rates)
        taps = [second_ref[0, j : j + 1, lanes] for j in range(3)]
        older, last = rims_ref[tile, 6:7, :], rims_ref[tile, 7:8, :]
        mends = [spread(taps[1] * last + taps[2] * older), spread(taps[2] * last)]
        gain = spread(gain_ref[:, lanes])
        states = state_ref[tile]
        later = states * start
        decay = [spread(decays[r : r + 1]) for r in range(MODES)]

        def half(length, incoming, reach_ref, enter_ref, own_ref, first_row):
            carry = [
                enter_ref[tile, r] + reach_ref[tile, r] * spread(incoming[r : r + 1])
                for r in range(MODES)
            ]
            for k in range(length):
                carry = [decay[r] * carry[r] for r in range(MODES)]
                total = own_ref[tile, pl.ds(SEG * k, SEG), :]
                for value in carry:
                    total = total + value
                rows = pl.ds(first_row + SEG * k, SEG)
                query = query2_ref[tile, rows, :]
                if first_row == 0 and k < 2:
                    query = query + jnp.where(top, mends[k], 0.0)
                mixed = query * total
                squares_t[rows, :] = squares_t[rows, :] + mixed * mixed
                mixed_out[tile, pl.ds(first_row + k, SEG, stride=length), :] = mixed * gain

        half(HEAD, states, reach_head_ref, enter_head_ref, own_head_ref, 0)
        half(MAIN, later, reach_main_ref, enter_main_ref, own_main_ref, HEAD_ROWS)
        return _

    lax.fori_loop(0, query2_ref.shape[0], body, 0)
    sums = jnp.sum(squares_t[...], axis=1, keepdims=True)
    squares_t[...] = jnp.broadcast_to(sums, squares_t.shape)
    head = [squares_t[pl.ds(i, HEAD, stride=SEG), :] for i in range(SEG)]
    main = [squares_t[pl.ds(HEAD_ROWS + i, MAIN, stride=SEG), :] for i in range(SEG)]
    ordered = jnp.concatenate(head + main, 0)
    squares_out[...] = ordered.T[0:1, :]


def scale_kernel(divisor, mixed_ref, squares_ref, out_hbm, out_t, sems):
    scale = lax.rsqrt(squares_ref[...] / divisor + norm_eps)
    chunks = sems.shape[0]
    tiles = mixed_ref.shape[0] // chunks
    copies = []
    for chunk in range(chunks):
        for tile in range(chunk * tiles, (chunk + 1) * tiles):
            out_t[pl.ds(tile * LANES, LANES), :] = mixed_ref[tile].T * scale
        rows = pl.ds(chunk * tiles * LANES, tiles * LANES)
        copy = pltpu.make_async_copy(out_t.at[rows, :], out_hbm.at[rows, :], sems.at[chunk])
        copy.start()
        copies.append(copy)
    for copy in copies:
        copy.wait()


def from_behind(block):
    count = lax.axis_size("seq")
    return lax.ppermute(block, "seq", [(i, i + 1) for i in range(count - 1)])


def in_hbm(x):
    return pltpu.with_memory_space_constraint(x, pltpu.HBM)


def call(kernel, in_specs, out_specs, out_shape, scratch, flops, size, name):
    return pl.pallas_call(
        kernel,
        in_specs=in_specs,
        out_specs=out_specs,
        out_shape=out_shape,
        scratch_shapes=scratch,
        compiler_params=pltpu.CompilerParams(vmem_limit_bytes=LIMIT),
        cost_estimate=pl.CostEstimate(flops=flops, bytes_accessed=size, transcendentals=0),
        name=name,
    )


def exchange(rows):
    count, lanes = rows.shape
    return lax.all_to_all(
        rows.reshape(count, 1, lanes), "seq", split_axis=0, concat_axis=0, tiled=True
    ).reshape(count, lanes)


def local(
    query_proj,
    key_proj,
    value_proj,
    second_query,
    second_key,
    short_filter,
    second_short,
    medium_filter,
    decay_rate,
    residue,
    skip_gain,
    norm_gain,
):
    channels = query_proj.shape[0]
    count = lax.axis_size("seq")
    tiles = channels // LANES
    group = min(2, tiles)
    chunks = min(4, tiles)
    short_t = jnp.transpose(short_filter, (0, 2, 1))
    second_t = jnp.transpose(second_short, (0, 2, 1))
    rate_t = decay_rate.T
    amplitude = residue.T * jnp.sqrt(-jnp.expm1(-2.0 * rate_t))
    skip = skip_gain[None, :]
    gain = norm_gain[None, :]
    forward, spectrum, inverse, halo_forward, halo_inverse = tables()
    held = pl.BlockSpec(memory_space=pltpu.VMEM)
    outside = pl.BlockSpec(memory_space=pl.ANY)
    words = channels * T

    def struct(*shape):
        return jax.ShapeDtypeStruct(shape, F32)

    fields = [
        in_hbm(x) for x in (key_proj, value_proj, query_proj, second_query, second_key, medium_filter)
    ]
    tail = call(
        tail_kernel,
        [outside, outside, held],
        held,
        struct(tiles, TAPS, LANES),
        [pltpu.VMEM((channels, LANES), F32)] * 2 + [pltpu.SemaphoreType.DMA((chunks,))] * 2,
        words * 8,
        words * 6,
        "tail",
    )(fields[0], fields[1], short_t)
    halo = from_behind(tail)

    *turned_fields, taps_t, rims = call(
        prep_kernel,
        [outside] * 6 + [held],
        [held] * 7,
        [struct(tiles, T, LANES)] * 5
        + [struct(tiles, HEAD_ROWS, LANES), struct(tiles, RIMS, LANES)],
        [pltpu.VMEM((channels, T), F32)] * 5
        + [pltpu.VMEM((channels, TAPS), F32), pltpu.SemaphoreType.DMA((6, chunks))],
        words * 20,
        words * 40,
        "prep",
    )(*fields, short_t)
    border = from_behind(rims)

    (
        taps,
        tap_spectrum,
        medium,
        query,
        key2,
        query2,
        own_main,
        enter_main,
        leave_main,
        reach_head,
        reach_main,
    ) = call(
        local_kernel,
        [held] * 14,
        [held] * 11,
        [
            struct(tiles, HEAD_ROWS, LANES),
            struct(tiles, 384, LANES),
            struct(tiles, HEAD_ROWS, LANES),
            struct(tiles, HEAD_ROWS, LANES),
            struct(tiles, HEAD_ROWS, LANES),
            struct(tiles, T, LANES),
            struct(tiles, MAIN_ROWS, LANES),
            struct(tiles, MODES, SEG, LANES),
            struct(tiles, MODES, LANES),
            struct(tiles, MODES, SEG, LANES),
            struct(tiles, MODES, SEG, LANES),
        ],
        [pltpu.VMEM((T, group * LANES), F32)] * 2 + [pltpu.VMEM((group, T, LANES), F32)] * 2,
        words * 8000,
        words * 60,
        "local",
    )(
        *turned_fields,
        taps_t,
        short_t,
        second_t,
        rate_t,
        amplitude,
        skip,
        forward,
        spectrum,
        inverse,
    )

    own_head, enter_head, enter_main, state = call(
        join_kernel,
        [held] * 19,
        [held] * 4,
        [
            struct(tiles, HEAD_ROWS, LANES),
            struct(tiles, MODES, SEG, LANES),
            struct(tiles, MODES, SEG, LANES),
            struct(tiles, MODES, LANES),
        ],
        [pltpu.VMEM((HEAD_ROWS + 8, group * LANES), F32)],
        words * 2000,
        words * 20,
        "join",
    )(
        halo,
        border,
        tap_spectrum,
        medium,
        taps,
        query,
        key2,
        turned_fields[0],
        turned_fields[1],
        enter_main,
        leave_main,
        reach_main,
        short_t,
        second_t,
        rate_t,
        amplitude,
        skip,
        halo_forward,
        halo_inverse,
    )

    place = lax.axis_index("seq").astype(jnp.int32).reshape(1)
    scanned = call(
        scan_kernel,
        [pl.BlockSpec(memory_space=pltpu.SMEM), held, held],
        held,
        struct(count, LANES),
        [],
        count * LANES * 30,
        count * LANES * 8,
        "scan",
    )(place, exchange(state.reshape(count, LANES)), rate_t)
    incoming = exchange(scanned).reshape(tiles, MODES, LANES)

    mixed, squares = call(
        finish_kernel,
        [held] * 12,
        [held] * 2,
        [struct(tiles, T, LANES), struct(1, T)],
        [pltpu.VMEM((T, LANES), F32)],
        words * 40,
        words * 16,
        "finish",
    )(
        incoming,
        own_head,
        own_main,
        enter_head,
        enter_main,
        reach_head,
        reach_main,
        query2,
        border,
        second_t,
        rate_t,
        gain,
    )
    total = lax.psum(squares, "chan")
    return call(
        functools.partial(scale_kernel, float(channels * lax.axis_size("chan"))),
        [held, held],
        outside,
        struct(channels, T),
        [pltpu.VMEM((channels, T), F32), pltpu.SemaphoreType.DMA((chunks,))],
        words,
        words * 8,
        "scale",
    )(mixed, total)


def solution(mesh):
    return jax.shard_map(
        local,
        mesh=mesh,
        in_specs=(
            P("chan", "seq"),
            P("chan", "seq"),
            P("chan", "seq"),
            P("chan", "seq"),
            P("chan", "seq"),
            P(None, "chan", None),
            P(None, "chan", None),
            P("chan", None),
            P("chan", None),
            P("chan", None),
            P("chan"),
            P("chan"),
        ),
        out_specs=P("chan", "seq"),
        check_vma=False,
    )
```

```python
import functools

import jax
import jax.numpy as jnp
import ml_dtypes
import numpy as np
from jax import lax
from jax.experimental import pallas as pl
from jax.experimental.pallas import tpu as pltpu
from jax.sharding import PartitionSpec as P

norm_eps = 1e-06

T = 256
TAPS = 128
MODES = 8
LANES = 128
SEG = 8
HEAD = 17
MAIN = 15
HEAD_ROWS = HEAD * SEG
MAIN_ROWS = MAIN * SEG
RIMS = 16
LIMIT = 24 * 1024 * 1024

F32 = jnp.float32
BF16 = jnp.bfloat16


def row_times():
    head = [HEAD * i + k for k in range(HEAD) for i in range(SEG)]
    main = [HEAD_ROWS + MAIN * i + k for k in range(MAIN) for i in range(SEG)]
    return np.array(head + main)


def packed_forward(slots):
    k = np.arange(128)[:, None]
    angle = 2.0 * np.pi * k * np.asarray(slots)[None, :] / 256.0
    imag = -np.sin(angle)
    imag[0] = np.cos(np.pi * np.asarray(slots))
    return np.concatenate([np.cos(angle), imag], 0)


def packed_inverse(slots):
    k = np.arange(128)[None, :]
    angle = 2.0 * np.pi * k * np.asarray(slots)[:, None] / 256.0
    real = 2.0 * np.cos(angle)
    real[:, 0] = 1.0
    imag = -2.0 * np.sin(angle)
    imag[:, 0] = np.cos(np.pi * np.asarray(slots))
    return np.concatenate([real, imag], 1) / 256.0


def three_pass(matrix):
    high = matrix.astype(ml_dtypes.bfloat16)
    low = (matrix - high.astype(np.float64)).astype(ml_dtypes.bfloat16)
    return np.concatenate([high, low, high], 1)


def tables():
    times = row_times()
    first = packed_forward(times + 128) * (times < 128)[None, :]
    second = packed_forward(times)
    forward = np.concatenate([first, second], 0)
    taps = packed_forward(np.arange(TAPS))
    real, imag = taps[:128], taps[128:].copy()
    cross = real.copy()
    cross[0] = imag[0]
    imag[0] = 0.0
    spectrum = np.concatenate([real, imag, cross], 0)
    inverse = np.concatenate(
        [
            packed_inverse(times + 128) * (times < 128)[:, None],
            packed_inverse(times) * (times >= 128)[:, None],
        ],
        1,
    )
    halo = packed_forward(np.arange(128))
    halo[:, :2] = 0.0
    head_times = np.concatenate([times[:HEAD_ROWS], [-2, -1], np.full(6, 255)])
    halo_back = packed_inverse(head_times + 128) * (head_times < 128)[:, None]
    return [three_pass(m) for m in (forward, spectrum, inverse, halo, halo_back)]


def halves(x):
    high = x.astype(BF16)
    low = (x - high.astype(F32)).astype(BF16)
    return high, low


def matmul3(matrix, x):
    high, low = halves(x)
    stacked = jnp.concatenate([high, high, low], 0)
    return jnp.dot(matrix, stacked, preferred_element_type=F32)


def spectral_product(x, taps):
    real, imag = x[:128], x[128:]
    tap_real, tap_imag, tap_cross = taps[:128], taps[128:256], taps[256:]
    return jnp.concatenate(
        [real * tap_real - imag * tap_imag, real * tap_imag + imag * tap_cross], 0
    )


def sublane(shape):
    return lax.broadcasted_iota(jnp.int32, shape, 0)


def down(x, distance=1):
    return pltpu.roll(x, distance, axis=0)


def fir3(slabs, taps):
    return [
        taps[0] * slabs[k + 2] + taps[1] * slabs[k + 1] + taps[2] * slabs[k]
        for k in range(len(slabs) - 2)
    ]


def with_rims(head, main, rims=None):
    top = sublane(head[0].shape) == 0
    zero = jnp.zeros_like(head[0])
    before = (zero, zero) if rims is None else rims
    ends = [down(head[HEAD - 2]), down(head[HEAD - 1])]
    head_all = [jnp.where(top, before[k], ends[k]) for k in range(2)] + head
    if main is None:
        return head_all, None
    main_all = [jnp.where(top, ends[k], down(main[MAIN - 2 + k])) for k in range(2)] + main
    return head_all, main_all


def rows_of(ref, k, lanes):
    return ref[pl.ds(SEG * k, SEG), lanes]


def spread(row):
    return jnp.broadcast_to(row, (SEG, row.shape[1]))


def recurrence(inputs, decays, gains, skip):
    states = [gains[r] * inputs[0] for r in range(MODES)]
    outs = []
    for k, value in enumerate(inputs):
        if k:
            states = [decays[r] * states[r] + gains[r] * value for r in range(MODES)]
        total = skip * value
        for state in states:
            total = total + state
        outs.append(total)
    return outs, states


def segment_powers(rates, step):
    return [jnp.exp(-(step * distance) * rates) for distance in (1, 2, 4)]


def prefix(state, powers, mode):
    place = sublane(state.shape)
    total = state
    for power, distance in zip(powers, (1, 2, 4)):
        moved = jnp.where(place >= distance, down(total, distance), 0.0)
        total = total + spread(power[mode : mode + 1]) * moved
    return jnp.where(place >= 1, down(total), 0.0), total[SEG - 1 :]


def turned(block):
    return block.T


def tail_kernel(
    key_hbm, value_hbm, short_hbm, tail_ref, key_in, value_in, short_ref, key_sem, value_sem, short_sem
):
    chunks = key_sem.shape[0]
    rows = key_hbm.shape[0] // chunks
    copies = []
    filters = pltpu.make_async_copy(short_hbm, short_ref, short_sem)
    filters.start()
    for chunk in range(chunks):
        here = pl.ds(chunk * rows, rows)
        for source, target, sem in (
            (key_hbm, key_in, key_sem),
            (value_hbm, value_in, value_sem),
        ):
            copy = pltpu.make_async_copy(
                source.at[here, pl.ds(LANES, LANES)], target.at[here, :], sem.at[chunk]
            )
            copy.start()
            copies.append(copy)
    filters.wait()
    for chunk in range(chunks):
        copies[2 * chunk].wait()
        copies[2 * chunk + 1].wait()
        for tile in range(chunk * rows // LANES, (chunk + 1) * rows // LANES):
            lanes = pl.ds(tile * LANES, LANES)

            def feature(ref, index):
                here = turned(ref[lanes, :])
                taps = [short_ref[index, j : j + 1, lanes] for j in range(3)]
                return taps[0] * here + taps[1] * down(here) + taps[2] * down(here, 2)

            tail_ref[tile] = feature(key_in, 1) * feature(value_in, 2)


def prep_kernel(
    key_hbm,
    value_hbm,
    query_hbm,
    query2_hbm,
    key2_hbm,
    medium_hbm,
    short_ref,
    key_t,
    value_t,
    query_t,
    query2_t,
    key2_t,
    taps_t,
    rims_out,
    key_in,
    value_in,
    query_in,
    query2_in,
    key2_in,
    medium_in,
    sems,
):
    chunks = sems.shape[1]
    rows = key_hbm.shape[0] // chunks
    fields = (
        (key_hbm, key_in, key_t),
        (value_hbm, value_in, value_t),
        (query_hbm, query_in, query_t),
        (query2_hbm, query2_in, query2_t),
        (key2_hbm, key2_in, key2_t),
        (medium_hbm, medium_in, taps_t),
    )
    copies = []
    for chunk in range(chunks):
        here = pl.ds(chunk * rows, rows)
        for place, (source, target, _) in enumerate(fields):
            copy = pltpu.make_async_copy(
                source.at[here, :], target.at[here, :], sems.at[place, chunk]
            )
            copy.start()
            copies.append(copy)
    for chunk in range(chunks):
        for place in range(len(fields)):
            copies[chunk * len(fields) + place].wait()
        for tile in range(chunk * rows // LANES, (chunk + 1) * rows // LANES):
            lanes = pl.ds(tile * LANES, LANES)
            rims_out[tile] = jnp.zeros((RIMS, LANES), F32)
            for place, (_, source, target) in enumerate(fields):
                if place < 5:
                    target[tile] = turned(source[lanes, :])
                    rims_out[tile, 2 * place : 2 * place + 2, :] = target[tile, T - 2 : T, :]
                else:
                    target[tile, 0:TAPS, :] = turned(source[lanes, :])
                    target[tile, TAPS:HEAD_ROWS, :] = jnp.zeros((HEAD_ROWS - TAPS, LANES), F32)

            def feature(ref, index, time):
                return sum(
                    short_ref[index, j : j + 1, lanes] * ref[tile, time - j : time - j + 1, :]
                    for j in range(3)
                )

            for k in range(2):
                rims_out[tile, 10 + k : 11 + k, :] = feature(query_t, 0, T - 2 + k)
            for k in range(3):
                rims_out[tile, 12 + k : 13 + k, :] = feature(key_t, 1, T // 2 - 1 + k) * feature(
                    value_t, 2, T // 2 - 1 + k
                )


def local_kernel(
    place_ref,
    key_t,
    value_t,
    query_t,
    query2_t,
    key2_t,
    taps_t,
    short_ref,
    second_ref,
    rate_ref,
    amplitude_ref,
    skip_ref,
    forward_ref,
    spectrum_ref,
    inverse_ref,
    taps_out,
    spectrum_out,
    medium_out,
    query_out,
    key2_out,
    enter_out,
    leave_out,
    reach_main_out,
    own_rate_out,
    late_hbm,
    gated_t,
    medium_t,
    query_all,
    key2_all,
    late,
    late_sem,
):
    index = place_ref[0]
    mine = pl.ds(pl.multiple_of((index // MODES) * LANES, LANES), LANES)
    rates = rate_ref[:, mine]
    chosen = sublane(rates.shape) == lax.rem(index, MODES)
    own_rate_out[...] = jnp.sum(jnp.where(chosen, rates, 0.0), axis=0, keepdims=True)

    tiles = key_t.shape[0]
    group = gated_t.shape[1] // LANES
    top = sublane((SEG, LANES)) == 0
    segment = sublane((SEG, LANES)).astype(F32)

    def slabs_of(ref, tile):
        head = [ref[tile, pl.ds(k, SEG, stride=HEAD), :] for k in range(HEAD)]
        main = [ref[tile, pl.ds(HEAD_ROWS + k, SEG, stride=MAIN), :] for k in range(MAIN)]
        return head, main

    def feature(ref, tile, taps_of, index, lanes):
        taps = [spread(taps_of[index, j : j + 1, lanes]) for j in range(3)]
        head, main = with_rims(*slabs_of(ref, tile))
        return fir3(head, taps) + fir3(main, taps)

    def body(step, _):
        for part in range(group):
            tile = step * group + part
            lanes = pl.ds(pl.multiple_of(tile * LANES, LANES), LANES)
            local = pl.ds(part * LANES, LANES)
            keys = feature(key_t, tile, short_ref, 1, lanes)
            values = feature(value_t, tile, short_ref, 2, lanes)
            for k in range(HEAD + MAIN):
                gated = keys[k] * values[k]
                if k < 2:
                    gated = jnp.where(top, 0.0, gated)
                gated_t[pl.ds(SEG * k, SEG), local] = gated
            for k, slab in enumerate(feature(query_t, tile, short_ref, 0, lanes)):
                query_all[part, pl.ds(SEG * k, SEG), :] = slab
            query_out[tile] = query_all[part, 0:HEAD_ROWS, :]
            for k, slab in enumerate(feature(key2_t, tile, second_ref, 1, lanes)):
                key2_all[part, pl.ds(SEG * k, SEG), :] = slab
            key2_out[tile] = key2_all[part, 0:HEAD_ROWS, :]
            for k, slab in enumerate(feature(query2_t, tile, second_ref, 0, lanes)):
                late[tile, pl.ds(SEG * k, SEG), :] = slab
            for k in range(HEAD):
                taps_out[tile, pl.ds(SEG * k, SEG), :] = taps_t[
                    tile, pl.ds(k, SEG, stride=HEAD), :
                ]

        filters = [taps_t[step * group + part, 0:TAPS, :] for part in range(group)]
        spectrum = matmul3(spectrum_ref[...], jnp.concatenate(filters, 1))
        both = matmul3(forward_ref[...], gated_t[...])
        first = spectral_product(both[:T], spectrum)
        second = spectral_product(both[T:], spectrum)
        medium_t[...] = matmul3(inverse_ref[...], jnp.concatenate([first, second], 0))

        for part in range(group):
            tile = step * group + part
            lanes = pl.ds(pl.multiple_of(tile * LANES, LANES), LANES)
            local = pl.ds(part * LANES, LANES)
            spectrum_out[tile] = spectrum[:, part * LANES : (part + 1) * LANES]
            medium_out[tile] = medium_t[0:HEAD_ROWS, local]
            taps = [spread(second_ref[2, j : j + 1, lanes]) for j in range(3)]
            firsts = [
                rows_of(medium_t, k, local) * query_all[part, pl.ds(SEG * k, SEG), :]
                for k in range(HEAD - 2, HEAD + MAIN)
            ]
            ends = [down(firsts[0]), down(firsts[1])]
            main = firsts[2:]
            main_all = [jnp.where(top, ends[k], down(main[MAIN - 2 + k])) for k in range(2)] + main
            values2 = fir3(main_all, taps)
            inputs = [
                key2_all[part, pl.ds(SEG * (HEAD + k), SEG), :] * values2[k] for k in range(MAIN)
            ]
            rates, gains = rate_ref[:, lanes], amplitude_ref[:, lanes]
            decays = jnp.exp(-rates)
            outs, ends = recurrence(
                inputs,
                [spread(decays[r : r + 1]) for r in range(MODES)],
                [spread(gains[r : r + 1]) for r in range(MODES)],
                spread(skip_ref[:, lanes]),
            )
            for k in range(MAIN):
                late[tile, pl.ds(T + SEG * k, SEG), :] = outs[k]
            pltpu.make_async_copy(late.at[tile], late_hbm.at[tile], late_sem.at[tile]).start()
            powers = segment_powers(rates, float(MAIN))
            for r in range(MODES):
                enter, leave = prefix(ends[r], powers, r)
                enter_out[tile, r] = enter
                leave_out[tile, r : r + 1, :] = leave
                rate = spread(rates[r : r + 1])
                reach_main_out[tile, r] = jnp.exp(-(rate * (segment * float(MAIN))))
        return _

    lax.fori_loop(0, tiles // group, body, 0)
    for tile in range(tiles):
        pltpu.make_async_copy(late.at[tile], late_hbm.at[tile], late_sem.at[tile]).wait()


def join_kernel(
    halo_ref,
    rims_ref,
    spectrum_ref,
    medium_ref,
    taps_ref,
    query_ref,
    key2_ref,
    key_t,
    value_t,
    enter_main_ref,
    leave_main_ref,
    reach_main_ref,
    short_ref,
    second_ref,
    rate_ref,
    amplitude_ref,
    skip_ref,
    forward_ref,
    inverse_ref,
    state_out,
    late_hbm,
    medium_t,
    late,
    late_sem,
):
    tiles = halo_ref.shape[0]
    group = medium_t.shape[1] // LANES
    top = sublane((SEG, LANES)) == 0

    def body(step, _):
        tile_list = [step * group + part for part in range(group)]
        halo = matmul3(
            forward_ref[...], jnp.concatenate([halo_ref[tile] for tile in tile_list], 1)
        )
        filters = jnp.concatenate([spectrum_ref[tile] for tile in tile_list], 1)
        medium_t[...] = matmul3(inverse_ref[...], spectral_product(halo, filters))
        for part, tile in enumerate(tile_list):
            one(tile, pl.ds(part * LANES, LANES))
        return _

    def one(tile, local):
        lanes = pl.ds(pl.multiple_of(tile * LANES, LANES), LANES)

        def rim(k):
            return rims_ref[tile, k : k + 1, :]

        def taps_of(ref, index):
            return [ref[index, j : j + 1, lanes] for j in range(3)]

        def early(ref, place, index):
            taps = taps_of(short_ref, index)
            zero, one = ref[tile, 0:1, :], ref[tile, 1:2, :]
            older, last = rim(2 * place), rim(2 * place + 1)
            return (
                taps[0] * zero + taps[1] * last + taps[2] * older,
                taps[0] * one + taps[1] * zero + taps[2] * last,
            )

        def mended(ref, place, taps):
            slabs = [ref[tile, pl.ds(SEG * k, SEG), :] for k in range(HEAD)]
            older, last = rim(2 * place), rim(2 * place + 1)
            slabs[0] = slabs[0] + jnp.where(top, spread(taps[1] * last + taps[2] * older), 0.0)
            slabs[1] = slabs[1] + jnp.where(top, spread(taps[2] * last), 0.0)
            return slabs

        def tap(j):
            row = SEG * (j % HEAD) + j // HEAD
            return taps_ref[tile, row : row + 1, :]

        keys, values = early(key_t, 0, 1), early(value_t, 1, 2)
        gated = [spread(keys[k] * values[k]) for k in range(2)]
        taps = [taps_ref[tile, pl.ds(SEG * k, SEG), :] for k in range(HEAD)]
        shifted = [jnp.where(top, 0.0, down(taps[HEAD - 1]))] + taps
        query = mended(query_ref, 2, taps_of(short_ref, 0))
        key2 = mended(key2_ref, 4, taps_of(second_ref, 1))
        mediums = [
            medium_ref[tile, pl.ds(SEG * k, SEG), :]
            + rows_of(medium_t, k, local)
            + taps[k] * gated[0]
            + shifted[k] * gated[1]
            for k in range(HEAD)
        ]
        far, farther, farthest = rim(14), rim(13), rim(12)
        mediums[0] = mediums[0] + jnp.where(top, spread(tap(127) * far), 0.0)
        older = medium_t[HEAD_ROWS : HEAD_ROWS + 1, local] + (
            tap(125) * far + tap(126) * farther + tap(127) * farthest
        )
        last = medium_t[HEAD_ROWS + 1 : HEAD_ROWS + 2, local] + (
            tap(126) * far + tap(127) * farther
        )
        firsts = [query[k] * mediums[k] for k in range(HEAD)]
        firsts_all, _ = with_rims(firsts, None, (spread(rim(10) * older), spread(rim(11) * last)))
        values2 = fir3(firsts_all, [spread(t) for t in taps_of(second_ref, 2)])
        inputs = [key2[k] * values2[k] for k in range(HEAD)]
        rates, gains = rate_ref[:, lanes], amplitude_ref[:, lanes]
        decays = jnp.exp(-rates)
        outs, ends = recurrence(
            inputs,
            [spread(decays[r : r + 1]) for r in range(MODES)],
            [spread(gains[r : r + 1]) for r in range(MODES)],
            spread(skip_ref[:, lanes]),
        )
        for k in range(HEAD):
            late[tile, pl.ds(SEG * k, SEG), :] = outs[k]
        powers = segment_powers(rates, float(HEAD))
        whole = jnp.exp(-float(MAIN_ROWS) * rates)
        for r in range(MODES):
            enter, leave = prefix(ends[r], powers, r)
            late[tile, pl.ds(HEAD_ROWS + SEG * r, SEG), :] = enter
            late[tile, pl.ds(HEAD_ROWS + SEG * (MODES + r), SEG), :] = enter_main_ref[
                tile, r
            ] + reach_main_ref[tile, r] * spread(leave)
            state_out[tile, r : r + 1, :] = (
                leave_main_ref[tile, r : r + 1, :] + leave * whole[r : r + 1]
            )
        pltpu.make_async_copy(late.at[tile], late_hbm.at[tile], late_sem.at[tile]).start()

    lax.fori_loop(0, tiles // group, body, 0, unroll=True)
    for tile in range(tiles):
        pltpu.make_async_copy(late.at[tile], late_hbm.at[tile], late_sem.at[tile]).wait()


def scan_kernel(state_ref, rate_ref, out_ref):
    blocks = state_ref.shape[0]
    position = sublane(state_ref.shape)
    rate = rate_ref[...]
    total = state_ref[...]
    distance = 1
    while distance < blocks:
        moved = jnp.where(position >= distance, down(total, distance), 0.0)
        total = total + jnp.exp(-(float(T) * distance) * rate) * moved
        distance *= 2
    out_ref[...] = jnp.where(position >= 1, down(total), 0.0)


def finish_kernel(
    state_ref,
    early_hbm,
    late_hbm,
    rims_ref,
    second_ref,
    rate_ref,
    gain_ref,
    mixed_out,
    squares_out,
    early,
    late,
    reach,
    squares_t,
    sems,
):
    tiles = early_hbm.shape[0]
    chunks = sems.shape[1]
    count = tiles // chunks
    copies = []
    for chunk in range(chunks):
        here = pl.ds(chunk * count, count)
        for place, (source, target) in enumerate(((early_hbm, early), (late_hbm, late))):
            copy = pltpu.make_async_copy(source.at[here], target.at[here], sems.at[place, chunk])
            copy.start()
            copies.append(copy)
    squares_t[...] = jnp.zeros_like(squares_t)
    top = sublane((SEG, LANES)) == 0
    segment = sublane((SEG, LANES)).astype(F32)

    def reaches(tile, _):
        lanes = pl.ds(pl.multiple_of(tile * LANES, LANES), LANES)
        for r in range(MODES):
            rate = spread(rate_ref[r : r + 1, lanes])
            reach[tile, r] = jnp.exp(-(rate * (segment * float(HEAD))))
            reach[tile, MODES + r] = jnp.exp(-(rate * (segment * float(MAIN) + float(HEAD_ROWS))))
        return _

    lax.fori_loop(0, tiles, reaches, 0)

    def body(tile, _):
        lanes = pl.ds(pl.multiple_of(tile * LANES, LANES), LANES)
        decays = jnp.exp(-rate_ref[:, lanes])
        taps = [second_ref[0, j : j + 1, lanes] for j in range(3)]
        older, last = rims_ref[tile, 6:7, :], rims_ref[tile, 7:8, :]
        mends = [spread(taps[1] * last + taps[2] * older), spread(taps[2] * last)]
        gain = spread(gain_ref[:, lanes])
        states = state_ref[tile]
        decay = [spread(decays[r : r + 1]) for r in range(MODES)]

        def half(length, half_index, own_ref, own_row, first_row):
            enter_row = HEAD_ROWS + half_index * MODES * SEG
            carry = [
                late[tile, pl.ds(enter_row + SEG * r, SEG), :]
                + reach[tile, half_index * MODES + r] * spread(states[r : r + 1])
                for r in range(MODES)
            ]
            for k in range(length):
                carry = [decay[r] * carry[r] for r in range(MODES)]
                total = own_ref[tile, pl.ds(own_row + SEG * k, SEG), :]
                for value in carry:
                    total = total + value
                rows = pl.ds(first_row + SEG * k, SEG)
                query = early[tile, rows, :]
                if first_row == 0 and k < 2:
                    query = query + jnp.where(top, mends[k], 0.0)
                mixed = query * total
                squares_t[rows, :] = squares_t[rows, :] + mixed * mixed
                mixed_out[tile, pl.ds(first_row + k, SEG, stride=length), :] = mixed * gain

        half(HEAD, 0, late, 0, 0)
        half(MAIN, 1, early, T, HEAD_ROWS)
        return _

    for chunk in range(chunks):
        copies[2 * chunk].wait()
        copies[2 * chunk + 1].wait()
        lax.fori_loop(chunk * count, (chunk + 1) * count, body, 0)
    sums = jnp.sum(squares_t[...], axis=1, keepdims=True)
    squares_t[...] = jnp.broadcast_to(sums, squares_t.shape)
    head = [squares_t[pl.ds(i, HEAD, stride=SEG), :] for i in range(SEG)]
    main = [squares_t[pl.ds(HEAD_ROWS + i, MAIN, stride=SEG), :] for i in range(SEG)]
    ordered = jnp.concatenate(head + main, 0)
    squares_out[...] = ordered.T[0:1, :]


def scale_kernel(divisor, mixed_ref, squares_ref, out_hbm, out_t, sems):
    scale = lax.rsqrt(squares_ref[...] / divisor + norm_eps)
    chunks = sems.shape[0]
    tiles = mixed_ref.shape[0] // chunks
    copies = []
    for chunk in range(chunks):
        for tile in range(chunk * tiles, (chunk + 1) * tiles):
            out_t[pl.ds(tile * LANES, LANES), :] = mixed_ref[tile].T * scale
        rows = pl.ds(chunk * tiles * LANES, tiles * LANES)
        copy = pltpu.make_async_copy(out_t.at[rows, :], out_hbm.at[rows, :], sems.at[chunk])
        copy.start()
        copies.append(copy)
    for copy in copies:
        copy.wait()


def from_behind(block):
    count = lax.axis_size("seq")
    return lax.ppermute(block, "seq", [(i, i + 1) for i in range(count - 1)])


def in_hbm(x):
    return pltpu.with_memory_space_constraint(x, pltpu.HBM)


def call(kernel, in_specs, out_specs, out_shape, scratch, flops, size, name):
    return pl.pallas_call(
        kernel,
        in_specs=in_specs,
        out_specs=out_specs,
        out_shape=out_shape,
        scratch_shapes=scratch,
        compiler_params=pltpu.CompilerParams(vmem_limit_bytes=LIMIT),
        cost_estimate=pl.CostEstimate(flops=flops, bytes_accessed=size, transcendentals=0),
        name=name,
    )


def exchange(rows):
    count, lanes = rows.shape
    return lax.all_to_all(
        rows.reshape(count, 1, lanes), "seq", split_axis=0, concat_axis=0, tiled=True
    ).reshape(count, lanes)


def local(
    query_proj,
    key_proj,
    value_proj,
    second_query,
    second_key,
    short_filter,
    second_short,
    medium_filter,
    decay_rate,
    residue,
    skip_gain,
    norm_gain,
):
    channels = query_proj.shape[0]
    count = lax.axis_size("seq")
    tiles = channels // LANES
    group = min(4, tiles)
    join_group = min(2, tiles)
    chunks = min(4, tiles)
    short_t = jnp.transpose(short_filter, (0, 2, 1))
    second_t = jnp.transpose(second_short, (0, 2, 1))
    rate_t = decay_rate.T
    amplitude = residue.T * jnp.sqrt(-jnp.expm1(-2.0 * rate_t))
    skip = skip_gain[None, :]
    gain = norm_gain[None, :]
    forward, spectrum, inverse, halo_forward, halo_inverse = tables()
    held = pl.BlockSpec(memory_space=pltpu.VMEM)
    outside = pl.BlockSpec(memory_space=pl.ANY)
    words = channels * T

    def struct(*shape):
        return jax.ShapeDtypeStruct(shape, F32)

    def hbm(*shape):
        return pltpu.HBM(shape, F32)

    fields = [
        in_hbm(x) for x in (key_proj, value_proj, query_proj, second_query, second_key, medium_filter)
    ]
    tail = call(
        tail_kernel,
        [outside] * 3,
        held,
        struct(tiles, TAPS, LANES),
        [pltpu.VMEM((channels, LANES), F32)] * 2
        + [pltpu.VMEM((3, 3, channels), F32)]
        + [pltpu.SemaphoreType.DMA((chunks,))] * 2
        + [pltpu.SemaphoreType.DMA],
        words * 8,
        words * 6,
        "tail",
    )(fields[0], fields[1], in_hbm(short_t))
    halo = from_behind(tail)

    *turned_fields, taps_t, rims = call(
        prep_kernel,
        [outside] * 6 + [held],
        [held] * 7,
        [struct(tiles, T, LANES)] * 5
        + [struct(tiles, HEAD_ROWS, LANES), struct(tiles, RIMS, LANES)],
        [pltpu.VMEM((channels, T), F32)] * 5
        + [pltpu.VMEM((channels, TAPS), F32), pltpu.SemaphoreType.DMA((6, chunks))],
        words * 20,
        words * 40,
        "prep",
    )(*fields, short_t)
    border = from_behind(rims)

    place = lax.axis_index("seq").astype(jnp.int32).reshape(1)
    (
        taps,
        tap_spectrum,
        medium,
        query,
        key2,
        enter_main,
        leave_main,
        reach_main,
        own_rate,
        early,
    ) = call(
        local_kernel,
        [pl.BlockSpec(memory_space=pltpu.SMEM)] + [held] * 14,
        [held] * 9 + [outside],
        [
            struct(tiles, HEAD_ROWS, LANES),
            struct(tiles, 384, LANES),
            struct(tiles, HEAD_ROWS, LANES),
            struct(tiles, HEAD_ROWS, LANES),
            struct(tiles, HEAD_ROWS, LANES),
            struct(tiles, MODES, SEG, LANES),
            struct(tiles, MODES, LANES),
            struct(tiles, MODES, SEG, LANES),
            struct(1, LANES),
            hbm(tiles, T + MAIN_ROWS, LANES),
        ],
        [pltpu.VMEM((T, group * LANES), F32)] * 2
        + [pltpu.VMEM((group, T, LANES), F32)] * 2
        + [pltpu.VMEM((tiles, T + MAIN_ROWS, LANES), F32), pltpu.SemaphoreType.DMA((tiles,))],
        words * 8000,
        words * 60,
        "local",
    )(
        place,
        *turned_fields,
        taps_t,
        short_t,
        second_t,
        rate_t,
        amplitude,
        skip,
        forward,
        spectrum,
        inverse,
    )

    late_rows = HEAD_ROWS + 2 * MODES * SEG
    state, late = call(
        join_kernel,
        [held] * 19,
        [held, outside],
        [struct(tiles, MODES, LANES), hbm(tiles, late_rows, LANES)],
        [
            pltpu.VMEM((HEAD_ROWS + 8, join_group * LANES), F32),
            pltpu.VMEM((tiles, late_rows, LANES), F32),
            pltpu.SemaphoreType.DMA((tiles,)),
        ],
        words * 2000,
        words * 20,
        "join",
    )(
        halo,
        border,
        tap_spectrum,
        medium,
        taps,
        query,
        key2,
        turned_fields[0],
        turned_fields[1],
        enter_main,
        leave_main,
        reach_main,
        short_t,
        second_t,
        rate_t,
        amplitude,
        skip,
        halo_forward,
        halo_inverse,
    )

    scanned = call(
        scan_kernel,
        [held] * 2,
        held,
        struct(count, LANES),
        [],
        count * LANES * 30,
        count * LANES * 8,
        "scan",
    )(exchange(state.reshape(count, LANES)), own_rate)
    incoming = exchange(scanned).reshape(tiles, MODES, LANES)

    mixed, squares = call(
        finish_kernel,
        [held, outside, outside] + [held] * 4,
        [held] * 2,
        [struct(tiles, T, LANES), struct(1, T)],
        [
            pltpu.VMEM((tiles, T + MAIN_ROWS, LANES), F32),
            pltpu.VMEM((tiles, late_rows, LANES), F32),
            pltpu.VMEM((tiles, 2 * MODES, SEG, LANES), F32),
            pltpu.VMEM((T, LANES), F32),
            pltpu.SemaphoreType.DMA((2, chunks)),
        ],
        words * 40,
        words * 16,
        "finish",
    )(incoming, in_hbm(early), in_hbm(late), border, second_t, rate_t, gain)
    total = lax.psum(squares, "chan")
    return call(
        functools.partial(scale_kernel, float(channels * lax.axis_size("chan"))),
        [held, held],
        outside,
        struct(channels, T),
        [pltpu.VMEM((channels, T), F32), pltpu.SemaphoreType.DMA((chunks,))],
        words,
        words * 8,
        "scale",
    )(mixed, total)


def solution(mesh):
    return jax.shard_map(
        local,
        mesh=mesh,
        in_specs=(
            P("chan", "seq"),
            P("chan", "seq"),
            P("chan", "seq"),
            P("chan", "seq"),
            P("chan", "seq"),
            P(None, "chan", None),
            P(None, "chan", None),
            P("chan", None),
            P("chan", None),
            P("chan", None),
            P("chan"),
            P("chan"),
        ),
        out_specs=P("chan", "seq"),
        check_vma=False,
    )
```

```python
import functools

import jax
import jax.numpy as jnp
import ml_dtypes
import numpy as np
from jax import lax
from jax.experimental import pallas as pl
from jax.experimental.pallas import tpu as pltpu
from jax.sharding import PartitionSpec as P

norm_eps = 1e-06

T = 256
TAPS = 128
MODES = 8
LANES = 128
SEG = 8
HEAD = 17
MAIN = 15
HEAD_ROWS = HEAD * SEG
MAIN_ROWS = MAIN * SEG
RIMS = 16
LIMIT = 24 * 1024 * 1024

F32 = jnp.float32
BF16 = jnp.bfloat16


def row_times():
    head = [HEAD * i + k for k in range(HEAD) for i in range(SEG)]
    main = [HEAD_ROWS + MAIN * i + k for k in range(MAIN) for i in range(SEG)]
    return np.array(head + main)


def packed_forward(slots):
    k = np.arange(128)[:, None]
    angle = 2.0 * np.pi * k * np.asarray(slots)[None, :] / 256.0
    imag = -np.sin(angle)
    imag[0] = np.cos(np.pi * np.asarray(slots))
    return np.concatenate([np.cos(angle), imag], 0)


def packed_inverse(slots):
    k = np.arange(128)[None, :]
    angle = 2.0 * np.pi * k * np.asarray(slots)[:, None] / 256.0
    real = 2.0 * np.cos(angle)
    real[:, 0] = 1.0
    imag = -2.0 * np.sin(angle)
    imag[:, 0] = np.cos(np.pi * np.asarray(slots))
    return np.concatenate([real, imag], 1) / 256.0


def three_pass(matrix):
    high = matrix.astype(ml_dtypes.bfloat16)
    low = (matrix - high.astype(np.float64)).astype(ml_dtypes.bfloat16)
    return np.concatenate([high, low, high], 1)


def tables():
    times = row_times()
    first = packed_forward(times + 128) * (times < 128)[None, :]
    second = packed_forward(times)
    forward = np.concatenate([first, second], 0)
    taps = packed_forward(np.arange(TAPS))
    real, imag = taps[:128], taps[128:].copy()
    cross = real.copy()
    cross[0] = imag[0]
    imag[0] = 0.0
    spectrum = np.concatenate([real, imag, cross], 0)
    inverse = np.concatenate(
        [
            packed_inverse(times + 128) * (times < 128)[:, None],
            packed_inverse(times) * (times >= 128)[:, None],
        ],
        1,
    )
    halo = packed_forward(np.arange(128))
    halo[:, :2] = 0.0
    head_times = np.concatenate([times[:HEAD_ROWS], [-2, -1], np.full(6, 255)])
    halo_back = packed_inverse(head_times + 128) * (head_times < 128)[:, None]
    return [three_pass(m) for m in (forward, spectrum, inverse, halo, halo_back)]


def halves(x):
    high = x.astype(BF16)
    low = (x - high.astype(F32)).astype(BF16)
    return high, low


def matmul3(matrix, x):
    high, low = halves(x)
    stacked = jnp.concatenate([high, high, low], 0)
    return jnp.dot(matrix, stacked, preferred_element_type=F32)


def spectral_product(x, taps):
    real, imag = x[:128], x[128:]
    tap_real, tap_imag, tap_cross = taps[:128], taps[128:256], taps[256:]
    return jnp.concatenate(
        [real * tap_real - imag * tap_imag, real * tap_imag + imag * tap_cross], 0
    )


def sublane(shape):
    return lax.broadcasted_iota(jnp.int32, shape, 0)


def down(x, distance=1):
    return pltpu.roll(x, distance, axis=0)


def fir3(slabs, taps):
    return [
        taps[0] * slabs[k + 2] + taps[1] * slabs[k + 1] + taps[2] * slabs[k]
        for k in range(len(slabs) - 2)
    ]


def with_rims(head, main, rims=None):
    top = sublane(head[0].shape) == 0
    zero = jnp.zeros_like(head[0])
    before = (zero, zero) if rims is None else rims
    ends = [down(head[HEAD - 2]), down(head[HEAD - 1])]
    head_all = [jnp.where(top, before[k], ends[k]) for k in range(2)] + head
    if main is None:
        return head_all, None
    main_all = [jnp.where(top, ends[k], down(main[MAIN - 2 + k])) for k in range(2)] + main
    return head_all, main_all


def rows_of(ref, k, lanes):
    return ref[pl.ds(SEG * k, SEG), lanes]


def spread(row):
    return jnp.broadcast_to(row, (SEG, row.shape[1]))


def recurrence(inputs, decays, gains, skip):
    states = [gains[r] * inputs[0] for r in range(MODES)]
    outs = []
    for k, value in enumerate(inputs):
        if k:
            states = [decays[r] * states[r] + gains[r] * value for r in range(MODES)]
        total = skip * value
        for state in states:
            total = total + state
        outs.append(total)
    return outs, states


def segment_powers(rates, step):
    return [jnp.exp(-(step * distance) * rates) for distance in (1, 2, 4)]


def prefix(state, powers, mode):
    place = sublane(state.shape)
    total = state
    for power, distance in zip(powers, (1, 2, 4)):
        moved = jnp.where(place >= distance, down(total, distance), 0.0)
        total = total + spread(power[mode : mode + 1]) * moved
    return jnp.where(place >= 1, down(total), 0.0), total[SEG - 1 :]


def turned(block):
    return block.T


def tail_kernel(
    place_ref,
    key_hbm,
    value_hbm,
    short_hbm,
    rate_hbm,
    tail_ref,
    own_rate_out,
    key_in,
    value_in,
    short_ref,
    rates_in,
    key_sem,
    value_sem,
    short_sem,
    rate_sem,
):
    chunks = key_sem.shape[0]
    rows = key_hbm.shape[0] // chunks
    copies = []
    filters = pltpu.make_async_copy(short_hbm, short_ref, short_sem)
    filters.start()
    index = place_ref[0]
    mine = pl.ds(pl.multiple_of((index // MODES) * LANES, LANES), LANES)
    rates = pltpu.make_async_copy(rate_hbm.at[:, mine], rates_in, rate_sem)
    rates.start()
    for chunk in range(chunks):
        here = pl.ds(chunk * rows, rows)
        for source, target, sem in (
            (key_hbm, key_in, key_sem),
            (value_hbm, value_in, value_sem),
        ):
            copy = pltpu.make_async_copy(
                source.at[here, pl.ds(LANES, LANES)], target.at[here, :], sem.at[chunk]
            )
            copy.start()
            copies.append(copy)
    filters.wait()
    for chunk in range(chunks):
        copies[2 * chunk].wait()
        copies[2 * chunk + 1].wait()
        for tile in range(chunk * rows // LANES, (chunk + 1) * rows // LANES):
            lanes = pl.ds(tile * LANES, LANES)

            def feature(ref, index):
                here = turned(ref[lanes, :])
                taps = [short_ref[index, j : j + 1, lanes] for j in range(3)]
                return taps[0] * here + taps[1] * down(here) + taps[2] * down(here, 2)

            tail_ref[tile] = feature(key_in, 1) * feature(value_in, 2)
    rates.wait()
    chosen = sublane(rates_in.shape) == lax.rem(index, MODES)
    own_rate_out[...] = jnp.sum(jnp.where(chosen, rates_in[...], 0.0), axis=0, keepdims=True)


def prep_kernel(
    key_hbm,
    value_hbm,
    query_hbm,
    query2_hbm,
    key2_hbm,
    medium_hbm,
    short_ref,
    key_t,
    value_t,
    query_t,
    query2_t,
    key2_t,
    taps_t,
    rims_out,
    key_in,
    value_in,
    query_in,
    query2_in,
    key2_in,
    medium_in,
    sems,
):
    chunks = sems.shape[1]
    rows = key_hbm.shape[0] // chunks
    fields = (
        (key_hbm, key_in, key_t),
        (value_hbm, value_in, value_t),
        (query_hbm, query_in, query_t),
        (query2_hbm, query2_in, query2_t),
        (key2_hbm, key2_in, key2_t),
        (medium_hbm, medium_in, taps_t),
    )
    copies = []
    for chunk in range(chunks):
        here = pl.ds(chunk * rows, rows)
        for place, (source, target, _) in enumerate(fields):
            copy = pltpu.make_async_copy(
                source.at[here, :], target.at[here, :], sems.at[place, chunk]
            )
            copy.start()
            copies.append(copy)
    for chunk in range(chunks):
        for place in range(len(fields)):
            copies[chunk * len(fields) + place].wait()
        for tile in range(chunk * rows // LANES, (chunk + 1) * rows // LANES):
            lanes = pl.ds(tile * LANES, LANES)
            rims_out[tile] = jnp.zeros((RIMS, LANES), F32)
            for place, (_, source, target) in enumerate(fields):
                if place < 5:
                    target[tile] = turned(source[lanes, :])
                    rims_out[tile, 2 * place : 2 * place + 2, :] = target[tile, T - 2 : T, :]
                else:
                    target[tile, 0:TAPS, :] = turned(source[lanes, :])
                    target[tile, TAPS:HEAD_ROWS, :] = jnp.zeros((HEAD_ROWS - TAPS, LANES), F32)

            def feature(ref, index, time):
                return sum(
                    short_ref[index, j : j + 1, lanes] * ref[tile, time - j : time - j + 1, :]
                    for j in range(3)
                )

            for k in range(2):
                rims_out[tile, 10 + k : 11 + k, :] = feature(query_t, 0, T - 2 + k)
            for k in range(3):
                rims_out[tile, 12 + k : 13 + k, :] = feature(key_t, 1, T // 2 - 1 + k) * feature(
                    value_t, 2, T // 2 - 1 + k
                )


def local_kernel(
    key_t,
    value_t,
    query_t,
    query2_t,
    key2_t,
    taps_t,
    short_ref,
    second_ref,
    rate_ref,
    amplitude_ref,
    skip_ref,
    forward_ref,
    spectrum_ref,
    inverse_ref,
    taps_out,
    spectrum_out,
    medium_out,
    query_out,
    key2_out,
    enter_out,
    leave_out,
    reach_main_out,
    late_hbm,
    gated_t,
    medium_t,
    query_all,
    key2_all,
    late,
    late_sem,
):

    tiles = key_t.shape[0]
    group = gated_t.shape[1] // LANES
    top = sublane((SEG, LANES)) == 0
    segment = sublane((SEG, LANES)).astype(F32)

    def slabs_of(ref, tile):
        head = [ref[tile, pl.ds(k, SEG, stride=HEAD), :] for k in range(HEAD)]
        main = [ref[tile, pl.ds(HEAD_ROWS + k, SEG, stride=MAIN), :] for k in range(MAIN)]
        return head, main

    def feature(ref, tile, taps_of, index, lanes):
        taps = [spread(taps_of[index, j : j + 1, lanes]) for j in range(3)]
        head, main = with_rims(*slabs_of(ref, tile))
        return fir3(head, taps) + fir3(main, taps)

    def body(step, _):
        for part in range(group):
            tile = step * group + part
            lanes = pl.ds(pl.multiple_of(tile * LANES, LANES), LANES)
            local = pl.ds(part * LANES, LANES)
            keys = feature(key_t, tile, short_ref, 1, lanes)
            values = feature(value_t, tile, short_ref, 2, lanes)
            for k in range(HEAD + MAIN):
                gated = keys[k] * values[k]
                if k < 2:
                    gated = jnp.where(top, 0.0, gated)
                gated_t[pl.ds(SEG * k, SEG), local] = gated
            for k, slab in enumerate(feature(query_t, tile, short_ref, 0, lanes)):
                query_all[part, pl.ds(SEG * k, SEG), :] = slab
            query_out[tile] = query_all[part, 0:HEAD_ROWS, :]
            for k, slab in enumerate(feature(key2_t, tile, second_ref, 1, lanes)):
                key2_all[part, pl.ds(SEG * k, SEG), :] = slab
            key2_out[tile] = key2_all[part, 0:HEAD_ROWS, :]
            for k, slab in enumerate(feature(query2_t, tile, second_ref, 0, lanes)):
                late[tile, pl.ds(SEG * k, SEG), :] = slab
            for k in range(HEAD):
                taps_out[tile, pl.ds(SEG * k, SEG), :] = taps_t[
                    tile, pl.ds(k, SEG, stride=HEAD), :
                ]

        filters = [taps_t[step * group + part, 0:TAPS, :] for part in range(group)]
        spectrum = matmul3(spectrum_ref[...], jnp.concatenate(filters, 1))
        both = matmul3(forward_ref[...], gated_t[...])
        first = spectral_product(both[:T], spectrum)
        second = spectral_product(both[T:], spectrum)
        medium_t[...] = matmul3(inverse_ref[...], jnp.concatenate([first, second], 0))

        for part in range(group):
            tile = step * group + part
            lanes = pl.ds(pl.multiple_of(tile * LANES, LANES), LANES)
            local = pl.ds(part * LANES, LANES)
            spectrum_out[tile] = spectrum[:, part * LANES : (part + 1) * LANES]
            medium_out[tile] = medium_t[0:HEAD_ROWS, local]
            taps = [spread(second_ref[2, j : j + 1, lanes]) for j in range(3)]
            firsts = [
                rows_of(medium_t, k, local) * query_all[part, pl.ds(SEG * k, SEG), :]
                for k in range(HEAD - 2, HEAD + MAIN)
            ]
            ends = [down(firsts[0]), down(firsts[1])]
            main = firsts[2:]
            main_all = [jnp.where(top, ends[k], down(main[MAIN - 2 + k])) for k in range(2)] + main
            values2 = fir3(main_all, taps)
            inputs = [
                key2_all[part, pl.ds(SEG * (HEAD + k), SEG), :] * values2[k] for k in range(MAIN)
            ]
            rates, gains = rate_ref[:, lanes], amplitude_ref[:, lanes]
            decays = jnp.exp(-rates)
            outs, ends = recurrence(
                inputs,
                [spread(decays[r : r + 1]) for r in range(MODES)],
                [spread(gains[r : r + 1]) for r in range(MODES)],
                spread(skip_ref[:, lanes]),
            )
            for k in range(MAIN):
                late[tile, pl.ds(T + SEG * k, SEG), :] = outs[k]
            pltpu.make_async_copy(late.at[tile], late_hbm.at[tile], late_sem.at[tile]).start()
            powers = segment_powers(rates, float(MAIN))
            for r in range(MODES):
                enter, leave = prefix(ends[r], powers, r)
                enter_out[tile, r] = enter
                leave_out[tile, r : r + 1, :] = leave
                rate = spread(rates[r : r + 1])
                reach_main_out[tile, r] = jnp.exp(-(rate * (segment * float(MAIN))))
        return _

    lax.fori_loop(0, tiles // group, body, 0)
    for tile in range(tiles):
        pltpu.make_async_copy(late.at[tile], late_hbm.at[tile], late_sem.at[tile]).wait()


def join_kernel(
    halo_ref,
    rims_ref,
    spectrum_ref,
    medium_ref,
    taps_ref,
    query_ref,
    key2_ref,
    key_t,
    value_t,
    enter_main_ref,
    leave_main_ref,
    reach_main_ref,
    short_ref,
    second_ref,
    rate_ref,
    amplitude_ref,
    skip_ref,
    forward_ref,
    inverse_ref,
    state_out,
    late_hbm,
    medium_t,
    late,
    late_sem,
):
    tiles = halo_ref.shape[0]
    group = medium_t.shape[1] // LANES
    top = sublane((SEG, LANES)) == 0

    def body(step, _):
        tile_list = [step * group + part for part in range(group)]
        halo = matmul3(
            forward_ref[...], jnp.concatenate([halo_ref[tile] for tile in tile_list], 1)
        )
        filters = jnp.concatenate([spectrum_ref[tile] for tile in tile_list], 1)
        medium_t[...] = matmul3(inverse_ref[...], spectral_product(halo, filters))
        for part, tile in enumerate(tile_list):
            one(tile, pl.ds(part * LANES, LANES))
        return _

    def one(tile, local):
        lanes = pl.ds(pl.multiple_of(tile * LANES, LANES), LANES)

        def rim(k):
            return rims_ref[tile, k : k + 1, :]

        def taps_of(ref, index):
            return [ref[index, j : j + 1, lanes] for j in range(3)]

        def early(ref, place, index):
            taps = taps_of(short_ref, index)
            zero, one = ref[tile, 0:1, :], ref[tile, 1:2, :]
            older, last = rim(2 * place), rim(2 * place + 1)
            return (
                taps[0] * zero + taps[1] * last + taps[2] * older,
                taps[0] * one + taps[1] * zero + taps[2] * last,
            )

        def mended(ref, place, taps):
            slabs = [ref[tile, pl.ds(SEG * k, SEG), :] for k in range(HEAD)]
            older, last = rim(2 * place), rim(2 * place + 1)
            slabs[0] = slabs[0] + jnp.where(top, spread(taps[1] * last + taps[2] * older), 0.0)
            slabs[1] = slabs[1] + jnp.where(top, spread(taps[2] * last), 0.0)
            return slabs

        def tap(j):
            row = SEG * (j % HEAD) + j // HEAD
            return taps_ref[tile, row : row + 1, :]

        keys, values = early(key_t, 0, 1), early(value_t, 1, 2)
        gated = [spread(keys[k] * values[k]) for k in range(2)]
        taps = [taps_ref[tile, pl.ds(SEG * k, SEG), :] for k in range(HEAD)]
        shifted = [jnp.where(top, 0.0, down(taps[HEAD - 1]))] + taps
        query = mended(query_ref, 2, taps_of(short_ref, 0))
        key2 = mended(key2_ref, 4, taps_of(second_ref, 1))
        mediums = [
            medium_ref[tile, pl.ds(SEG * k, SEG), :]
            + rows_of(medium_t, k, local)
            + taps[k] * gated[0]
            + shifted[k] * gated[1]
            for k in range(HEAD)
        ]
        far, farther, farthest = rim(14), rim(13), rim(12)
        mediums[0] = mediums[0] + jnp.where(top, spread(tap(127) * far), 0.0)
        older = medium_t[HEAD_ROWS : HEAD_ROWS + 1, local] + (
            tap(125) * far + tap(126) * farther + tap(127) * farthest
        )
        last = medium_t[HEAD_ROWS + 1 : HEAD_ROWS + 2, local] + (
            tap(126) * far + tap(127) * farther
        )
        firsts = [query[k] * mediums[k] for k in range(HEAD)]
        firsts_all, _ = with_rims(firsts, None, (spread(rim(10) * older), spread(rim(11) * last)))
        values2 = fir3(firsts_all, [spread(t) for t in taps_of(second_ref, 2)])
        inputs = [key2[k] * values2[k] for k in range(HEAD)]
        rates, gains = rate_ref[:, lanes], amplitude_ref[:, lanes]
        decays = jnp.exp(-rates)
        outs, ends = recurrence(
            inputs,
            [spread(decays[r : r + 1]) for r in range(MODES)],
            [spread(gains[r : r + 1]) for r in range(MODES)],
            spread(skip_ref[:, lanes]),
        )
        for k in range(HEAD):
            late[tile, pl.ds(SEG * k, SEG), :] = outs[k]
        powers = segment_powers(rates, float(HEAD))
        whole = jnp.exp(-float(MAIN_ROWS) * rates)
        for r in range(MODES):
            enter, leave = prefix(ends[r], powers, r)
            late[tile, pl.ds(HEAD_ROWS + SEG * r, SEG), :] = enter
            late[tile, pl.ds(HEAD_ROWS + SEG * (MODES + r), SEG), :] = enter_main_ref[
                tile, r
            ] + reach_main_ref[tile, r] * spread(leave)
            state_out[tile, r : r + 1, :] = (
                leave_main_ref[tile, r : r + 1, :] + leave * whole[r : r + 1]
            )
        pltpu.make_async_copy(late.at[tile], late_hbm.at[tile], late_sem.at[tile]).start()

    lax.fori_loop(0, tiles // group, body, 0, unroll=True)
    for tile in range(tiles):
        pltpu.make_async_copy(late.at[tile], late_hbm.at[tile], late_sem.at[tile]).wait()


def scan_kernel(state_ref, rate_ref, out_ref):
    blocks = state_ref.shape[0]
    position = sublane(state_ref.shape)
    rate = rate_ref[...]
    total = state_ref[...]
    distance = 1
    while distance < blocks:
        moved = jnp.where(position >= distance, down(total, distance), 0.0)
        total = total + jnp.exp(-(float(T) * distance) * rate) * moved
        distance *= 2
    out_ref[...] = jnp.where(position >= 1, down(total), 0.0)


def finish_kernel(
    state_ref,
    early_hbm,
    late_hbm,
    rims_ref,
    second_ref,
    rate_ref,
    gain_ref,
    mixed_out,
    squares_out,
    early,
    late,
    reach,
    squares_t,
    sems,
):
    tiles = early_hbm.shape[0]
    chunks = sems.shape[1]
    count = tiles // chunks
    copies = []
    for chunk in range(chunks):
        here = pl.ds(chunk * count, count)
        for place, (source, target) in enumerate(((early_hbm, early), (late_hbm, late))):
            copy = pltpu.make_async_copy(source.at[here], target.at[here], sems.at[place, chunk])
            copy.start()
            copies.append(copy)
    squares_t[...] = jnp.zeros_like(squares_t)
    top = sublane((SEG, LANES)) == 0
    segment = sublane((SEG, LANES)).astype(F32)

    def reaches(tile, _):
        lanes = pl.ds(pl.multiple_of(tile * LANES, LANES), LANES)
        for r in range(MODES):
            rate = spread(rate_ref[r : r + 1, lanes])
            reach[tile, r] = jnp.exp(-(rate * (segment * float(HEAD))))
            reach[tile, MODES + r] = jnp.exp(-(rate * (segment * float(MAIN) + float(HEAD_ROWS))))
        return _

    lax.fori_loop(0, tiles, reaches, 0)

    def body(tile, _):
        lanes = pl.ds(pl.multiple_of(tile * LANES, LANES), LANES)
        decays = jnp.exp(-rate_ref[:, lanes])
        taps = [second_ref[0, j : j + 1, lanes] for j in range(3)]
        older, last = rims_ref[tile, 6:7, :], rims_ref[tile, 7:8, :]
        mends = [spread(taps[1] * last + taps[2] * older), spread(taps[2] * last)]
        gain = spread(gain_ref[:, lanes])
        states = state_ref[tile]
        decay = [spread(decays[r : r + 1]) for r in range(MODES)]

        def half(length, half_index, own_ref, own_row, first_row):
            enter_row = HEAD_ROWS + half_index * MODES * SEG
            carry = [
                late[tile, pl.ds(enter_row + SEG * r, SEG), :]
                + reach[tile, half_index * MODES + r] * spread(states[r : r + 1])
                for r in range(MODES)
            ]
            for k in range(length):
                carry = [decay[r] * carry[r] for r in range(MODES)]
                total = own_ref[tile, pl.ds(own_row + SEG * k, SEG), :]
                for value in carry:
                    total = total + value
                rows = pl.ds(first_row + SEG * k, SEG)
                query = early[tile, rows, :]
                if first_row == 0 and k < 2:
                    query = query + jnp.where(top, mends[k], 0.0)
                mixed = query * total
                squares_t[rows, :] = squares_t[rows, :] + mixed * mixed
                mixed_out[tile, pl.ds(first_row + k, SEG, stride=length), :] = mixed * gain

        half(HEAD, 0, late, 0, 0)
        half(MAIN, 1, early, T, HEAD_ROWS)
        return _

    for chunk in range(chunks):
        copies[2 * chunk].wait()
        copies[2 * chunk + 1].wait()
        lax.fori_loop(chunk * count, (chunk + 1) * count, body, 0)
    sums = jnp.sum(squares_t[...], axis=1, keepdims=True)
    squares_t[...] = jnp.broadcast_to(sums, squares_t.shape)
    head = [squares_t[pl.ds(i, HEAD, stride=SEG), :] for i in range(SEG)]
    main = [squares_t[pl.ds(HEAD_ROWS + i, MAIN, stride=SEG), :] for i in range(SEG)]
    ordered = jnp.concatenate(head + main, 0)
    squares_out[...] = ordered.T[0:1, :]


def scale_kernel(divisor, mixed_ref, squares_ref, out_hbm, out_t, sems):
    scale = lax.rsqrt(squares_ref[...] / divisor + norm_eps)
    chunks = sems.shape[0]
    tiles = mixed_ref.shape[0] // chunks
    copies = []
    for chunk in range(chunks):
        for tile in range(chunk * tiles, (chunk + 1) * tiles):
            out_t[pl.ds(tile * LANES, LANES), :] = mixed_ref[tile].T * scale
        rows = pl.ds(chunk * tiles * LANES, tiles * LANES)
        copy = pltpu.make_async_copy(out_t.at[rows, :], out_hbm.at[rows, :], sems.at[chunk])
        copy.start()
        copies.append(copy)
    for copy in copies:
        copy.wait()


def from_behind(block):
    count = lax.axis_size("seq")
    return lax.ppermute(block, "seq", [(i, i + 1) for i in range(count - 1)])


def in_hbm(x):
    return pltpu.with_memory_space_constraint(x, pltpu.HBM)


def call(kernel, in_specs, out_specs, out_shape, scratch, flops, size, name):
    return pl.pallas_call(
        kernel,
        in_specs=in_specs,
        out_specs=out_specs,
        out_shape=out_shape,
        scratch_shapes=scratch,
        compiler_params=pltpu.CompilerParams(vmem_limit_bytes=LIMIT),
        cost_estimate=pl.CostEstimate(flops=flops, bytes_accessed=size, transcendentals=0),
        name=name,
    )


def exchange(rows):
    count, lanes = rows.shape
    return lax.all_to_all(
        rows.reshape(count, 1, lanes), "seq", split_axis=0, concat_axis=0, tiled=True
    ).reshape(count, lanes)


def local(
    query_proj,
    key_proj,
    value_proj,
    second_query,
    second_key,
    short_filter,
    second_short,
    medium_filter,
    decay_rate,
    residue,
    skip_gain,
    norm_gain,
):
    channels = query_proj.shape[0]
    count = lax.axis_size("seq")
    tiles = channels // LANES
    group = min(4, tiles)
    join_group = min(2, tiles)
    chunks = min(4, tiles)
    short_t = jnp.transpose(short_filter, (0, 2, 1))
    second_t = jnp.transpose(second_short, (0, 2, 1))
    rate_t = decay_rate.T
    amplitude = residue.T * jnp.sqrt(-jnp.expm1(-2.0 * rate_t))
    skip = skip_gain[None, :]
    gain = norm_gain[None, :]
    forward, spectrum, inverse, halo_forward, halo_inverse = tables()
    held = pl.BlockSpec(memory_space=pltpu.VMEM)
    outside = pl.BlockSpec(memory_space=pl.ANY)
    words = channels * T

    def struct(*shape):
        return jax.ShapeDtypeStruct(shape, F32)

    def hbm(*shape):
        return pltpu.HBM(shape, F32)

    fields = [
        in_hbm(x) for x in (key_proj, value_proj, query_proj, second_query, second_key, medium_filter)
    ]
    place = lax.axis_index("seq").astype(jnp.int32).reshape(1)
    tail, own_rate = call(
        tail_kernel,
        [pl.BlockSpec(memory_space=pltpu.SMEM)] + [outside] * 4,
        [held] * 2,
        [struct(tiles, TAPS, LANES), struct(1, LANES)],
        [pltpu.VMEM((channels, LANES), F32)] * 2
        + [pltpu.VMEM((3, 3, channels), F32), pltpu.VMEM((MODES, LANES), F32)]
        + [pltpu.SemaphoreType.DMA((chunks,))] * 2
        + [pltpu.SemaphoreType.DMA] * 2,
        words * 8,
        words * 6,
        "tail",
    )(place, fields[0], fields[1], in_hbm(short_t), in_hbm(rate_t))
    halo = from_behind(tail)

    *turned_fields, taps_t, rims = call(
        prep_kernel,
        [outside] * 6 + [held],
        [held] * 7,
        [struct(tiles, T, LANES)] * 5
        + [struct(tiles, HEAD_ROWS, LANES), struct(tiles, RIMS, LANES)],
        [pltpu.VMEM((channels, T), F32)] * 5
        + [pltpu.VMEM((channels, TAPS), F32), pltpu.SemaphoreType.DMA((6, chunks))],
        words * 20,
        words * 40,
        "prep",
    )(*fields, short_t)
    border = from_behind(rims)

    (
        taps,
        tap_spectrum,
        medium,
        query,
        key2,
        enter_main,
        leave_main,
        reach_main,
        early,
    ) = call(
        local_kernel,
        [held] * 14,
        [held] * 8 + [outside],
        [
            struct(tiles, HEAD_ROWS, LANES),
            struct(tiles, 384, LANES),
            struct(tiles, HEAD_ROWS, LANES),
            struct(tiles, HEAD_ROWS, LANES),
            struct(tiles, HEAD_ROWS, LANES),
            struct(tiles, MODES, SEG, LANES),
            struct(tiles, MODES, LANES),
            struct(tiles, MODES, SEG, LANES),
            hbm(tiles, T + MAIN_ROWS, LANES),
        ],
        [pltpu.VMEM((T, group * LANES), F32)] * 2
        + [pltpu.VMEM((group, T, LANES), F32)] * 2
        + [pltpu.VMEM((tiles, T + MAIN_ROWS, LANES), F32), pltpu.SemaphoreType.DMA((tiles,))],
        words * 8000,
        words * 60,
        "local",
    )(
        *turned_fields,
        taps_t,
        short_t,
        second_t,
        rate_t,
        amplitude,
        skip,
        forward,
        spectrum,
        inverse,
    )

    late_rows = HEAD_ROWS + 2 * MODES * SEG
    state, late = call(
        join_kernel,
        [held] * 19,
        [held, outside],
        [struct(tiles, MODES, LANES), hbm(tiles, late_rows, LANES)],
        [
            pltpu.VMEM((HEAD_ROWS + 8, join_group * LANES), F32),
            pltpu.VMEM((tiles, late_rows, LANES), F32),
            pltpu.SemaphoreType.DMA((tiles,)),
        ],
        words * 2000,
        words * 20,
        "join",
    )(
        halo,
        border,
        tap_spectrum,
        medium,
        taps,
        query,
        key2,
        turned_fields[0],
        turned_fields[1],
        enter_main,
        leave_main,
        reach_main,
        short_t,
        second_t,
        rate_t,
        amplitude,
        skip,
        halo_forward,
        halo_inverse,
    )

    scanned = call(
        scan_kernel,
        [held] * 2,
        held,
        struct(count, LANES),
        [],
        count * LANES * 30,
        count * LANES * 8,
        "scan",
    )(exchange(state.reshape(count, LANES)), own_rate)
    incoming = exchange(scanned).reshape(tiles, MODES, LANES)

    mixed, squares = call(
        finish_kernel,
        [held, outside, outside] + [held] * 4,
        [held] * 2,
        [struct(tiles, T, LANES), struct(1, T)],
        [
            pltpu.VMEM((tiles, T + MAIN_ROWS, LANES), F32),
            pltpu.VMEM((tiles, late_rows, LANES), F32),
            pltpu.VMEM((tiles, 2 * MODES, SEG, LANES), F32),
            pltpu.VMEM((T, LANES), F32),
            pltpu.SemaphoreType.DMA((2, chunks)),
        ],
        words * 40,
        words * 16,
        "finish",
    )(incoming, in_hbm(early), in_hbm(late), border, second_t, rate_t, gain)
    total = lax.psum(squares, "chan")
    return call(
        functools.partial(scale_kernel, float(channels * lax.axis_size("chan"))),
        [held, held],
        outside,
        struct(channels, T),
        [pltpu.VMEM((channels, T), F32), pltpu.SemaphoreType.DMA((chunks,))],
        words,
        words * 8,
        "scale",
    )(mixed, total)


def solution(mesh):
    return jax.shard_map(
        local,
        mesh=mesh,
        in_specs=(
            P("chan", "seq"),
            P("chan", "seq"),
            P("chan", "seq"),
            P("chan", "seq"),
            P("chan", "seq"),
            P(None, "chan", None),
            P(None, "chan", None),
            P("chan", None),
            P("chan", None),
            P("chan", None),
            P("chan"),
            P("chan"),
        ),
        out_specs=P("chan", "seq"),
        check_vma=False,
    )
```

```python
import functools

import jax
import jax.numpy as jnp
import ml_dtypes
import numpy as np
from jax import lax
from jax.experimental import pallas as pl
from jax.experimental.pallas import tpu as pltpu
from jax.sharding import PartitionSpec as P

norm_eps = 1e-06

T = 256
TAPS = 128
MODES = 8
LANES = 128
SEG = 8
HEAD = 17
MAIN = 15
HEAD_ROWS = HEAD * SEG
MAIN_ROWS = MAIN * SEG
RIMS = 16
RING = 8
LIMIT = 24 * 1024 * 1024

F32 = jnp.float32
BF16 = jnp.bfloat16


def row_times():
    head = [HEAD * i + k for k in range(HEAD) for i in range(SEG)]
    main = [HEAD_ROWS + MAIN * i + k for k in range(MAIN) for i in range(SEG)]
    return np.array(head + main)


def packed_forward(slots):
    k = np.arange(128)[:, None]
    angle = 2.0 * np.pi * k * np.asarray(slots)[None, :] / 256.0
    imag = -np.sin(angle)
    imag[0] = np.cos(np.pi * np.asarray(slots))
    return np.concatenate([np.cos(angle), imag], 0)


def packed_inverse(slots):
    k = np.arange(128)[None, :]
    angle = 2.0 * np.pi * k * np.asarray(slots)[:, None] / 256.0
    real = 2.0 * np.cos(angle)
    real[:, 0] = 1.0
    imag = -2.0 * np.sin(angle)
    imag[:, 0] = np.cos(np.pi * np.asarray(slots))
    return np.concatenate([real, imag], 1) / 256.0


def three_pass(matrix):
    high = matrix.astype(ml_dtypes.bfloat16)
    low = (matrix - high.astype(np.float64)).astype(ml_dtypes.bfloat16)
    return np.concatenate([high, low, high], 1)


def tables():
    times = row_times()
    first = packed_forward(times + 128) * (times < 128)[None, :]
    second = packed_forward(times)
    forward = np.concatenate([first, second], 0)
    taps = packed_forward(np.arange(TAPS))
    real, imag = taps[:128], taps[128:].copy()
    cross = real.copy()
    cross[0] = imag[0]
    imag[0] = 0.0
    spectrum = np.concatenate([real, imag, cross], 0)
    inverse = np.concatenate(
        [
            packed_inverse(times + 128) * (times < 128)[:, None],
            packed_inverse(times) * (times >= 128)[:, None],
        ],
        1,
    )
    halo = packed_forward(np.arange(128))
    halo[:, :2] = 0.0
    head_times = np.concatenate([times[:HEAD_ROWS], [-2, -1], np.full(6, 255)])
    halo_back = packed_inverse(head_times + 128) * (head_times < 128)[:, None]
    return [three_pass(m) for m in (forward, spectrum, inverse, halo, halo_back)]


def halves(x):
    high = x.astype(BF16)
    low = (x - high.astype(F32)).astype(BF16)
    return high, low


def matmul3(matrix, x):
    high, low = halves(x)
    stacked = jnp.concatenate([high, high, low], 0)
    return jnp.dot(matrix, stacked, preferred_element_type=F32)


def spectral_product(x, taps):
    real, imag = x[:128], x[128:]
    tap_real, tap_imag, tap_cross = taps[:128], taps[128:256], taps[256:]
    return jnp.concatenate(
        [real * tap_real - imag * tap_imag, real * tap_imag + imag * tap_cross], 0
    )


def sublane(shape):
    return lax.broadcasted_iota(jnp.int32, shape, 0)


def down(x, distance=1):
    return pltpu.roll(x, distance, axis=0)


def fir3(slabs, taps):
    return [
        taps[0] * slabs[k + 2] + taps[1] * slabs[k + 1] + taps[2] * slabs[k]
        for k in range(len(slabs) - 2)
    ]


def with_rims(head, main, rims=None):
    top = sublane(head[0].shape) == 0
    zero = jnp.zeros_like(head[0])
    before = (zero, zero) if rims is None else rims
    ends = [down(head[HEAD - 2]), down(head[HEAD - 1])]
    head_all = [jnp.where(top, before[k], ends[k]) for k in range(2)] + head
    if main is None:
        return head_all, None
    main_all = [jnp.where(top, ends[k], down(main[MAIN - 2 + k])) for k in range(2)] + main
    return head_all, main_all


def rows_of(ref, k, lanes):
    return ref[pl.ds(SEG * k, SEG), lanes]


def spread(row):
    return jnp.broadcast_to(row, (SEG, row.shape[1]))


def recurrence(inputs, decays, gains, skip):
    states = [gains[r] * inputs[0] for r in range(MODES)]
    outs = []
    for k, value in enumerate(inputs):
        if k:
            states = [decays[r] * states[r] + gains[r] * value for r in range(MODES)]
        total = skip * value
        for state in states:
            total = total + state
        outs.append(total)
    return outs, states


def segment_powers(rates, step):
    return [jnp.exp(-(step * distance) * rates) for distance in (1, 2, 4)]


def prefix(state, powers, mode):
    place = sublane(state.shape)
    total = state
    for power, distance in zip(powers, (1, 2, 4)):
        moved = jnp.where(place >= distance, down(total, distance), 0.0)
        total = total + spread(power[mode : mode + 1]) * moved
    return jnp.where(place >= 1, down(total), 0.0), total[SEG - 1 :]


def turned(block):
    return block.T


def tail_kernel(
    place_ref,
    key_hbm,
    value_hbm,
    short_hbm,
    rate_hbm,
    tail_ref,
    own_rate_out,
    key_in,
    value_in,
    short_ref,
    rates_in,
    key_sem,
    value_sem,
    short_sem,
    rate_sem,
):
    chunks = key_sem.shape[0]
    rows = key_hbm.shape[0] // chunks
    copies = []
    filters = pltpu.make_async_copy(short_hbm, short_ref, short_sem)
    filters.start()
    index = place_ref[0]
    share = rates_in.shape[0]
    first = lax.rem(index, RING) * (share * LANES)
    rates = []
    for part in range(share):
        mine = pl.ds(pl.multiple_of(first + part * LANES, LANES), LANES)
        copy = pltpu.make_async_copy(rate_hbm.at[:, mine], rates_in.at[part], rate_sem.at[part])
        copy.start()
        rates.append(copy)
    for chunk in range(chunks):
        here = pl.ds(chunk * rows, rows)
        for source, target, sem in (
            (key_hbm, key_in, key_sem),
            (value_hbm, value_in, value_sem),
        ):
            copy = pltpu.make_async_copy(
                source.at[here, pl.ds(LANES, LANES)], target.at[here, :], sem.at[chunk]
            )
            copy.start()
            copies.append(copy)
    filters.wait()
    for chunk in range(chunks):
        copies[2 * chunk].wait()
        copies[2 * chunk + 1].wait()
        for tile in range(chunk * rows // LANES, (chunk + 1) * rows // LANES):
            lanes = pl.ds(tile * LANES, LANES)

            def feature(ref, index):
                here = turned(ref[lanes, :])
                taps = [short_ref[index, j : j + 1, lanes] for j in range(3)]
                return taps[0] * here + taps[1] * down(here) + taps[2] * down(here, 2)

            tail_ref[tile] = feature(key_in, 1) * feature(value_in, 2)
    for copy in rates:
        copy.wait()
    own_rate_out[...] = rates_in[...]


def prep_kernel(
    key_hbm,
    value_hbm,
    query_hbm,
    query2_hbm,
    key2_hbm,
    medium_hbm,
    short_ref,
    key_t,
    value_t,
    query_t,
    query2_t,
    key2_t,
    taps_t,
    rims_out,
    key_in,
    value_in,
    query_in,
    query2_in,
    key2_in,
    medium_in,
    sems,
):
    chunks = sems.shape[1]
    rows = key_hbm.shape[0] // chunks
    fields = (
        (key_hbm, key_in, key_t),
        (value_hbm, value_in, value_t),
        (query_hbm, query_in, query_t),
        (query2_hbm, query2_in, query2_t),
        (key2_hbm, key2_in, key2_t),
        (medium_hbm, medium_in, taps_t),
    )
    copies = []
    for chunk in range(chunks):
        here = pl.ds(chunk * rows, rows)
        for place, (source, target, _) in enumerate(fields):
            copy = pltpu.make_async_copy(
                source.at[here, :], target.at[here, :], sems.at[place, chunk]
            )
            copy.start()
            copies.append(copy)
    for chunk in range(chunks):
        for place in range(len(fields)):
            copies[chunk * len(fields) + place].wait()
        for tile in range(chunk * rows // LANES, (chunk + 1) * rows // LANES):
            lanes = pl.ds(tile * LANES, LANES)
            rims_out[tile] = jnp.zeros((RIMS, LANES), F32)
            for place, (_, source, target) in enumerate(fields):
                if place < 5:
                    target[tile] = turned(source[lanes, :])
                    rims_out[tile, 2 * place : 2 * place + 2, :] = target[tile, T - 2 : T, :]
                else:
                    target[tile, 0:TAPS, :] = turned(source[lanes, :])
                    target[tile, TAPS:HEAD_ROWS, :] = jnp.zeros((HEAD_ROWS - TAPS, LANES), F32)

            def feature(ref, index, time):
                return sum(
                    short_ref[index, j : j + 1, lanes] * ref[tile, time - j : time - j + 1, :]
                    for j in range(3)
                )

            for k in range(2):
                rims_out[tile, 10 + k : 11 + k, :] = feature(query_t, 0, T - 2 + k)
            for k in range(3):
                rims_out[tile, 12 + k : 13 + k, :] = feature(key_t, 1, T // 2 - 1 + k) * feature(
                    value_t, 2, T // 2 - 1 + k
                )


def local_kernel(
    key_t,
    value_t,
    query_t,
    query2_t,
    key2_t,
    taps_t,
    short_ref,
    second_ref,
    rate_ref,
    amplitude_ref,
    skip_ref,
    forward_ref,
    spectrum_ref,
    inverse_ref,
    taps_out,
    spectrum_out,
    medium_out,
    query_out,
    key2_out,
    enter_out,
    leave_out,
    reach_main_out,
    late_hbm,
    gated_t,
    medium_t,
    query_all,
    key2_all,
    late,
    late_sem,
):

    tiles = key_t.shape[0]
    group = gated_t.shape[1] // LANES
    top = sublane((SEG, LANES)) == 0
    segment = sublane((SEG, LANES)).astype(F32)

    def slabs_of(ref, tile):
        head = [ref[tile, pl.ds(k, SEG, stride=HEAD), :] for k in range(HEAD)]
        main = [ref[tile, pl.ds(HEAD_ROWS + k, SEG, stride=MAIN), :] for k in range(MAIN)]
        return head, main

    def feature(ref, tile, taps_of, index, lanes):
        taps = [spread(taps_of[index, j : j + 1, lanes]) for j in range(3)]
        head, main = with_rims(*slabs_of(ref, tile))
        return fir3(head, taps) + fir3(main, taps)

    def body(step, _):
        for part in range(group):
            tile = step * group + part
            lanes = pl.ds(pl.multiple_of(tile * LANES, LANES), LANES)
            local = pl.ds(part * LANES, LANES)
            keys = feature(key_t, tile, short_ref, 1, lanes)
            values = feature(value_t, tile, short_ref, 2, lanes)
            for k in range(HEAD + MAIN):
                gated = keys[k] * values[k]
                if k < 2:
                    gated = jnp.where(top, 0.0, gated)
                gated_t[pl.ds(SEG * k, SEG), local] = gated
            for k, slab in enumerate(feature(query_t, tile, short_ref, 0, lanes)):
                query_all[part, pl.ds(SEG * k, SEG), :] = slab
            query_out[tile] = query_all[part, 0:HEAD_ROWS, :]
            for k, slab in enumerate(feature(key2_t, tile, second_ref, 1, lanes)):
                key2_all[part, pl.ds(SEG * k, SEG), :] = slab
            key2_out[tile] = key2_all[part, 0:HEAD_ROWS, :]
            for k, slab in enumerate(feature(query2_t, tile, second_ref, 0, lanes)):
                late[tile, pl.ds(SEG * k, SEG), :] = slab
            for k in range(HEAD):
                taps_out[tile, pl.ds(SEG * k, SEG), :] = taps_t[
                    tile, pl.ds(k, SEG, stride=HEAD), :
                ]

        filters = [taps_t[step * group + part, 0:TAPS, :] for part in range(group)]
        spectrum = matmul3(spectrum_ref[...], jnp.concatenate(filters, 1))
        both = matmul3(forward_ref[...], gated_t[...])
        first = spectral_product(both[:T], spectrum)
        second = spectral_product(both[T:], spectrum)
        medium_t[...] = matmul3(inverse_ref[...], jnp.concatenate([first, second], 0))

        for part in range(group):
            tile = step * group + part
            lanes = pl.ds(pl.multiple_of(tile * LANES, LANES), LANES)
            local = pl.ds(part * LANES, LANES)
            spectrum_out[tile] = spectrum[:, part * LANES : (part + 1) * LANES]
            medium_out[tile] = medium_t[0:HEAD_ROWS, local]
            taps = [spread(second_ref[2, j : j + 1, lanes]) for j in range(3)]
            firsts = [
                rows_of(medium_t, k, local) * query_all[part, pl.ds(SEG * k, SEG), :]
                for k in range(HEAD - 2, HEAD + MAIN)
            ]
            ends = [down(firsts[0]), down(firsts[1])]
            main = firsts[2:]
            main_all = [jnp.where(top, ends[k], down(main[MAIN - 2 + k])) for k in range(2)] + main
            values2 = fir3(main_all, taps)
            inputs = [
                key2_all[part, pl.ds(SEG * (HEAD + k), SEG), :] * values2[k] for k in range(MAIN)
            ]
            rates, gains = rate_ref[:, lanes], amplitude_ref[:, lanes]
            decays = jnp.exp(-rates)
            outs, ends = recurrence(
                inputs,
                [spread(decays[r : r + 1]) for r in range(MODES)],
                [spread(gains[r : r + 1]) for r in range(MODES)],
                spread(skip_ref[:, lanes]),
            )
            for k in range(MAIN):
                late[tile, pl.ds(T + SEG * k, SEG), :] = outs[k]
            pltpu.make_async_copy(late.at[tile], late_hbm.at[tile], late_sem.at[tile]).start()
            powers = segment_powers(rates, float(MAIN))
            for r in range(MODES):
                enter, leave = prefix(ends[r], powers, r)
                enter_out[tile, r] = enter
                leave_out[tile, r : r + 1, :] = leave
                rate = spread(rates[r : r + 1])
                reach_main_out[tile, r] = jnp.exp(-(rate * (segment * float(MAIN))))
        return _

    lax.fori_loop(0, tiles // group, body, 0)
    for tile in range(tiles):
        pltpu.make_async_copy(late.at[tile], late_hbm.at[tile], late_sem.at[tile]).wait()


def join_kernel(
    halo_ref,
    rims_ref,
    spectrum_ref,
    medium_ref,
    taps_ref,
    query_ref,
    key2_ref,
    key_t,
    value_t,
    enter_main_ref,
    leave_main_ref,
    reach_main_ref,
    short_ref,
    second_ref,
    rate_ref,
    amplitude_ref,
    skip_ref,
    forward_ref,
    inverse_ref,
    state_out,
    late_hbm,
    medium_t,
    late,
    late_sem,
):
    tiles = halo_ref.shape[0]
    group = medium_t.shape[1] // LANES
    top = sublane((SEG, LANES)) == 0

    def body(step, _):
        tile_list = [step * group + part for part in range(group)]
        halo = matmul3(
            forward_ref[...], jnp.concatenate([halo_ref[tile] for tile in tile_list], 1)
        )
        filters = jnp.concatenate([spectrum_ref[tile] for tile in tile_list], 1)
        medium_t[...] = matmul3(inverse_ref[...], spectral_product(halo, filters))
        for part, tile in enumerate(tile_list):
            one(tile, pl.ds(part * LANES, LANES))
        return _

    def one(tile, local):
        lanes = pl.ds(pl.multiple_of(tile * LANES, LANES), LANES)

        def rim(k):
            return rims_ref[tile, k : k + 1, :]

        def taps_of(ref, index):
            return [ref[index, j : j + 1, lanes] for j in range(3)]

        def early(ref, place, index):
            taps = taps_of(short_ref, index)
            zero, one = ref[tile, 0:1, :], ref[tile, 1:2, :]
            older, last = rim(2 * place), rim(2 * place + 1)
            return (
                taps[0] * zero + taps[1] * last + taps[2] * older,
                taps[0] * one + taps[1] * zero + taps[2] * last,
            )

        def mended(ref, place, taps):
            slabs = [ref[tile, pl.ds(SEG * k, SEG), :] for k in range(HEAD)]
            older, last = rim(2 * place), rim(2 * place + 1)
            slabs[0] = slabs[0] + jnp.where(top, spread(taps[1] * last + taps[2] * older), 0.0)
            slabs[1] = slabs[1] + jnp.where(top, spread(taps[2] * last), 0.0)
            return slabs

        def tap(j):
            row = SEG * (j % HEAD) + j // HEAD
            return taps_ref[tile, row : row + 1, :]

        keys, values = early(key_t, 0, 1), early(value_t, 1, 2)
        gated = [spread(keys[k] * values[k]) for k in range(2)]
        taps = [taps_ref[tile, pl.ds(SEG * k, SEG), :] for k in range(HEAD)]
        shifted = [jnp.where(top, 0.0, down(taps[HEAD - 1]))] + taps
        query = mended(query_ref, 2, taps_of(short_ref, 0))
        key2 = mended(key2_ref, 4, taps_of(second_ref, 1))
        mediums = [
            medium_ref[tile, pl.ds(SEG * k, SEG), :]
            + rows_of(medium_t, k, local)
            + taps[k] * gated[0]
            + shifted[k] * gated[1]
            for k in range(HEAD)
        ]
        far, farther, farthest = rim(14), rim(13), rim(12)
        mediums[0] = mediums[0] + jnp.where(top, spread(tap(127) * far), 0.0)
        older = medium_t[HEAD_ROWS : HEAD_ROWS + 1, local] + (
            tap(125) * far + tap(126) * farther + tap(127) * farthest
        )
        last = medium_t[HEAD_ROWS + 1 : HEAD_ROWS + 2, local] + (
            tap(126) * far + tap(127) * farther
        )
        firsts = [query[k] * mediums[k] for k in range(HEAD)]
        firsts_all, _ = with_rims(firsts, None, (spread(rim(10) * older), spread(rim(11) * last)))
        values2 = fir3(firsts_all, [spread(t) for t in taps_of(second_ref, 2)])
        inputs = [key2[k] * values2[k] for k in range(HEAD)]
        rates, gains = rate_ref[:, lanes], amplitude_ref[:, lanes]
        decays = jnp.exp(-rates)
        outs, ends = recurrence(
            inputs,
            [spread(decays[r : r + 1]) for r in range(MODES)],
            [spread(gains[r : r + 1]) for r in range(MODES)],
            spread(skip_ref[:, lanes]),
        )
        for k in range(HEAD):
            late[tile, pl.ds(SEG * k, SEG), :] = outs[k]
        powers = segment_powers(rates, float(HEAD))
        whole = jnp.exp(-float(MAIN_ROWS) * rates)
        for r in range(MODES):
            enter, leave = prefix(ends[r], powers, r)
            late[tile, pl.ds(HEAD_ROWS + SEG * r, SEG), :] = enter
            late[tile, pl.ds(HEAD_ROWS + SEG * (MODES + r), SEG), :] = enter_main_ref[
                tile, r
            ] + reach_main_ref[tile, r] * spread(leave)
            state_out[tile, r : r + 1, :] = (
                leave_main_ref[tile, r : r + 1, :] + leave * whole[r : r + 1]
            )
        pltpu.make_async_copy(late.at[tile], late_hbm.at[tile], late_sem.at[tile]).start()

    lax.fori_loop(0, tiles // group, body, 0, unroll=True)
    for tile in range(tiles):
        pltpu.make_async_copy(late.at[tile], late_hbm.at[tile], late_sem.at[tile]).wait()


def ring_kernel(states_hbm, rate_ref, out_ref, states, sem):
    copy = pltpu.make_async_copy(states_hbm, states, sem)
    copy.start()
    decay = jnp.exp(-float(T) * rate_ref[...])
    copy.wait()
    total = states[0]
    for k in range(1, states.shape[0]):
        total = decay * total + states[k]
    for k in range(out_ref.shape[0]):
        out_ref[k] = total


def scan_kernel(place_ref, states_hbm, rings_ref, rate_ref, out_ref, states, sem):
    copy = pltpu.make_async_copy(states_hbm, states, sem)
    copy.start()
    ring = place_ref[0] // RING
    rates = rate_ref[...]
    decay = jnp.exp(-float(T) * rates)
    around = jnp.exp(-float(T * RING) * rates)
    entering = jnp.zeros_like(rates)
    for k in range(rings_ref.shape[0] - 1):
        entering = jnp.where(k < ring, around * entering + rings_ref[k], entering)
    copy.wait()
    for k in range(states.shape[0]):
        out_ref[k] = entering
        entering = decay * entering + states[k]


def finish_kernel(
    state_ref,
    early_hbm,
    late_hbm,
    rims_ref,
    second_ref,
    rate_ref,
    gain_ref,
    mixed_out,
    squares_out,
    early,
    late,
    reach,
    squares_t,
    sems,
):
    tiles = early_hbm.shape[0]
    chunks = sems.shape[1]
    count = tiles // chunks
    copies = []
    for chunk in range(chunks):
        here = pl.ds(chunk * count, count)
        for place, (source, target) in enumerate(((early_hbm, early), (late_hbm, late))):
            copy = pltpu.make_async_copy(source.at[here], target.at[here], sems.at[place, chunk])
            copy.start()
            copies.append(copy)
    squares_t[...] = jnp.zeros_like(squares_t)
    top = sublane((SEG, LANES)) == 0
    segment = sublane((SEG, LANES)).astype(F32)

    def reaches(tile, _):
        lanes = pl.ds(pl.multiple_of(tile * LANES, LANES), LANES)
        for r in range(MODES):
            rate = spread(rate_ref[r : r + 1, lanes])
            reach[tile, r] = jnp.exp(-(rate * (segment * float(HEAD))))
            reach[tile, MODES + r] = jnp.exp(-(rate * (segment * float(MAIN) + float(HEAD_ROWS))))
        return _

    lax.fori_loop(0, tiles, reaches, 0)

    def body(tile, _):
        lanes = pl.ds(pl.multiple_of(tile * LANES, LANES), LANES)
        decays = jnp.exp(-rate_ref[:, lanes])
        taps = [second_ref[0, j : j + 1, lanes] for j in range(3)]
        older, last = rims_ref[tile, 6:7, :], rims_ref[tile, 7:8, :]
        mends = [spread(taps[1] * last + taps[2] * older), spread(taps[2] * last)]
        gain = spread(gain_ref[:, lanes])
        states = state_ref[tile]
        decay = [spread(decays[r : r + 1]) for r in range(MODES)]

        def half(length, half_index, own_ref, own_row, first_row):
            enter_row = HEAD_ROWS + half_index * MODES * SEG
            carry = [
                late[tile, pl.ds(enter_row + SEG * r, SEG), :]
                + reach[tile, half_index * MODES + r] * spread(states[r : r + 1])
                for r in range(MODES)
            ]
            for k in range(length):
                carry = [decay[r] * carry[r] for r in range(MODES)]
                total = own_ref[tile, pl.ds(own_row + SEG * k, SEG), :]
                for value in carry:
                    total = total + value
                rows = pl.ds(first_row + SEG * k, SEG)
                query = early[tile, rows, :]
                if first_row == 0 and k < 2:
                    query = query + jnp.where(top, mends[k], 0.0)
                mixed = query * total
                squares_t[rows, :] = squares_t[rows, :] + mixed * mixed
                mixed_out[tile, pl.ds(first_row + k, SEG, stride=length), :] = mixed * gain

        half(HEAD, 0, late, 0, 0)
        half(MAIN, 1, early, T, HEAD_ROWS)
        return _

    for chunk in range(chunks):
        copies[2 * chunk].wait()
        copies[2 * chunk + 1].wait()
        lax.fori_loop(chunk * count, (chunk + 1) * count, body, 0)
    sums = jnp.sum(squares_t[...], axis=1, keepdims=True)
    squares_t[...] = jnp.broadcast_to(sums, squares_t.shape)
    head = [squares_t[pl.ds(i, HEAD, stride=SEG), :] for i in range(SEG)]
    main = [squares_t[pl.ds(HEAD_ROWS + i, MAIN, stride=SEG), :] for i in range(SEG)]
    ordered = jnp.concatenate(head + main, 0)
    squares_out[...] = ordered.T[0:1, :]


def scale_kernel(divisor, mixed_ref, squares_ref, out_hbm, out_t, sems):
    scale = lax.rsqrt(squares_ref[...] / divisor + norm_eps)
    chunks = sems.shape[0]
    tiles = mixed_ref.shape[0] // chunks
    copies = []
    for chunk in range(chunks):
        for tile in range(chunk * tiles, (chunk + 1) * tiles):
            out_t[pl.ds(tile * LANES, LANES), :] = mixed_ref[tile].T * scale
        rows = pl.ds(chunk * tiles * LANES, tiles * LANES)
        copy = pltpu.make_async_copy(out_t.at[rows, :], out_hbm.at[rows, :], sems.at[chunk])
        copy.start()
        copies.append(copy)
    for copy in copies:
        copy.wait()


def from_behind(block):
    count = lax.axis_size("seq")
    return lax.ppermute(block, "seq", [(i, i + 1) for i in range(count - 1)])


def in_hbm(x):
    return pltpu.with_memory_space_constraint(x, pltpu.HBM)


def call(kernel, in_specs, out_specs, out_shape, scratch, flops, size, name):
    return pl.pallas_call(
        kernel,
        in_specs=in_specs,
        out_specs=out_specs,
        out_shape=out_shape,
        scratch_shapes=scratch,
        compiler_params=pltpu.CompilerParams(vmem_limit_bytes=LIMIT),
        cost_estimate=pl.CostEstimate(flops=flops, bytes_accessed=size, transcendentals=0),
        name=name,
    )


def exchange(rows, groups):
    return lax.all_to_all(
        rows, "seq", split_axis=0, concat_axis=0, axis_index_groups=groups, tiled=True
    )


def local(
    query_proj,
    key_proj,
    value_proj,
    second_query,
    second_key,
    short_filter,
    second_short,
    medium_filter,
    decay_rate,
    residue,
    skip_gain,
    norm_gain,
):
    channels = query_proj.shape[0]
    count = lax.axis_size("seq")
    tiles = channels // LANES
    group = min(4, tiles)
    join_group = min(2, tiles)
    chunks = min(4, tiles)
    short_t = jnp.transpose(short_filter, (0, 2, 1))
    second_t = jnp.transpose(second_short, (0, 2, 1))
    rate_t = decay_rate.T
    amplitude = residue.T * jnp.sqrt(-jnp.expm1(-2.0 * rate_t))
    skip = skip_gain[None, :]
    gain = norm_gain[None, :]
    forward, spectrum, inverse, halo_forward, halo_inverse = tables()
    held = pl.BlockSpec(memory_space=pltpu.VMEM)
    outside = pl.BlockSpec(memory_space=pl.ANY)
    words = channels * T

    def struct(*shape):
        return jax.ShapeDtypeStruct(shape, F32)

    def hbm(*shape):
        return pltpu.HBM(shape, F32)

    fields = [
        in_hbm(x) for x in (key_proj, value_proj, query_proj, second_query, second_key, medium_filter)
    ]
    rings = count // RING
    share = tiles // RING
    ring_groups = [[ring * RING + k for k in range(RING)] for ring in range(rings)]
    across_groups = [[ring * RING + k for ring in range(rings)] for k in range(RING)]
    place = lax.axis_index("seq").astype(jnp.int32).reshape(1)
    tail, own_rate = call(
        tail_kernel,
        [pl.BlockSpec(memory_space=pltpu.SMEM)] + [outside] * 4,
        [held] * 2,
        [struct(tiles, TAPS, LANES), struct(share, MODES, LANES)],
        [pltpu.VMEM((channels, LANES), F32)] * 2
        + [pltpu.VMEM((3, 3, channels), F32), pltpu.VMEM((share, MODES, LANES), F32)]
        + [pltpu.SemaphoreType.DMA((chunks,))] * 2
        + [pltpu.SemaphoreType.DMA, pltpu.SemaphoreType.DMA((share,))],
        words * 8,
        words * 6,
        "tail",
    )(place, fields[0], fields[1], in_hbm(short_t), in_hbm(rate_t))
    halo = from_behind(tail)

    *turned_fields, taps_t, rims = call(
        prep_kernel,
        [outside] * 6 + [held],
        [held] * 7,
        [struct(tiles, T, LANES)] * 5
        + [struct(tiles, HEAD_ROWS, LANES), struct(tiles, RIMS, LANES)],
        [pltpu.VMEM((channels, T), F32)] * 5
        + [pltpu.VMEM((channels, TAPS), F32), pltpu.SemaphoreType.DMA((6, chunks))],
        words * 20,
        words * 40,
        "prep",
    )(*fields, short_t)
    border = from_behind(rims)

    (
        taps,
        tap_spectrum,
        medium,
        query,
        key2,
        enter_main,
        leave_main,
        reach_main,
        early,
    ) = call(
        local_kernel,
        [held] * 14,
        [held] * 8 + [outside],
        [
            struct(tiles, HEAD_ROWS, LANES),
            struct(tiles, 384, LANES),
            struct(tiles, HEAD_ROWS, LANES),
            struct(tiles, HEAD_ROWS, LANES),
            struct(tiles, HEAD_ROWS, LANES),
            struct(tiles, MODES, SEG, LANES),
            struct(tiles, MODES, LANES),
            struct(tiles, MODES, SEG, LANES),
            hbm(tiles, T + MAIN_ROWS, LANES),
        ],
        [pltpu.VMEM((T, group * LANES), F32)] * 2
        + [pltpu.VMEM((group, T, LANES), F32)] * 2
        + [pltpu.VMEM((tiles, T + MAIN_ROWS, LANES), F32), pltpu.SemaphoreType.DMA((tiles,))],
        words * 8000,
        words * 60,
        "local",
    )(
        *turned_fields,
        taps_t,
        short_t,
        second_t,
        rate_t,
        amplitude,
        skip,
        forward,
        spectrum,
        inverse,
    )

    late_rows = HEAD_ROWS + 2 * MODES * SEG
    state, late = call(
        join_kernel,
        [held] * 19,
        [held, outside],
        [struct(tiles, MODES, LANES), hbm(tiles, late_rows, LANES)],
        [
            pltpu.VMEM((HEAD_ROWS + 8, join_group * LANES), F32),
            pltpu.VMEM((tiles, late_rows, LANES), F32),
            pltpu.SemaphoreType.DMA((tiles,)),
        ],
        words * 2000,
        words * 20,
        "join",
    )(
        halo,
        border,
        tap_spectrum,
        medium,
        taps,
        query,
        key2,
        turned_fields[0],
        turned_fields[1],
        enter_main,
        leave_main,
        reach_main,
        short_t,
        second_t,
        rate_t,
        amplitude,
        skip,
        halo_forward,
        halo_inverse,
    )

    share_shape = (RING, share, MODES, LANES)
    ring_states = in_hbm(exchange(state.reshape(share_shape), ring_groups))
    totals = call(
        ring_kernel,
        [outside, held],
        held,
        struct(rings, share, MODES, LANES),
        [pltpu.VMEM(share_shape, F32), pltpu.SemaphoreType.DMA],
        count * LANES * 30,
        count * LANES * 8,
        "ring",
    )(ring_states, own_rate)
    scanned = call(
        scan_kernel,
        [pl.BlockSpec(memory_space=pltpu.SMEM), outside, held, held],
        held,
        struct(*share_shape),
        [pltpu.VMEM(share_shape, F32), pltpu.SemaphoreType.DMA],
        count * LANES * 30,
        count * LANES * 8,
        "scan",
    )(place, ring_states, exchange(totals, across_groups), own_rate)
    incoming = exchange(scanned, ring_groups).reshape(tiles, MODES, LANES)

    mixed, squares = call(
        finish_kernel,
        [held, outside, outside] + [held] * 4,
        [held] * 2,
        [struct(tiles, T, LANES), struct(1, T)],
        [
            pltpu.VMEM((tiles, T + MAIN_ROWS, LANES), F32),
            pltpu.VMEM((tiles, late_rows, LANES), F32),
            pltpu.VMEM((tiles, 2 * MODES, SEG, LANES), F32),
            pltpu.VMEM((T, LANES), F32),
            pltpu.SemaphoreType.DMA((2, chunks)),
        ],
        words * 40,
        words * 16,
        "finish",
    )(incoming, in_hbm(early), in_hbm(late), border, second_t, rate_t, gain)
    total = lax.psum(squares, "chan")
    return call(
        functools.partial(scale_kernel, float(channels * lax.axis_size("chan"))),
        [held, held],
        outside,
        struct(channels, T),
        [pltpu.VMEM((channels, T), F32), pltpu.SemaphoreType.DMA((chunks,))],
        words,
        words * 8,
        "scale",
    )(mixed, total)


def solution(mesh):
    return jax.shard_map(
        local,
        mesh=mesh,
        in_specs=(
            P("chan", "seq"),
            P("chan", "seq"),
            P("chan", "seq"),
            P("chan", "seq"),
            P("chan", "seq"),
            P(None, "chan", None),
            P(None, "chan", None),
            P("chan", None),
            P("chan", None),
            P("chan", None),
            P("chan"),
            P("chan"),
        ),
        out_specs=P("chan", "seq"),
        check_vma=False,
    )
```

```python
import functools

import jax
import jax.numpy as jnp
import ml_dtypes
import numpy as np
from jax import lax
from jax.experimental import pallas as pl
from jax.experimental.pallas import tpu as pltpu
from jax.sharding import PartitionSpec as P

norm_eps = 1e-06

T = 256
TAPS = 128
MODES = 8
LANES = 128
SEG = 8
HEAD = 17
MAIN = 15
HEAD_ROWS = HEAD * SEG
MAIN_ROWS = MAIN * SEG
RIMS = 16
RING = 8
LIMIT = 24 * 1024 * 1024

F32 = jnp.float32
BF16 = jnp.bfloat16


def row_times():
    head = [HEAD * i + k for k in range(HEAD) for i in range(SEG)]
    main = [HEAD_ROWS + MAIN * i + k for k in range(MAIN) for i in range(SEG)]
    return np.array(head + main)


def packed_forward(slots):
    k = np.arange(128)[:, None]
    angle = 2.0 * np.pi * k * np.asarray(slots)[None, :] / 256.0
    imag = -np.sin(angle)
    imag[0] = np.cos(np.pi * np.asarray(slots))
    return np.concatenate([np.cos(angle), imag], 0)


def packed_inverse(slots):
    k = np.arange(128)[None, :]
    angle = 2.0 * np.pi * k * np.asarray(slots)[:, None] / 256.0
    real = 2.0 * np.cos(angle)
    real[:, 0] = 1.0
    imag = -2.0 * np.sin(angle)
    imag[:, 0] = np.cos(np.pi * np.asarray(slots))
    return np.concatenate([real, imag], 1) / 256.0


def three_pass(matrix):
    high = matrix.astype(ml_dtypes.bfloat16)
    low = (matrix - high.astype(np.float64)).astype(ml_dtypes.bfloat16)
    return np.concatenate([high, low, high], 1)


def tables():
    times = row_times()
    first = packed_forward(times + 128) * (times < 128)[None, :]
    second = packed_forward(times)
    forward = np.concatenate([first, second], 0)
    taps = packed_forward(np.arange(TAPS))
    real, imag = taps[:128], taps[128:].copy()
    cross = real.copy()
    cross[0] = imag[0]
    imag[0] = 0.0
    spectrum = np.concatenate([real, imag, cross], 0)
    inverse = np.concatenate(
        [
            packed_inverse(times + 128) * (times < 128)[:, None],
            packed_inverse(times) * (times >= 128)[:, None],
        ],
        1,
    )
    halo = packed_forward(np.arange(128))
    halo[:, :2] = 0.0
    head_times = np.concatenate([times[:HEAD_ROWS], [-2, -1], np.full(6, 255)])
    halo_back = packed_inverse(head_times + 128) * (head_times < 128)[:, None]
    return [three_pass(m) for m in (forward, spectrum, inverse, halo, halo_back)]


def halves(x):
    high = x.astype(BF16)
    low = (x - high.astype(F32)).astype(BF16)
    return high, low


def matmul3(matrix, x):
    high, low = halves(x)
    stacked = jnp.concatenate([high, high, low], 0)
    return jnp.dot(matrix, stacked, preferred_element_type=F32)


def spectral_product(x, taps):
    real, imag = x[:128], x[128:]
    tap_real, tap_imag, tap_cross = taps[:128], taps[128:256], taps[256:]
    return jnp.concatenate(
        [real * tap_real - imag * tap_imag, real * tap_imag + imag * tap_cross], 0
    )


def sublane(shape):
    return lax.broadcasted_iota(jnp.int32, shape, 0)


def down(x, distance=1):
    return pltpu.roll(x, distance, axis=0)


def fir3(slabs, taps):
    return [
        taps[0] * slabs[k + 2] + taps[1] * slabs[k + 1] + taps[2] * slabs[k]
        for k in range(len(slabs) - 2)
    ]


def with_rims(head, main, rims=None):
    top = sublane(head[0].shape) == 0
    zero = jnp.zeros_like(head[0])
    before = (zero, zero) if rims is None else rims
    ends = [down(head[HEAD - 2]), down(head[HEAD - 1])]
    head_all = [jnp.where(top, before[k], ends[k]) for k in range(2)] + head
    if main is None:
        return head_all, None
    main_all = [jnp.where(top, ends[k], down(main[MAIN - 2 + k])) for k in range(2)] + main
    return head_all, main_all


def rows_of(ref, k, lanes):
    return ref[pl.ds(SEG * k, SEG), lanes]


def spread(row):
    return jnp.broadcast_to(row, (SEG, row.shape[1]))


def recurrence(inputs, decays, gains, skip):
    states = [gains[r] * inputs[0] for r in range(MODES)]
    outs = []
    for k, value in enumerate(inputs):
        if k:
            states = [decays[r] * states[r] + gains[r] * value for r in range(MODES)]
        total = skip * value
        for state in states:
            total = total + state
        outs.append(total)
    return outs, states


def segment_powers(rates, step):
    return [jnp.exp(-(step * distance) * rates) for distance in (1, 2, 4)]


def prefix(state, powers, mode):
    place = sublane(state.shape)
    total = state
    for power, distance in zip(powers, (1, 2, 4)):
        moved = jnp.where(place >= distance, down(total, distance), 0.0)
        total = total + spread(power[mode : mode + 1]) * moved
    return jnp.where(place >= 1, down(total), 0.0), total[SEG - 1 :]


def turned(block):
    return block.T


def tail_kernel(
    place_ref,
    key_hbm,
    value_hbm,
    short_hbm,
    rate_hbm,
    tail_ref,
    own_rate_out,
    key_in,
    value_in,
    short_ref,
    rates_in,
    key_sem,
    value_sem,
    short_sem,
    rate_sem,
):
    chunks = key_sem.shape[0]
    rows = key_in.shape[0] // chunks
    copies = []
    filters = pltpu.make_async_copy(short_hbm, short_ref, short_sem)
    filters.start()
    index = place_ref[0]
    share = rates_in.shape[0]
    first = lax.rem(index, RING) * (share * LANES)
    rates = []
    for part in range(share):
        mine = pl.ds(pl.multiple_of(first + part * LANES, LANES), LANES)
        copy = pltpu.make_async_copy(rate_hbm.at[:, mine], rates_in.at[part], rate_sem.at[part])
        copy.start()
        rates.append(copy)
    for chunk in range(chunks):
        here = pl.ds(chunk * rows, rows)
        for source, target, sem in (
            (key_hbm, key_in, key_sem),
            (value_hbm, value_in, value_sem),
        ):
            copy = pltpu.make_async_copy(
                source.at[here, pl.ds(LANES, LANES)], target.at[here, :], sem.at[chunk]
            )
            copy.start()
            copies.append(copy)
    filters.wait()
    for chunk in range(chunks):
        copies[2 * chunk].wait()
        copies[2 * chunk + 1].wait()
        for tile in range(chunk * rows // LANES, (chunk + 1) * rows // LANES):
            lanes = pl.ds(tile * LANES, LANES)

            def feature(ref, index):
                here = turned(ref[lanes, :])
                taps = [short_ref[index, j : j + 1, lanes] for j in range(3)]
                return taps[0] * here + taps[1] * down(here) + taps[2] * down(here, 2)

            tail_ref[tile] = feature(key_in, 1) * feature(value_in, 2)
    for copy in rates:
        copy.wait()
    own_rate_out[...] = rates_in[...]


def prep_kernel(
    key_hbm,
    value_hbm,
    query_hbm,
    query2_hbm,
    key2_hbm,
    medium_hbm,
    short_ref,
    _,
    key_t,
    value_t,
    query_t,
    query2_t,
    key2_t,
    taps_t,
    rims_out,
    tail_out,
    key_in,
    value_in,
    query_in,
    query2_in,
    key2_in,
    medium_in,
    sems,
):
    chunks = sems.shape[1]
    rows = key_hbm.shape[0] // chunks
    fields = (
        (key_hbm, key_in, key_t),
        (value_hbm, value_in, value_t),
        (query_hbm, query_in, query_t),
        (query2_hbm, query2_in, query2_t),
        (key2_hbm, key2_in, key2_t),
        (medium_hbm, medium_in, taps_t),
    )
    copies = []
    for chunk in range(chunks):
        here = pl.ds(chunk * rows, rows)
        for place, (source, target, _) in enumerate(fields):
            copy = pltpu.make_async_copy(
                source.at[here, :], target.at[here, :], sems.at[place, chunk]
            )
            copy.start()
            copies.append(copy)
    for chunk in range(chunks):
        for place in range(len(fields)):
            copies[chunk * len(fields) + place].wait()
        for tile in range(chunk * rows // LANES, (chunk + 1) * rows // LANES):
            lanes = pl.ds(tile * LANES, LANES)
            rims_out[tile] = jnp.zeros((RIMS, LANES), F32)
            for place, (_, source, target) in enumerate(fields):
                if place < 5:
                    target[tile] = turned(source[lanes, :])
                    rims_out[tile, 2 * place : 2 * place + 2, :] = target[tile, T - 2 : T, :]
                else:
                    target[tile, 0:TAPS, :] = turned(source[lanes, :])
                    target[tile, TAPS:HEAD_ROWS, :] = jnp.zeros((HEAD_ROWS - TAPS, LANES), F32)

            def feature(ref, index, time):
                return sum(
                    short_ref[index, j : j + 1, lanes] * ref[tile, time - j : time - j + 1, :]
                    for j in range(3)
                )

            late = tile - (key_t.shape[0] - tail_out.shape[0])
            if late >= 0:
                gated = 1.0
                for ref, index in ((key_t, 1), (value_t, 2)):
                    here = ref[tile, T // 2 : T, :]
                    taps = [short_ref[index, j : j + 1, lanes] for j in range(3)]
                    gated = gated * (taps[0] * here + taps[1] * down(here) + taps[2] * down(here, 2))
                tail_out[late] = gated
            for k in range(2):
                rims_out[tile, 10 + k : 11 + k, :] = feature(query_t, 0, T - 2 + k)
            for k in range(3):
                rims_out[tile, 12 + k : 13 + k, :] = feature(key_t, 1, T // 2 - 1 + k) * feature(
                    value_t, 2, T // 2 - 1 + k
                )


def local_kernel(
    key_t,
    value_t,
    query_t,
    query2_t,
    key2_t,
    taps_t,
    short_ref,
    second_ref,
    rate_ref,
    amplitude_ref,
    skip_ref,
    forward_ref,
    spectrum_ref,
    inverse_ref,
    taps_out,
    spectrum_out,
    medium_out,
    query_out,
    key2_out,
    enter_out,
    leave_out,
    reach_main_out,
    late_hbm,
    gated_t,
    medium_t,
    query_all,
    key2_all,
    late,
    late_sem,
):

    tiles = key_t.shape[0]
    group = gated_t.shape[1] // LANES
    top = sublane((SEG, LANES)) == 0
    segment = sublane((SEG, LANES)).astype(F32)

    def slabs_of(ref, tile):
        head = [ref[tile, pl.ds(k, SEG, stride=HEAD), :] for k in range(HEAD)]
        main = [ref[tile, pl.ds(HEAD_ROWS + k, SEG, stride=MAIN), :] for k in range(MAIN)]
        return head, main

    def feature(ref, tile, taps_of, index, lanes):
        taps = [spread(taps_of[index, j : j + 1, lanes]) for j in range(3)]
        head, main = with_rims(*slabs_of(ref, tile))
        return fir3(head, taps) + fir3(main, taps)

    def body(step, _):
        for part in range(group):
            tile = step * group + part
            lanes = pl.ds(pl.multiple_of(tile * LANES, LANES), LANES)
            local = pl.ds(part * LANES, LANES)
            keys = feature(key_t, tile, short_ref, 1, lanes)
            values = feature(value_t, tile, short_ref, 2, lanes)
            for k in range(HEAD + MAIN):
                gated = keys[k] * values[k]
                if k < 2:
                    gated = jnp.where(top, 0.0, gated)
                gated_t[pl.ds(SEG * k, SEG), local] = gated
            for k, slab in enumerate(feature(query_t, tile, short_ref, 0, lanes)):
                query_all[part, pl.ds(SEG * k, SEG), :] = slab
            query_out[tile] = query_all[part, 0:HEAD_ROWS, :]
            for k, slab in enumerate(feature(key2_t, tile, second_ref, 1, lanes)):
                key2_all[part, pl.ds(SEG * k, SEG), :] = slab
            key2_out[tile] = key2_all[part, 0:HEAD_ROWS, :]
            for k, slab in enumerate(feature(query2_t, tile, second_ref, 0, lanes)):
                late[tile, pl.ds(SEG * k, SEG), :] = slab
            for k in range(HEAD):
                taps_out[tile, pl.ds(SEG * k, SEG), :] = taps_t[
                    tile, pl.ds(k, SEG, stride=HEAD), :
                ]

        filters = [taps_t[step * group + part, 0:TAPS, :] for part in range(group)]
        spectrum = matmul3(spectrum_ref[...], jnp.concatenate(filters, 1))
        both = matmul3(forward_ref[...], gated_t[...])
        first = spectral_product(both[:T], spectrum)
        second = spectral_product(both[T:], spectrum)
        medium_t[...] = matmul3(inverse_ref[...], jnp.concatenate([first, second], 0))

        for part in range(group):
            tile = step * group + part
            lanes = pl.ds(pl.multiple_of(tile * LANES, LANES), LANES)
            local = pl.ds(part * LANES, LANES)
            spectrum_out[tile] = spectrum[:, part * LANES : (part + 1) * LANES]
            medium_out[tile] = medium_t[0:HEAD_ROWS, local]
            taps = [spread(second_ref[2, j : j + 1, lanes]) for j in range(3)]
            firsts = [
                rows_of(medium_t, k, local) * query_all[part, pl.ds(SEG * k, SEG), :]
                for k in range(HEAD - 2, HEAD + MAIN)
            ]
            ends = [down(firsts[0]), down(firsts[1])]
            main = firsts[2:]
            main_all = [jnp.where(top, ends[k], down(main[MAIN - 2 + k])) for k in range(2)] + main
            values2 = fir3(main_all, taps)
            inputs = [
                key2_all[part, pl.ds(SEG * (HEAD + k), SEG), :] * values2[k] for k in range(MAIN)
            ]
            rates, gains = rate_ref[:, lanes], amplitude_ref[:, lanes]
            decays = jnp.exp(-rates)
            outs, ends = recurrence(
                inputs,
                [spread(decays[r : r + 1]) for r in range(MODES)],
                [spread(gains[r : r + 1]) for r in range(MODES)],
                spread(skip_ref[:, lanes]),
            )
            for k in range(MAIN):
                late[tile, pl.ds(T + SEG * k, SEG), :] = outs[k]
            pltpu.make_async_copy(late.at[tile], late_hbm.at[tile], late_sem.at[tile]).start()
            powers = segment_powers(rates, float(MAIN))
            for r in range(MODES):
                enter, leave = prefix(ends[r], powers, r)
                enter_out[tile, r] = enter
                leave_out[tile, r : r + 1, :] = leave
                rate = spread(rates[r : r + 1])
                reach_main_out[tile, r] = jnp.exp(-(rate * (segment * float(MAIN))))
        return _

    lax.fori_loop(0, tiles // group, body, 0)
    for tile in range(tiles):
        pltpu.make_async_copy(late.at[tile], late_hbm.at[tile], late_sem.at[tile]).wait()


def join_kernel(
    base,
    halo_ref,
    rims_ref,
    spectrum_ref,
    medium_ref,
    taps_ref,
    query_ref,
    key2_ref,
    key_t,
    value_t,
    enter_main_ref,
    leave_main_ref,
    reach_main_ref,
    short_ref,
    second_ref,
    rate_ref,
    amplitude_ref,
    skip_ref,
    forward_ref,
    inverse_ref,
    *rest,
):
    *before, state_out, late_hbm, medium_t, late, late_sem = rest
    tiles = halo_ref.shape[0]
    group = medium_t.shape[1] // LANES
    top = sublane((SEG, LANES)) == 0
    for ref in before:
        state_out[0:base] = ref[...]

    def body(step, _):
        tile_list = [base + step * group + part for part in range(group)]
        halo = matmul3(
            forward_ref[...], jnp.concatenate([halo_ref[tile - base] for tile in tile_list], 1)
        )
        filters = jnp.concatenate([spectrum_ref[tile] for tile in tile_list], 1)
        medium_t[...] = matmul3(inverse_ref[...], spectral_product(halo, filters))
        for part, tile in enumerate(tile_list):
            one(tile, pl.ds(part * LANES, LANES))
        return _

    def copy_of(tile):
        return pltpu.make_async_copy(late.at[tile], late_hbm.at[tile], late_sem.at[tile])

    def one(tile, local):
        lanes = pl.ds(pl.multiple_of(tile * LANES, LANES), LANES)

        def rim(k):
            return rims_ref[tile, k : k + 1, :]

        def taps_of(ref, index):
            return [ref[index, j : j + 1, lanes] for j in range(3)]

        def early(ref, place, index):
            taps = taps_of(short_ref, index)
            zero, one = ref[tile, 0:1, :], ref[tile, 1:2, :]
            older, last = rim(2 * place), rim(2 * place + 1)
            return (
                taps[0] * zero + taps[1] * last + taps[2] * older,
                taps[0] * one + taps[1] * zero + taps[2] * last,
            )

        def mended(ref, place, taps):
            slabs = [ref[tile, pl.ds(SEG * k, SEG), :] for k in range(HEAD)]
            older, last = rim(2 * place), rim(2 * place + 1)
            slabs[0] = slabs[0] + jnp.where(top, spread(taps[1] * last + taps[2] * older), 0.0)
            slabs[1] = slabs[1] + jnp.where(top, spread(taps[2] * last), 0.0)
            return slabs

        def tap(j):
            row = SEG * (j % HEAD) + j // HEAD
            return taps_ref[tile, row : row + 1, :]

        keys, values = early(key_t, 0, 1), early(value_t, 1, 2)
        gated = [spread(keys[k] * values[k]) for k in range(2)]
        taps = [taps_ref[tile, pl.ds(SEG * k, SEG), :] for k in range(HEAD)]
        shifted = [jnp.where(top, 0.0, down(taps[HEAD - 1]))] + taps
        query = mended(query_ref, 2, taps_of(short_ref, 0))
        key2 = mended(key2_ref, 4, taps_of(second_ref, 1))
        mediums = [
            medium_ref[tile, pl.ds(SEG * k, SEG), :]
            + rows_of(medium_t, k, local)
            + taps[k] * gated[0]
            + shifted[k] * gated[1]
            for k in range(HEAD)
        ]
        far, farther, farthest = rim(14), rim(13), rim(12)
        mediums[0] = mediums[0] + jnp.where(top, spread(tap(127) * far), 0.0)
        older = medium_t[HEAD_ROWS : HEAD_ROWS + 1, local] + (
            tap(125) * far + tap(126) * farther + tap(127) * farthest
        )
        last = medium_t[HEAD_ROWS + 1 : HEAD_ROWS + 2, local] + (
            tap(126) * far + tap(127) * farther
        )
        firsts = [query[k] * mediums[k] for k in range(HEAD)]
        firsts_all, _ = with_rims(firsts, None, (spread(rim(10) * older), spread(rim(11) * last)))
        values2 = fir3(firsts_all, [spread(t) for t in taps_of(second_ref, 2)])
        inputs = [key2[k] * values2[k] for k in range(HEAD)]
        rates, gains = rate_ref[:, lanes], amplitude_ref[:, lanes]
        decays = jnp.exp(-rates)
        outs, ends = recurrence(
            inputs,
            [spread(decays[r : r + 1]) for r in range(MODES)],
            [spread(gains[r : r + 1]) for r in range(MODES)],
            spread(skip_ref[:, lanes]),
        )
        for k in range(HEAD):
            late[tile - base, pl.ds(SEG * k, SEG), :] = outs[k]
        powers = segment_powers(rates, float(HEAD))
        whole = jnp.exp(-float(MAIN_ROWS) * rates)
        for r in range(MODES):
            enter, leave = prefix(ends[r], powers, r)
            late[tile - base, pl.ds(HEAD_ROWS + SEG * r, SEG), :] = enter
            late[tile - base, pl.ds(HEAD_ROWS + SEG * (MODES + r), SEG), :] = enter_main_ref[
                tile, r
            ] + reach_main_ref[tile, r] * spread(leave)
            state_out[tile, r : r + 1, :] = (
                leave_main_ref[tile, r : r + 1, :] + leave * whole[r : r + 1]
            )
        copy_of(tile - base).start()

    lax.fori_loop(0, tiles // group, body, 0, unroll=True)
    for tile in range(tiles):
        copy_of(tile).wait()


def ring_kernel(states_hbm, rate_ref, out_ref, states, sem):
    copy = pltpu.make_async_copy(states_hbm, states, sem)
    copy.start()
    decay = jnp.exp(-float(T) * rate_ref[...])
    copy.wait()
    total = states[0]
    for k in range(1, states.shape[0]):
        total = decay * total + states[k]
    for k in range(out_ref.shape[0]):
        out_ref[k] = total


def scan_kernel(place_ref, states_hbm, rings_ref, rate_ref, out_ref, states, sem):
    copy = pltpu.make_async_copy(states_hbm, states, sem)
    copy.start()
    ring = place_ref[0] // RING
    rates = rate_ref[...]
    decay = jnp.exp(-float(T) * rates)
    around = jnp.exp(-float(T * RING) * rates)
    entering = jnp.zeros_like(rates)
    for k in range(rings_ref.shape[0] - 1):
        entering = jnp.where(k < ring, around * entering + rings_ref[k], entering)
    copy.wait()
    for k in range(states.shape[0]):
        out_ref[k] = entering
        entering = decay * entering + states[k]


def finish_kernel(
    state_ref,
    early_hbm,
    late_hbm,
    later_hbm,
    rims_ref,
    second_ref,
    rate_ref,
    gain_ref,
    mixed_out,
    squares_out,
    early,
    late,
    reach,
    squares_t,
    sems,
):
    tiles = early_hbm.shape[0]
    chunks = sems.shape[1]
    count = tiles // chunks
    copies = []
    for chunk in range(chunks):
        here = pl.ds(chunk * count, count)
        first = chunk * count
        if first < late_hbm.shape[0]:
            joined = late_hbm.at[here]
        else:
            joined = later_hbm.at[pl.ds(first - late_hbm.shape[0], count)]
        for place, (source, target) in enumerate(((early_hbm.at[here], early), (joined, late))):
            copy = pltpu.make_async_copy(source, target.at[here], sems.at[place, chunk])
            copy.start()
            copies.append(copy)
    squares_t[...] = jnp.zeros_like(squares_t)
    top = sublane((SEG, LANES)) == 0
    segment = sublane((SEG, LANES)).astype(F32)

    def reaches(tile, _):
        lanes = pl.ds(pl.multiple_of(tile * LANES, LANES), LANES)
        for r in range(MODES):
            rate = spread(rate_ref[r : r + 1, lanes])
            reach[tile, r] = jnp.exp(-(rate * (segment * float(HEAD))))
            reach[tile, MODES + r] = jnp.exp(-(rate * (segment * float(MAIN) + float(HEAD_ROWS))))
        return _

    lax.fori_loop(0, tiles, reaches, 0)

    def body(tile, _):
        lanes = pl.ds(pl.multiple_of(tile * LANES, LANES), LANES)
        decays = jnp.exp(-rate_ref[:, lanes])
        taps = [second_ref[0, j : j + 1, lanes] for j in range(3)]
        older, last = rims_ref[tile, 6:7, :], rims_ref[tile, 7:8, :]
        mends = [spread(taps[1] * last + taps[2] * older), spread(taps[2] * last)]
        gain = spread(gain_ref[:, lanes])
        states = state_ref[tile]
        decay = [spread(decays[r : r + 1]) for r in range(MODES)]

        def half(length, half_index, own_ref, own_row, first_row):
            enter_row = HEAD_ROWS + half_index * MODES * SEG
            carry = [
                late[tile, pl.ds(enter_row + SEG * r, SEG), :]
                + reach[tile, half_index * MODES + r] * spread(states[r : r + 1])
                for r in range(MODES)
            ]
            for k in range(length):
                carry = [decay[r] * carry[r] for r in range(MODES)]
                total = own_ref[tile, pl.ds(own_row + SEG * k, SEG), :]
                for value in carry:
                    total = total + value
                rows = pl.ds(first_row + SEG * k, SEG)
                query = early[tile, rows, :]
                if first_row == 0 and k < 2:
                    query = query + jnp.where(top, mends[k], 0.0)
                mixed = query * total
                squares_t[rows, :] = squares_t[rows, :] + mixed * mixed
                mixed_out[tile, pl.ds(first_row + k, SEG, stride=length), :] = mixed * gain

        half(HEAD, 0, late, 0, 0)
        half(MAIN, 1, early, T, HEAD_ROWS)
        return _

    for chunk in range(chunks):
        copies[2 * chunk].wait()
        copies[2 * chunk + 1].wait()
        lax.fori_loop(chunk * count, (chunk + 1) * count, body, 0)
    sums = jnp.sum(squares_t[...], axis=1, keepdims=True)
    squares_t[...] = jnp.broadcast_to(sums, squares_t.shape)
    head = [squares_t[pl.ds(i, HEAD, stride=SEG), :] for i in range(SEG)]
    main = [squares_t[pl.ds(HEAD_ROWS + i, MAIN, stride=SEG), :] for i in range(SEG)]
    ordered = jnp.concatenate(head + main, 0)
    squares_out[...] = ordered.T[0:1, :]


def scale_kernel(divisor, mixed_ref, squares_ref, out_hbm, out_t, sems):
    scale = lax.rsqrt(squares_ref[...] / divisor + norm_eps)
    chunks = sems.shape[0]
    tiles = mixed_ref.shape[0] // chunks
    copies = []
    for chunk in range(chunks):
        for tile in range(chunk * tiles, (chunk + 1) * tiles):
            out_t[pl.ds(tile * LANES, LANES), :] = mixed_ref[tile].T * scale
        rows = pl.ds(chunk * tiles * LANES, tiles * LANES)
        copy = pltpu.make_async_copy(out_t.at[rows, :], out_hbm.at[rows, :], sems.at[chunk])
        copy.start()
        copies.append(copy)
    for copy in copies:
        copy.wait()


def from_behind(block):
    count = lax.axis_size("seq")
    return lax.ppermute(block, "seq", [(i, i + 1) for i in range(count - 1)])


def in_hbm(x):
    return pltpu.with_memory_space_constraint(x, pltpu.HBM)


def call(kernel, in_specs, out_specs, out_shape, scratch, flops, size, name):
    return pl.pallas_call(
        kernel,
        in_specs=in_specs,
        out_specs=out_specs,
        out_shape=out_shape,
        scratch_shapes=scratch,
        compiler_params=pltpu.CompilerParams(vmem_limit_bytes=LIMIT),
        cost_estimate=pl.CostEstimate(flops=flops, bytes_accessed=size, transcendentals=0),
        name=name,
    )


def exchange(rows, groups):
    return lax.all_to_all(
        rows, "seq", split_axis=0, concat_axis=0, axis_index_groups=groups, tiled=True
    )


def local(
    query_proj,
    key_proj,
    value_proj,
    second_query,
    second_key,
    short_filter,
    second_short,
    medium_filter,
    decay_rate,
    residue,
    skip_gain,
    norm_gain,
):
    channels = query_proj.shape[0]
    count = lax.axis_size("seq")
    tiles = channels // LANES
    group = min(4, tiles)
    join_group = min(2, tiles)
    chunks = min(4, tiles)
    parts = (tiles - tiles // chunks, tiles // chunks)
    short_t = jnp.transpose(short_filter, (0, 2, 1))
    second_t = jnp.transpose(second_short, (0, 2, 1))
    rate_t = decay_rate.T
    amplitude = residue.T * jnp.sqrt(-jnp.expm1(-2.0 * rate_t))
    skip = skip_gain[None, :]
    gain = norm_gain[None, :]
    forward, spectrum, inverse, halo_forward, halo_inverse = tables()
    held = pl.BlockSpec(memory_space=pltpu.VMEM)
    outside = pl.BlockSpec(memory_space=pl.ANY)
    words = channels * T

    def struct(*shape):
        return jax.ShapeDtypeStruct(shape, F32)

    def hbm(*shape):
        return pltpu.HBM(shape, F32)

    fields = [
        in_hbm(x) for x in (key_proj, value_proj, query_proj, second_query, second_key, medium_filter)
    ]
    rings = count // RING
    share = tiles // RING
    ring_groups = [[ring * RING + k for k in range(RING)] for ring in range(rings)]
    across_groups = [[ring * RING + k for ring in range(rings)] for k in range(RING)]
    place = lax.axis_index("seq").astype(jnp.int32).reshape(1)
    tail, own_rate = call(
        tail_kernel,
        [pl.BlockSpec(memory_space=pltpu.SMEM)] + [outside] * 4,
        [held] * 2,
        [struct(parts[0], TAPS, LANES), struct(share, MODES, LANES)],
        [pltpu.VMEM((parts[0] * LANES, LANES), F32)] * 2
        + [pltpu.VMEM((3, 3, channels), F32), pltpu.VMEM((share, MODES, LANES), F32)]
        + [pltpu.SemaphoreType.DMA((parts[0] // (tiles // chunks),))] * 2
        + [pltpu.SemaphoreType.DMA, pltpu.SemaphoreType.DMA((share,))],
        words * 8,
        words * 6,
        "tail",
    )(place, fields[0], fields[1], in_hbm(short_t), in_hbm(rate_t))
    halo = from_behind(tail)

    *turned_fields, taps_t, rims, tail_two = call(
        prep_kernel,
        [outside] * 6 + [held] * 2,
        [held] * 8,
        [struct(tiles, T, LANES)] * 5
        + [struct(tiles, HEAD_ROWS, LANES), struct(tiles, RIMS, LANES)]
        + [struct(parts[1], TAPS, LANES)],
        [pltpu.VMEM((channels, T), F32)] * 5
        + [pltpu.VMEM((channels, TAPS), F32), pltpu.SemaphoreType.DMA((6, chunks))],
        words * 20,
        words * 40,
        "prep",
    )(*fields, short_t, own_rate)
    border = from_behind(rims)
    halo_two = from_behind(tail_two)

    (
        taps,
        tap_spectrum,
        medium,
        query,
        key2,
        enter_main,
        leave_main,
        reach_main,
        early,
    ) = call(
        local_kernel,
        [held] * 14,
        [held] * 8 + [outside],
        [
            struct(tiles, HEAD_ROWS, LANES),
            struct(tiles, 384, LANES),
            struct(tiles, HEAD_ROWS, LANES),
            struct(tiles, HEAD_ROWS, LANES),
            struct(tiles, HEAD_ROWS, LANES),
            struct(tiles, MODES, SEG, LANES),
            struct(tiles, MODES, LANES),
            struct(tiles, MODES, SEG, LANES),
            hbm(tiles, T + MAIN_ROWS, LANES),
        ],
        [pltpu.VMEM((T, group * LANES), F32)] * 2
        + [pltpu.VMEM((group, T, LANES), F32)] * 2
        + [pltpu.VMEM((tiles, T + MAIN_ROWS, LANES), F32), pltpu.SemaphoreType.DMA((tiles,))],
        words * 8000,
        words * 60,
        "local",
    )(
        *turned_fields,
        taps_t,
        short_t,
        second_t,
        rate_t,
        amplitude,
        skip,
        forward,
        spectrum,
        inverse,
    )

    late_rows = HEAD_ROWS + 2 * MODES * SEG
    state, late = (), []
    for base, part in zip((0, parts[0]), (halo, halo_two)):
        count_here = part.shape[0]
        *state, joined = call(
            functools.partial(join_kernel, base),
            [held] * (19 + len(state)),
            [held, outside],
            [struct(base + count_here, MODES, LANES), hbm(count_here, late_rows, LANES)],
            [
                pltpu.VMEM((HEAD_ROWS + 8, join_group * LANES), F32),
                pltpu.VMEM((count_here, late_rows, LANES), F32),
                pltpu.SemaphoreType.DMA((count_here,)),
            ],
            count_here * 500 * T * LANES,
            count_here * 20 * T * LANES,
            "join",
        )(
            part,
            border,
            tap_spectrum,
            medium,
            taps,
            query,
            key2,
            turned_fields[0],
            turned_fields[1],
            enter_main,
            leave_main,
            reach_main,
            short_t,
            second_t,
            rate_t,
            amplitude,
            skip,
            halo_forward,
            halo_inverse,
            *state,
        )
        late.append(in_hbm(joined))
    (state,) = state

    share_shape = (RING, share, MODES, LANES)
    ring_states = in_hbm(exchange(state.reshape(share_shape), ring_groups))
    totals = call(
        ring_kernel,
        [outside, held],
        held,
        struct(rings, share, MODES, LANES),
        [pltpu.VMEM(share_shape, F32), pltpu.SemaphoreType.DMA],
        count * LANES * 30,
        count * LANES * 8,
        "ring",
    )(ring_states, own_rate)
    scanned = call(
        scan_kernel,
        [pl.BlockSpec(memory_space=pltpu.SMEM), outside, held, held],
        held,
        struct(*share_shape),
        [pltpu.VMEM(share_shape, F32), pltpu.SemaphoreType.DMA],
        count * LANES * 30,
        count * LANES * 8,
        "scan",
    )(place, ring_states, exchange(totals, across_groups), own_rate)
    incoming = exchange(scanned, ring_groups).reshape(tiles, MODES, LANES)

    mixed, squares = call(
        finish_kernel,
        [held] + [outside] * 3 + [held] * 4,
        [held] * 2,
        [struct(tiles, T, LANES), struct(1, T)],
        [
            pltpu.VMEM((tiles, T + MAIN_ROWS, LANES), F32),
            pltpu.VMEM((tiles, late_rows, LANES), F32),
            pltpu.VMEM((tiles, 2 * MODES, SEG, LANES), F32),
            pltpu.VMEM((T, LANES), F32),
            pltpu.SemaphoreType.DMA((2, chunks)),
        ],
        words * 40,
        words * 16,
        "finish",
    )(incoming, in_hbm(early), *late, border, second_t, rate_t, gain)
    total = lax.psum(squares, "chan")
    return call(
        functools.partial(scale_kernel, float(channels * lax.axis_size("chan"))),
        [held, held],
        outside,
        struct(channels, T),
        [pltpu.VMEM((channels, T), F32), pltpu.SemaphoreType.DMA((chunks,))],
        words,
        words * 8,
        "scale",
    )(mixed, total)


def solution(mesh):
    return jax.shard_map(
        local,
        mesh=mesh,
        in_specs=(
            P("chan", "seq"),
            P("chan", "seq"),
            P("chan", "seq"),
            P("chan", "seq"),
            P("chan", "seq"),
            P(None, "chan", None),
            P(None, "chan", None),
            P("chan", None),
            P("chan", None),
            P("chan", None),
            P("chan"),
            P("chan"),
        ),
        out_specs=P("chan", "seq"),
        check_vma=False,
    )
```

```python
import functools

import jax
import jax.numpy as jnp
import ml_dtypes
import numpy as np
from jax import lax
from jax.experimental import pallas as pl
from jax.experimental.pallas import tpu as pltpu
from jax.sharding import PartitionSpec as P

norm_eps = 1e-06

T = 256
TAPS = 128
MODES = 8
LANES = 128
SEG = 8
HEAD = 17
MAIN = 15
HEAD_ROWS = HEAD * SEG
MAIN_ROWS = MAIN * SEG
EARLY_ROWS = 144
RIMS = 16
RING = 8
LIMIT = 24 * 1024 * 1024

F32 = jnp.float32
BF16 = jnp.bfloat16


def row_times():
    head = [HEAD * i + k for k in range(HEAD) for i in range(SEG)]
    main = [HEAD_ROWS + MAIN * i + k for k in range(MAIN) for i in range(SEG)]
    return np.array(head + main)


def packed_forward(slots):
    k = np.arange(128)[:, None]
    angle = 2.0 * np.pi * k * np.asarray(slots)[None, :] / 256.0
    imag = -np.sin(angle)
    imag[0] = np.cos(np.pi * np.asarray(slots))
    return np.concatenate([np.cos(angle), imag], 0)


def packed_inverse(slots):
    k = np.arange(128)[None, :]
    angle = 2.0 * np.pi * k * np.asarray(slots)[:, None] / 256.0
    real = 2.0 * np.cos(angle)
    real[:, 0] = 1.0
    imag = -2.0 * np.sin(angle)
    imag[:, 0] = np.cos(np.pi * np.asarray(slots))
    return np.concatenate([real, imag], 1) / 256.0


def three_pass(matrix):
    high = matrix.astype(ml_dtypes.bfloat16)
    low = (matrix - high.astype(np.float64)).astype(ml_dtypes.bfloat16)
    return np.concatenate([high, low, high], 1)


def tables():
    times = row_times()
    early = times[:EARLY_ROWS]
    first = packed_forward(early + 128) * (early < 128)[None, :]
    second = packed_forward(times)
    taps = packed_forward(np.arange(TAPS))
    real, imag = taps[:128], taps[128:].copy()
    cross = real.copy()
    cross[0] = imag[0]
    imag[0] = 0.0
    spectrum = np.concatenate([real, imag, cross], 0)
    first_back = packed_inverse(early + 128) * (early < 128)[:, None]
    second_back = packed_inverse(times) * (times >= 128)[:, None]
    halo = packed_forward(np.arange(128))
    halo[:, :2] = 0.0
    head_times = np.concatenate([times[:HEAD_ROWS], [-2, -1], np.full(6, 255)])
    halo_back = packed_inverse(head_times + 128) * (head_times < 128)[:, None]
    matrices = (first, second, spectrum, first_back, second_back, halo, halo_back)
    return [three_pass(m) for m in matrices]


def halves(x):
    high = x.astype(BF16)
    low = (x - high.astype(F32)).astype(BF16)
    return high, low


def matmul_halves(matrix, high, low):
    stacked = jnp.concatenate([high, high, low], 0)
    return jnp.dot(matrix, stacked, preferred_element_type=F32)


def matmul3(matrix, x):
    return matmul_halves(matrix, *halves(x))


def spectral_product(x, taps):
    real, imag = x[:128], x[128:]
    tap_real, tap_imag, tap_cross = taps[:128], taps[128:256], taps[256:]
    return jnp.concatenate(
        [real * tap_real - imag * tap_imag, real * tap_imag + imag * tap_cross], 0
    )


def sublane(shape):
    return lax.broadcasted_iota(jnp.int32, shape, 0)


def down(x, distance=1):
    return pltpu.roll(x, distance, axis=0)


def fir3(slabs, taps):
    return [
        taps[0] * slabs[k + 2] + taps[1] * slabs[k + 1] + taps[2] * slabs[k]
        for k in range(len(slabs) - 2)
    ]


def with_rims(head, main, rims=None):
    top = sublane(head[0].shape) == 0
    zero = jnp.zeros_like(head[0])
    before = (zero, zero) if rims is None else rims
    ends = [down(head[HEAD - 2]), down(head[HEAD - 1])]
    head_all = [jnp.where(top, before[k], ends[k]) for k in range(2)] + head
    if main is None:
        return head_all, None
    main_all = [jnp.where(top, ends[k], down(main[MAIN - 2 + k])) for k in range(2)] + main
    return head_all, main_all


def rows_of(ref, k, lanes):
    return ref[pl.ds(SEG * k, SEG), lanes]


def spread(row):
    return jnp.broadcast_to(row, (SEG, row.shape[1]))


def recurrence(inputs, decays, gains, skip):
    states = [gains[r] * inputs[0] for r in range(MODES)]
    outs = []
    for k, value in enumerate(inputs):
        if k:
            states = [decays[r] * states[r] + gains[r] * value for r in range(MODES)]
        total = skip * value
        for state in states:
            total = total + state
        outs.append(total)
    return outs, states


def prefix(ends, rates, step, by_segment):
    for r in range(MODES):
        by_segment[pl.ds(r, SEG, stride=MODES), :] = ends[r]
    power = jnp.exp(-step * rates)
    enters = [jnp.zeros_like(rates)]
    for i in range(SEG):
        enters.append(power * enters[i] + by_segment[pl.ds(MODES * i, MODES), :])
    return enters[:SEG], enters[SEG]


def turned(block):
    return block.T


def tail_kernel(
    place_ref,
    key_hbm,
    value_hbm,
    short_hbm,
    rate_hbm,
    tail_ref,
    own_rate_out,
    key_in,
    value_in,
    short_ref,
    rates_in,
    key_sem,
    value_sem,
    short_sem,
    rate_sem,
):
    chunks = key_sem.shape[0]
    rows = key_in.shape[0] // chunks
    copies = []
    filters = pltpu.make_async_copy(short_hbm, short_ref, short_sem)
    filters.start()
    index = place_ref[0]
    share = rates_in.shape[0]
    first = lax.rem(index, RING) * (share * LANES)
    rates = []
    for part in range(share):
        mine = pl.ds(pl.multiple_of(first + part * LANES, LANES), LANES)
        copy = pltpu.make_async_copy(rate_hbm.at[:, mine], rates_in.at[part], rate_sem.at[part])
        copy.start()
        rates.append(copy)
    for chunk in range(chunks):
        here = pl.ds(chunk * rows, rows)
        for source, target, sem in (
            (key_hbm, key_in, key_sem),
            (value_hbm, value_in, value_sem),
        ):
            copy = pltpu.make_async_copy(
                source.at[here, pl.ds(LANES, LANES)], target.at[here, :], sem.at[chunk]
            )
            copy.start()
            copies.append(copy)
    filters.wait()
    for chunk in range(chunks):
        copies[2 * chunk].wait()
        copies[2 * chunk + 1].wait()
        for tile in range(chunk * rows // LANES, (chunk + 1) * rows // LANES):
            lanes = pl.ds(tile * LANES, LANES)

            def feature(ref, index):
                here = turned(ref[lanes, :])
                taps = [short_ref[index, j : j + 1, lanes] for j in range(3)]
                return taps[0] * here + taps[1] * down(here) + taps[2] * down(here, 2)

            tail_ref[tile] = feature(key_in, 1) * feature(value_in, 2)
    for copy in rates:
        copy.wait()
    own_rate_out[...] = rates_in[...]


def prep_kernel(
    key_hbm,
    value_hbm,
    query_hbm,
    query2_hbm,
    key2_hbm,
    medium_hbm,
    short_ref,
    _,
    key_t,
    value_t,
    query_t,
    query2_t,
    key2_t,
    taps_t,
    rims_out,
    tail_out,
    key_in,
    value_in,
    query_in,
    query2_in,
    key2_in,
    medium_in,
    sems,
):
    chunks = sems.shape[1]
    rows = key_hbm.shape[0] // chunks
    fields = (
        (key_hbm, key_in, key_t),
        (value_hbm, value_in, value_t),
        (query_hbm, query_in, query_t),
        (query2_hbm, query2_in, query2_t),
        (key2_hbm, key2_in, key2_t),
        (medium_hbm, medium_in, taps_t),
    )
    copies = []
    for chunk in range(chunks):
        here = pl.ds(chunk * rows, rows)
        for place, (source, target, _) in enumerate(fields):
            copy = pltpu.make_async_copy(
                source.at[here, :], target.at[here, :], sems.at[place, chunk]
            )
            copy.start()
            copies.append(copy)
    for chunk in range(chunks):
        for place in range(len(fields)):
            copies[chunk * len(fields) + place].wait()
        for tile in range(chunk * rows // LANES, (chunk + 1) * rows // LANES):
            lanes = pl.ds(tile * LANES, LANES)
            rims_out[tile] = jnp.zeros((RIMS, LANES), F32)
            for place, (_, source, target) in enumerate(fields):
                if place < 5:
                    target[tile] = turned(source[lanes, :])
                    rims_out[tile, 2 * place : 2 * place + 2, :] = target[tile, T - 2 : T, :]
                else:
                    target[tile, 0:TAPS, :] = turned(source[lanes, :])
                    target[tile, TAPS:HEAD_ROWS, :] = jnp.zeros((HEAD_ROWS - TAPS, LANES), F32)

            def feature(ref, index, time):
                return sum(
                    short_ref[index, j : j + 1, lanes] * ref[tile, time - j : time - j + 1, :]
                    for j in range(3)
                )

            late = tile - (key_t.shape[0] - tail_out.shape[0])
            if late >= 0:
                gated = 1.0
                for ref, index in ((key_t, 1), (value_t, 2)):
                    here = ref[tile, T // 2 : T, :]
                    taps = [short_ref[index, j : j + 1, lanes] for j in range(3)]
                    gated = gated * (taps[0] * here + taps[1] * down(here) + taps[2] * down(here, 2))
                tail_out[late] = gated
            for k in range(2):
                rims_out[tile, 10 + k : 11 + k, :] = feature(query_t, 0, T - 2 + k)
            for k in range(3):
                rims_out[tile, 12 + k : 13 + k, :] = feature(key_t, 1, T // 2 - 1 + k) * feature(
                    value_t, 2, T // 2 - 1 + k
                )


def local_kernel(
    key_t,
    value_t,
    query_t,
    query2_t,
    key2_t,
    taps_t,
    short_ref,
    second_ref,
    rate_ref,
    amplitude_ref,
    skip_ref,
    first_ref,
    second_window_ref,
    spectrum_ref,
    first_back_ref,
    second_back_ref,
    taps_out,
    spectrum_out,
    medium_out,
    query_out,
    key2_out,
    leave_out,
    late_hbm,
    gated_t,
    medium_t,
    query_all,
    key2_all,
    by_segment,
    late,
    late_sem,
):

    tiles = key_t.shape[0]
    group = gated_t.shape[1] // LANES
    top = sublane((SEG, LANES)) == 0

    def slabs_of(ref, tile):
        head = [ref[tile, pl.ds(k, SEG, stride=HEAD), :] for k in range(HEAD)]
        main = [ref[tile, pl.ds(HEAD_ROWS + k, SEG, stride=MAIN), :] for k in range(MAIN)]
        return head, main

    def feature(ref, tile, taps_of, index, lanes):
        taps = [spread(taps_of[index, j : j + 1, lanes]) for j in range(3)]
        head, main = with_rims(*slabs_of(ref, tile))
        return fir3(head, taps) + fir3(main, taps)

    def body(step, _):
        for part in range(group):
            tile = step * group + part
            lanes = pl.ds(pl.multiple_of(tile * LANES, LANES), LANES)
            local = pl.ds(part * LANES, LANES)
            keys = feature(key_t, tile, short_ref, 1, lanes)
            values = feature(value_t, tile, short_ref, 2, lanes)
            for k in range(HEAD + MAIN):
                gated = keys[k] * values[k]
                if k < 2:
                    gated = jnp.where(top, 0.0, gated)
                gated_t[pl.ds(SEG * k, SEG), local] = gated
            for k, slab in enumerate(feature(query_t, tile, short_ref, 0, lanes)):
                query_all[part, pl.ds(SEG * k, SEG), :] = slab
            query_out[tile] = query_all[part, 0:HEAD_ROWS, :]
            for k, slab in enumerate(feature(key2_t, tile, second_ref, 1, lanes)):
                key2_all[part, pl.ds(SEG * k, SEG), :] = slab
            key2_out[tile] = key2_all[part, 0:HEAD_ROWS, :]
            for k, slab in enumerate(feature(query2_t, tile, second_ref, 0, lanes)):
                late[tile, pl.ds(SEG * k, SEG), :] = slab
            for k in range(HEAD):
                taps_out[tile, pl.ds(SEG * k, SEG), :] = taps_t[
                    tile, pl.ds(k, SEG, stride=HEAD), :
                ]

        filters = [taps_t[step * group + part, 0:TAPS, :] for part in range(group)]
        spectrum = matmul3(spectrum_ref[...], jnp.concatenate(filters, 1))
        high, low = halves(gated_t[...])
        first = matmul_halves(first_ref[...], high[:EARLY_ROWS], low[:EARLY_ROWS])
        second = matmul_halves(second_window_ref[...], high, low)
        medium_t[...] = matmul3(second_back_ref[...], spectral_product(second, spectrum))
        head = matmul3(first_back_ref[...], spectral_product(first, spectrum))
        medium_t[0:HEAD_ROWS, :] = medium_t[0:HEAD_ROWS, :] + head[0:HEAD_ROWS]

        for part in range(group):
            tile = step * group + part
            lanes = pl.ds(pl.multiple_of(tile * LANES, LANES), LANES)
            local = pl.ds(part * LANES, LANES)
            spectrum_out[tile] = spectrum[:, part * LANES : (part + 1) * LANES]
            medium_out[tile] = medium_t[0:HEAD_ROWS, local]
            taps = [spread(second_ref[2, j : j + 1, lanes]) for j in range(3)]
            firsts = [
                rows_of(medium_t, k, local) * query_all[part, pl.ds(SEG * k, SEG), :]
                for k in range(HEAD - 2, HEAD + MAIN)
            ]
            ends = [down(firsts[0]), down(firsts[1])]
            main = firsts[2:]
            main_all = [jnp.where(top, ends[k], down(main[MAIN - 2 + k])) for k in range(2)] + main
            values2 = fir3(main_all, taps)
            inputs = [
                key2_all[part, pl.ds(SEG * (HEAD + k), SEG), :] * values2[k] for k in range(MAIN)
            ]
            rates, gains = rate_ref[:, lanes], amplitude_ref[:, lanes]
            decays = jnp.exp(-rates)
            outs, ends = recurrence(
                inputs,
                [spread(decays[r : r + 1]) for r in range(MODES)],
                [spread(gains[r : r + 1]) for r in range(MODES)],
                spread(skip_ref[:, lanes]),
            )
            for k in range(MAIN):
                late[tile, pl.ds(T + SEG * k, SEG), :] = outs[k]
            enters, leave_out[tile] = prefix(ends, rates, float(MAIN), by_segment.at[part])
            for i in range(SEG):
                late[tile, pl.ds(T + MAIN_ROWS + MODES * i, MODES), :] = enters[i]
            pltpu.make_async_copy(late.at[tile], late_hbm.at[tile], late_sem.at[tile]).start()
        return _

    lax.fori_loop(0, tiles // group, body, 0)
    for tile in range(tiles):
        pltpu.make_async_copy(late.at[tile], late_hbm.at[tile], late_sem.at[tile]).wait()


def join_kernel(
    base,
    halo_ref,
    rims_ref,
    spectrum_ref,
    medium_ref,
    taps_ref,
    query_ref,
    key2_ref,
    key_t,
    value_t,
    leave_main_ref,
    short_ref,
    second_ref,
    rate_ref,
    amplitude_ref,
    skip_ref,
    forward_ref,
    inverse_ref,
    *rest,
):
    tiles = halo_ref.shape[0]
    copies = []
    if base:
        state_ref, late_ref, state_out, late_hbm, medium_t, by_segment, late, late_sem = rest
        state_out[0:base] = state_ref[...]
        copies.append(
            pltpu.make_async_copy(late_ref, late_hbm.at[pl.ds(0, base)], late_sem.at[tiles])
        )
        copies[0].start()
    else:
        state_out, late, medium_t, by_segment = rest
    group = medium_t.shape[2] // LANES
    top = sublane((SEG, LANES)) == 0

    def body(step):
        tile_list = [base + step * group + part for part in range(group)]
        halo = matmul3(
            forward_ref[...], jnp.concatenate([halo_ref[tile - base] for tile in tile_list], 1)
        )
        filters = jnp.concatenate([spectrum_ref[tile] for tile in tile_list], 1)
        medium_t[step] = matmul3(inverse_ref[...], spectral_product(halo, filters))
        for part, tile in enumerate(tile_list):
            one(tile, medium_t.at[step], pl.ds(part * LANES, LANES), tile - base)

    def one(tile, medium_t, local, slot):
        lanes = pl.ds(tile * LANES, LANES)

        def rim(k):
            return rims_ref[tile, k : k + 1, :]

        def taps_of(ref, index):
            return [ref[index, j : j + 1, lanes] for j in range(3)]

        def early(ref, place, index):
            taps = taps_of(short_ref, index)
            zero, one = ref[tile, 0:1, :], ref[tile, 1:2, :]
            older, last = rim(2 * place), rim(2 * place + 1)
            return (
                taps[0] * zero + taps[1] * last + taps[2] * older,
                taps[0] * one + taps[1] * zero + taps[2] * last,
            )

        def mended(ref, place, taps):
            slabs = [ref[tile, pl.ds(SEG * k, SEG), :] for k in range(HEAD)]
            older, last = rim(2 * place), rim(2 * place + 1)
            slabs[0] = slabs[0] + jnp.where(top, spread(taps[1] * last + taps[2] * older), 0.0)
            slabs[1] = slabs[1] + jnp.where(top, spread(taps[2] * last), 0.0)
            return slabs

        def tap(j):
            row = SEG * (j % HEAD) + j // HEAD
            return taps_ref[tile, row : row + 1, :]

        keys, values = early(key_t, 0, 1), early(value_t, 1, 2)
        gated = [spread(keys[k] * values[k]) for k in range(2)]
        taps = [taps_ref[tile, pl.ds(SEG * k, SEG), :] for k in range(HEAD)]
        shifted = [jnp.where(top, 0.0, down(taps[HEAD - 1]))] + taps
        query = mended(query_ref, 2, taps_of(short_ref, 0))
        key2 = mended(key2_ref, 4, taps_of(second_ref, 1))
        mediums = [
            medium_ref[tile, pl.ds(SEG * k, SEG), :]
            + rows_of(medium_t, k, local)
            + taps[k] * gated[0]
            + shifted[k] * gated[1]
            for k in range(HEAD)
        ]
        far, farther, farthest = rim(14), rim(13), rim(12)
        mediums[0] = mediums[0] + jnp.where(top, spread(tap(127) * far), 0.0)
        older = medium_t[HEAD_ROWS : HEAD_ROWS + 1, local] + (
            tap(125) * far + tap(126) * farther + tap(127) * farthest
        )
        last = medium_t[HEAD_ROWS + 1 : HEAD_ROWS + 2, local] + (
            tap(126) * far + tap(127) * farther
        )
        firsts = [query[k] * mediums[k] for k in range(HEAD)]
        firsts_all, _ = with_rims(firsts, None, (spread(rim(10) * older), spread(rim(11) * last)))
        values2 = fir3(firsts_all, [spread(t) for t in taps_of(second_ref, 2)])
        inputs = [key2[k] * values2[k] for k in range(HEAD)]
        rates, gains = rate_ref[:, lanes], amplitude_ref[:, lanes]
        decays = jnp.exp(-rates)
        outs, ends = recurrence(
            inputs,
            [spread(decays[r : r + 1]) for r in range(MODES)],
            [spread(gains[r : r + 1]) for r in range(MODES)],
            spread(skip_ref[:, lanes]),
        )
        for k in range(HEAD):
            late[tile - base, pl.ds(SEG * k, SEG), :] = outs[k]
        enters, leave = prefix(ends, rates, float(HEAD), by_segment.at[slot])
        for i in range(SEG):
            late[tile - base, pl.ds(HEAD_ROWS + MODES * i, MODES), :] = enters[i]
        late[tile - base, pl.ds(HEAD_ROWS + MODES * SEG, MODES), :] = leave
        state_out[tile] = leave_main_ref[tile] + leave * jnp.exp(-float(MAIN_ROWS) * rates)
        if base:
            copy = pltpu.make_async_copy(
                late.at[tile - base], late_hbm.at[tile], late_sem.at[tile - base]
            )
            copy.start()
            copies.append(copy)

    for step in range(tiles // group):
        body(step)
    for copy in copies:
        copy.wait()


def ring_kernel(states_hbm, rate_ref, out_ref, states, sem):
    copy = pltpu.make_async_copy(states_hbm, states, sem)
    copy.start()
    decay = jnp.exp(-float(T) * rate_ref[...])
    copy.wait()
    total = states[0]
    for k in range(1, states.shape[0]):
        total = decay * total + states[k]
    for k in range(out_ref.shape[0]):
        out_ref[k] = total


def scan_kernel(place_ref, states_hbm, rings_ref, rate_ref, out_ref, states, sem):
    copy = pltpu.make_async_copy(states_hbm, states, sem)
    copy.start()
    ring = place_ref[0] // RING
    rates = rate_ref[...]
    decay = jnp.exp(-float(T) * rates)
    around = jnp.exp(-float(T * RING) * rates)
    entering = jnp.zeros_like(rates)
    for k in range(rings_ref.shape[0] - 1):
        entering = jnp.where(k < ring, around * entering + rings_ref[k], entering)
    copy.wait()
    for k in range(states.shape[0]):
        out_ref[k] = entering
        entering = decay * entering + states[k]


def finish_kernel(
    state_ref,
    early_hbm,
    late_hbm,
    rims_ref,
    second_ref,
    rate_ref,
    gain_ref,
    mixed_out,
    squares_out,
    early,
    late,
    by_segment,
    squares_t,
    sems,
):
    tiles = early_hbm.shape[0]
    chunks = sems.shape[1]
    count = tiles // chunks
    copies = []
    for chunk in range(chunks):
        here = pl.ds(chunk * count, count)
        for place, (source, target) in enumerate(((early_hbm, early), (late_hbm, late))):
            copy = pltpu.make_async_copy(source.at[here], target.at[here], sems.at[place, chunk])
            copy.start()
            copies.append(copy)
    squares_t[...] = jnp.zeros_like(squares_t)
    top = sublane((SEG, LANES)) == 0

    def body(tile):
        lanes = pl.ds(tile * LANES, LANES)
        rates = rate_ref[:, lanes]
        decays = jnp.exp(-rates)
        taps = [second_ref[0, j : j + 1, lanes] for j in range(3)]
        older, last = rims_ref[tile, 6:7, :], rims_ref[tile, 7:8, :]
        mends = [spread(taps[1] * last + taps[2] * older), spread(taps[2] * last)]
        gain = spread(gain_ref[:, lanes])
        states = state_ref[tile]
        decay = [spread(decays[r : r + 1]) for r in range(MODES)]

        def half(length, entering, enter_ref, enter_row, own_ref, own_row, first_row):
            step = jnp.exp(-float(length) * rates)
            slot = 0 if first_row == 0 else 1
            for i in range(SEG):
                rows = pl.ds(MODES * i, MODES)
                enter = enter_ref[tile, pl.ds(enter_row + MODES * i, MODES), :]
                by_segment[slot, rows, :] = enter + entering
                entering = step * entering
            carry = [by_segment[slot, pl.ds(r, SEG, stride=MODES), :] for r in range(MODES)]
            for k in range(length):
                carry = [decay[r] * carry[r] for r in range(MODES)]
                total = own_ref[tile, pl.ds(own_row + SEG * k, SEG), :]
                for value in carry:
                    total = total + value
                rows = pl.ds(first_row + SEG * k, SEG)
                query = early[tile, rows, :]
                if first_row == 0 and k < 2:
                    query = query + jnp.where(top, mends[k], 0.0)
                mixed = query * total
                squares_t[rows, :] = squares_t[rows, :] + mixed * mixed
                mixed_out[tile, pl.ds(first_row + k, SEG, stride=length), :] = mixed * gain

        leave = late[tile, pl.ds(HEAD_ROWS + MODES * SEG, MODES), :]
        later = leave + states * jnp.exp(-float(HEAD_ROWS) * rates)
        half(HEAD, states, late, HEAD_ROWS, late, 0, 0)
        half(MAIN, later, early, T + MAIN_ROWS, early, T, HEAD_ROWS)

    for chunk in range(chunks):
        copies[2 * chunk].wait()
        copies[2 * chunk + 1].wait()
        for tile in range(chunk * count, (chunk + 1) * count):
            body(tile)
    sums = jnp.sum(squares_t[...], axis=1, keepdims=True)
    squares_t[...] = jnp.broadcast_to(sums, squares_t.shape)
    head = [squares_t[pl.ds(i, HEAD, stride=SEG), :] for i in range(SEG)]
    main = [squares_t[pl.ds(HEAD_ROWS + i, MAIN, stride=SEG), :] for i in range(SEG)]
    ordered = jnp.concatenate(head + main, 0)
    squares_out[...] = ordered.T[0:1, :]


def scale_kernel(divisor, mixed_ref, squares_ref, out_hbm, out_t, sems):
    scale = lax.rsqrt(squares_ref[...] / divisor + norm_eps)
    chunks = sems.shape[0]
    tiles = mixed_ref.shape[0] // chunks
    copies = []
    for chunk in range(chunks):
        for tile in range(chunk * tiles, (chunk + 1) * tiles):
            out_t[pl.ds(tile * LANES, LANES), :] = mixed_ref[tile].T * scale
        rows = pl.ds(chunk * tiles * LANES, tiles * LANES)
        copy = pltpu.make_async_copy(out_t.at[rows, :], out_hbm.at[rows, :], sems.at[chunk])
        copy.start()
        copies.append(copy)
    for copy in copies:
        copy.wait()


def from_behind(block):
    count = lax.axis_size("seq")
    return lax.ppermute(block, "seq", [(i, i + 1) for i in range(count - 1)])


def in_hbm(x):
    return pltpu.with_memory_space_constraint(x, pltpu.HBM)


def call(kernel, in_specs, out_specs, out_shape, scratch, flops, size, name):
    return pl.pallas_call(
        kernel,
        in_specs=in_specs,
        out_specs=out_specs,
        out_shape=out_shape,
        scratch_shapes=scratch,
        compiler_params=pltpu.CompilerParams(vmem_limit_bytes=LIMIT),
        cost_estimate=pl.CostEstimate(flops=flops, bytes_accessed=size, transcendentals=0),
        name=name,
    )


def exchange(rows, groups):
    return lax.all_to_all(
        rows, "seq", split_axis=0, concat_axis=0, axis_index_groups=groups, tiled=True
    )


def local(
    query_proj,
    key_proj,
    value_proj,
    second_query,
    second_key,
    short_filter,
    second_short,
    medium_filter,
    decay_rate,
    residue,
    skip_gain,
    norm_gain,
):
    channels = query_proj.shape[0]
    count = lax.axis_size("seq")
    tiles = channels // LANES
    group = min(8, tiles)
    chunks = min(4, tiles)
    parts = (tiles - tiles // chunks, tiles // chunks)
    short_t = jnp.transpose(short_filter, (0, 2, 1))
    second_t = jnp.transpose(second_short, (0, 2, 1))
    rate_t = decay_rate.T
    amplitude = residue.T * jnp.sqrt(-jnp.expm1(-2.0 * rate_t))
    skip = skip_gain[None, :]
    gain = norm_gain[None, :]
    *windows, halo_forward, halo_inverse = tables()
    held = pl.BlockSpec(memory_space=pltpu.VMEM)
    outside = pl.BlockSpec(memory_space=pl.ANY)
    words = channels * T

    def struct(*shape):
        return jax.ShapeDtypeStruct(shape, F32)

    def hbm(*shape):
        return pltpu.HBM(shape, F32)

    fields = [
        in_hbm(x) for x in (key_proj, value_proj, query_proj, second_query, second_key, medium_filter)
    ]
    rings = count // RING
    share = tiles // RING
    ring_groups = [[ring * RING + k for k in range(RING)] for ring in range(rings)]
    across_groups = [[ring * RING + k for ring in range(rings)] for k in range(RING)]
    place = lax.axis_index("seq").astype(jnp.int32).reshape(1)
    tail, own_rate = call(
        tail_kernel,
        [pl.BlockSpec(memory_space=pltpu.SMEM)] + [outside] * 4,
        [held] * 2,
        [struct(parts[0], TAPS, LANES), struct(share, MODES, LANES)],
        [pltpu.VMEM((parts[0] * LANES, LANES), F32)] * 2
        + [pltpu.VMEM((3, 3, channels), F32), pltpu.VMEM((share, MODES, LANES), F32)]
        + [pltpu.SemaphoreType.DMA((2,))] * 2
        + [pltpu.SemaphoreType.DMA, pltpu.SemaphoreType.DMA((share,))],
        words * 8,
        words * 6,
        "tail",
    )(place, fields[0], fields[1], in_hbm(short_t), in_hbm(rate_t))
    halo = from_behind(tail)

    *turned_fields, taps_t, rims, tail_two = call(
        prep_kernel,
        [outside] * 6 + [held] * 2,
        [held] * 8,
        [struct(tiles, T, LANES)] * 5
        + [struct(tiles, HEAD_ROWS, LANES), struct(tiles, RIMS, LANES)]
        + [struct(parts[1], TAPS, LANES)],
        [pltpu.VMEM((channels, T), F32)] * 5
        + [pltpu.VMEM((channels, TAPS), F32), pltpu.SemaphoreType.DMA((6, chunks))],
        words * 20,
        words * 40,
        "prep",
    )(*fields, short_t, own_rate)
    border = from_behind(rims)
    halo_two = from_behind(tail_two)

    early_rows = T + MAIN_ROWS + MODES * SEG
    (
        taps,
        tap_spectrum,
        medium,
        query,
        key2,
        leave_main,
        early,
    ) = call(
        local_kernel,
        [held] * (11 + len(windows)),
        [held] * 6 + [outside],
        [
            struct(tiles, HEAD_ROWS, LANES),
            struct(tiles, 384, LANES),
            struct(tiles, HEAD_ROWS, LANES),
            struct(tiles, HEAD_ROWS, LANES),
            struct(tiles, HEAD_ROWS, LANES),
            struct(tiles, MODES, LANES),
            hbm(tiles, early_rows, LANES),
        ],
        [pltpu.VMEM((T, group * LANES), F32)] * 2
        + [pltpu.VMEM((group, T, LANES), F32)] * 2
        + [pltpu.VMEM((group, MODES * SEG, LANES), F32)]
        + [pltpu.VMEM((tiles, early_rows, LANES), F32), pltpu.SemaphoreType.DMA((tiles,))],
        words * 8000,
        words * 60,
        "local",
    )(
        *turned_fields,
        taps_t,
        short_t,
        second_t,
        rate_t,
        amplitude,
        skip,
        *windows,
    )

    late_rows = HEAD_ROWS + MODES * SEG + MODES
    joined = ()
    for base, part in zip((0, parts[0]), (halo, halo_two)):
        here = part.shape[0]
        join_group = 2 if base else 4
        late_shape = (base + here, late_rows, LANES)
        scratch = [
            pltpu.VMEM((here // join_group, HEAD_ROWS + 8, join_group * LANES), F32),
            pltpu.VMEM((here, MODES * SEG, LANES), F32),
        ]
        if base:
            scratch.append(pltpu.VMEM((here, late_rows, LANES), F32))
            scratch.append(pltpu.SemaphoreType.DMA((here + 1,)))
        joined = call(
            functools.partial(join_kernel, base),
            [held] * (17 + len(joined)),
            [held, outside if base else held],
            [struct(base + here, MODES, LANES), (hbm if base else struct)(*late_shape)],
            scratch,
            here * 500 * T * LANES,
            here * 20 * T * LANES,
            "join",
        )(
            part,
            border,
            tap_spectrum,
            medium,
            taps,
            query,
            key2,
            turned_fields[0],
            turned_fields[1],
            leave_main,
            short_t,
            second_t,
            rate_t,
            amplitude,
            skip,
            halo_forward,
            halo_inverse,
            *joined,
        )
    state, late = joined

    share_shape = (RING, share, MODES, LANES)
    ring_states = in_hbm(exchange(state.reshape(share_shape), ring_groups))
    totals = call(
        ring_kernel,
        [outside, held],
        held,
        struct(rings, share, MODES, LANES),
        [pltpu.VMEM(share_shape, F32), pltpu.SemaphoreType.DMA],
        count * LANES * 30,
        count * LANES * 8,
        "ring",
    )(ring_states, own_rate)
    scanned = call(
        scan_kernel,
        [pl.BlockSpec(memory_space=pltpu.SMEM), outside, held, held],
        held,
        struct(*share_shape),
        [pltpu.VMEM(share_shape, F32), pltpu.SemaphoreType.DMA],
        count * LANES * 30,
        count * LANES * 8,
        "scan",
    )(place, ring_states, exchange(totals, across_groups), own_rate)
    incoming = exchange(scanned, ring_groups).reshape(tiles, MODES, LANES)

    mixed, squares = call(
        finish_kernel,
        [held] + [outside] * 2 + [held] * 4,
        [held] * 2,
        [struct(tiles, T, LANES), struct(1, T)],
        [
            pltpu.VMEM((tiles, early_rows, LANES), F32),
            pltpu.VMEM((tiles, late_rows, LANES), F32),
            pltpu.VMEM((2, MODES * SEG, LANES), F32),
            pltpu.VMEM((T, LANES), F32),
            pltpu.SemaphoreType.DMA((2, 2 * chunks)),
        ],
        words * 40,
        words * 16,
        "finish",
    )(incoming, in_hbm(early), in_hbm(late), border, second_t, rate_t, gain)
    total = lax.psum(squares, "chan")
    return call(
        functools.partial(scale_kernel, float(channels * lax.axis_size("chan"))),
        [held, held],
        outside,
        struct(channels, T),
        [pltpu.VMEM((channels, T), F32), pltpu.SemaphoreType.DMA((chunks,))],
        words,
        words * 8,
        "scale",
    )(mixed, total)


def solution(mesh):
    return jax.shard_map(
        local,
        mesh=mesh,
        in_specs=(
            P("chan", "seq"),
            P("chan", "seq"),
            P("chan", "seq"),
            P("chan", "seq"),
            P("chan", "seq"),
            P(None, "chan", None),
            P(None, "chan", None),
            P("chan", None),
            P("chan", None),
            P("chan", None),
            P("chan"),
            P("chan"),
        ),
        out_specs=P("chan", "seq"),
        check_vma=False,
    )
```

```python
import functools

import jax
import jax.numpy as jnp
import ml_dtypes
import numpy as np
from jax import lax
from jax.experimental import pallas as pl
from jax.experimental.pallas import tpu as pltpu
from jax.sharding import PartitionSpec as P

norm_eps = 1e-06

T = 256
TAPS = 128
MODES = 8
LANES = 128
SEG = 8
HEAD = 17
MAIN = 15
HEAD_ROWS = HEAD * SEG
MAIN_ROWS = MAIN * SEG
EARLY_ROWS = 144
RIMS = 16
RING = 8
LIMIT = 24 * 1024 * 1024

F32 = jnp.float32
BF16 = jnp.bfloat16


def row_times():
    head = [HEAD * i + k for k in range(HEAD) for i in range(SEG)]
    main = [HEAD_ROWS + MAIN * i + k for k in range(MAIN) for i in range(SEG)]
    return np.array(head + main)


def packed_forward(slots):
    k = np.arange(128)[:, None]
    angle = 2.0 * np.pi * k * np.asarray(slots)[None, :] / 256.0
    imag = -np.sin(angle)
    imag[0] = np.cos(np.pi * np.asarray(slots))
    return np.concatenate([np.cos(angle), imag], 0)


def packed_inverse(slots):
    k = np.arange(128)[None, :]
    angle = 2.0 * np.pi * k * np.asarray(slots)[:, None] / 256.0
    real = 2.0 * np.cos(angle)
    real[:, 0] = 1.0
    imag = -2.0 * np.sin(angle)
    imag[:, 0] = np.cos(np.pi * np.asarray(slots))
    return np.concatenate([real, imag], 1) / 256.0


def three_pass(matrix):
    high = matrix.astype(ml_dtypes.bfloat16)
    low = (matrix - high.astype(np.float64)).astype(ml_dtypes.bfloat16)
    return np.concatenate([high, low, high], 1)


def tables():
    times = row_times()
    early = times[:EARLY_ROWS]
    first = packed_forward(early + 128) * (early < 128)[None, :]
    second = packed_forward(times)
    taps = packed_forward(np.arange(TAPS))
    real, imag = taps[:128], taps[128:].copy()
    cross = real.copy()
    cross[0] = imag[0]
    imag[0] = 0.0
    spectrum = np.concatenate([real, imag, cross], 0)
    first_back = packed_inverse(early + 128) * (early < 128)[:, None]
    second_back = packed_inverse(times) * (times >= 128)[:, None]
    halo = packed_forward(np.arange(128))
    halo[:, :2] = 0.0
    head_times = np.concatenate([times[:HEAD_ROWS], [-2, -1], np.full(6, 255)])
    halo_back = packed_inverse(head_times + 128) * (head_times < 128)[:, None]
    matrices = (first, second, spectrum, first_back, second_back, halo, halo_back)
    return [three_pass(m) for m in matrices]


def halves(x):
    high = x.astype(BF16)
    low = (x - high.astype(F32)).astype(BF16)
    return high, low


def matmul_halves(matrix, high, low):
    stacked = jnp.concatenate([high, high, low], 0)
    return jnp.dot(matrix, stacked, preferred_element_type=F32)


def matmul3(matrix, x):
    return matmul_halves(matrix, *halves(x))


def spectral_product(x, taps):
    real, imag = x[:128], x[128:]
    tap_real, tap_imag, tap_cross = taps[:128], taps[128:256], taps[256:]
    return jnp.concatenate(
        [real * tap_real - imag * tap_imag, real * tap_imag + imag * tap_cross], 0
    )


def sublane(shape):
    return lax.broadcasted_iota(jnp.int32, shape, 0)


def down(x, distance=1):
    return pltpu.roll(x, distance, axis=0)


def fir3(slabs, taps):
    return [
        taps[0] * slabs[k + 2] + taps[1] * slabs[k + 1] + taps[2] * slabs[k]
        for k in range(len(slabs) - 2)
    ]


def with_rims(head, main, rims=None):
    top = sublane(head[0].shape) == 0
    zero = jnp.zeros_like(head[0])
    before = (zero, zero) if rims is None else rims
    ends = [down(head[HEAD - 2]), down(head[HEAD - 1])]
    head_all = [jnp.where(top, before[k], ends[k]) for k in range(2)] + head
    if main is None:
        return head_all, None
    main_all = [jnp.where(top, ends[k], down(main[MAIN - 2 + k])) for k in range(2)] + main
    return head_all, main_all


def rows_of(ref, k, lanes):
    return ref[pl.ds(SEG * k, SEG), lanes]


def spread(row):
    return jnp.broadcast_to(row, (SEG, row.shape[1]))


def recurrence(inputs, decays, gains, skip):
    states = [gains[r] * inputs[0] for r in range(MODES)]
    outs = []
    for k, value in enumerate(inputs):
        if k:
            states = [decays[r] * states[r] + gains[r] * value for r in range(MODES)]
        total = skip * value
        for state in states:
            total = total + state
        outs.append(total)
    return outs, states


def prefix(ends, rates, step, by_segment):
    for r in range(MODES):
        by_segment[pl.ds(r, SEG, stride=MODES), :] = ends[r]
    power = jnp.exp(-step * rates)
    enters = [jnp.zeros_like(rates)]
    for i in range(SEG):
        enters.append(power * enters[i] + by_segment[pl.ds(MODES * i, MODES), :])
    return enters[:SEG], enters[SEG]


def turned(block):
    return block.T


def tail_kernel(
    place_ref,
    key_hbm,
    value_hbm,
    short_hbm,
    rate_hbm,
    tail_ref,
    own_rate_out,
    key_in,
    value_in,
    short_ref,
    rates_in,
    key_sem,
    value_sem,
    short_sem,
    rate_sem,
):
    chunks = key_sem.shape[0]
    tiles = tail_ref.shape[0]
    bounds = [chunk * tiles // chunks for chunk in range(chunks + 1)]
    copies = []
    filters = pltpu.make_async_copy(short_hbm, short_ref, short_sem)
    filters.start()
    index = place_ref[0]
    share = rates_in.shape[0]
    first = lax.rem(index, RING) * (share * LANES)
    rates = []
    for part in range(share):
        mine = pl.ds(pl.multiple_of(first + part * LANES, LANES), LANES)
        copy = pltpu.make_async_copy(rate_hbm.at[:, mine], rates_in.at[part], rate_sem.at[part])
        copy.start()
        rates.append(copy)
    for chunk in range(chunks):
        here = pl.ds(bounds[chunk] * LANES, (bounds[chunk + 1] - bounds[chunk]) * LANES)
        for source, target, sem in (
            (key_hbm, key_in, key_sem),
            (value_hbm, value_in, value_sem),
        ):
            copy = pltpu.make_async_copy(
                source.at[here, pl.ds(LANES, LANES)], target.at[here, :], sem.at[chunk]
            )
            copy.start()
            copies.append(copy)
    filters.wait()
    for chunk in range(chunks):
        copies[2 * chunk].wait()
        copies[2 * chunk + 1].wait()
        for tile in range(bounds[chunk], bounds[chunk + 1]):
            lanes = pl.ds(tile * LANES, LANES)

            def feature(ref, index):
                here = turned(ref[lanes, :])
                taps = [short_ref[index, j : j + 1, lanes] for j in range(3)]
                return taps[0] * here + taps[1] * down(here) + taps[2] * down(here, 2)

            tail_ref[tile] = feature(key_in, 1) * feature(value_in, 2)
    for copy in rates:
        copy.wait()
    own_rate_out[...] = rates_in[...]


def prep_kernel(
    key_hbm,
    value_hbm,
    query_hbm,
    query2_hbm,
    key2_hbm,
    medium_hbm,
    short_ref,
    _,
    key_t,
    value_t,
    query_t,
    query2_t,
    key2_t,
    taps_t,
    rims_out,
    tail_out,
    key_in,
    value_in,
    query_in,
    query2_in,
    key2_in,
    medium_in,
    sems,
):
    chunks = sems.shape[1]
    rows = key_hbm.shape[0] // chunks
    fields = (
        (key_hbm, key_in, key_t),
        (value_hbm, value_in, value_t),
        (query_hbm, query_in, query_t),
        (query2_hbm, query2_in, query2_t),
        (key2_hbm, key2_in, key2_t),
        (medium_hbm, medium_in, taps_t),
    )
    copies = []
    for chunk in range(chunks):
        here = pl.ds(chunk * rows, rows)
        for place, (source, target, _) in enumerate(fields):
            copy = pltpu.make_async_copy(
                source.at[here, :], target.at[here, :], sems.at[place, chunk]
            )
            copy.start()
            copies.append(copy)
    for chunk in range(chunks):
        for place in range(len(fields)):
            copies[chunk * len(fields) + place].wait()
        for tile in range(chunk * rows // LANES, (chunk + 1) * rows // LANES):
            lanes = pl.ds(tile * LANES, LANES)
            rims_out[tile] = jnp.zeros((RIMS, LANES), F32)
            for place, (_, source, target) in enumerate(fields):
                if place < 5:
                    target[tile] = turned(source[lanes, :])
                    rims_out[tile, 2 * place : 2 * place + 2, :] = target[tile, T - 2 : T, :]
                else:
                    target[tile, 0:TAPS, :] = turned(source[lanes, :])
                    target[tile, TAPS:HEAD_ROWS, :] = jnp.zeros((HEAD_ROWS - TAPS, LANES), F32)

            def feature(ref, index, time):
                return sum(
                    short_ref[index, j : j + 1, lanes] * ref[tile, time - j : time - j + 1, :]
                    for j in range(3)
                )

            late = tile - (key_t.shape[0] - tail_out.shape[0])
            if late >= 0:
                gated = 1.0
                for ref, index in ((key_t, 1), (value_t, 2)):
                    here = ref[tile, T // 2 : T, :]
                    taps = [short_ref[index, j : j + 1, lanes] for j in range(3)]
                    gated = gated * (taps[0] * here + taps[1] * down(here) + taps[2] * down(here, 2))
                tail_out[late] = gated
            for k in range(2):
                rims_out[tile, 10 + k : 11 + k, :] = feature(query_t, 0, T - 2 + k)
            for k in range(3):
                rims_out[tile, 12 + k : 13 + k, :] = feature(key_t, 1, T // 2 - 1 + k) * feature(
                    value_t, 2, T // 2 - 1 + k
                )


def local_kernel(
    key_t,
    value_t,
    query_t,
    query2_t,
    key2_t,
    taps_t,
    short_ref,
    second_ref,
    rate_ref,
    amplitude_ref,
    skip_ref,
    first_ref,
    second_window_ref,
    spectrum_ref,
    first_back_ref,
    second_back_ref,
    taps_out,
    spectrum_out,
    medium_out,
    query_out,
    key2_out,
    leave_out,
    late_hbm,
    gated_t,
    medium_t,
    query_all,
    key2_all,
    by_segment,
    late,
    late_sem,
):

    tiles = key_t.shape[0]
    group = gated_t.shape[1] // LANES
    top = sublane((SEG, LANES)) == 0

    def slabs_of(ref, tile):
        head = [ref[tile, pl.ds(k, SEG, stride=HEAD), :] for k in range(HEAD)]
        main = [ref[tile, pl.ds(HEAD_ROWS + k, SEG, stride=MAIN), :] for k in range(MAIN)]
        return head, main

    def feature(ref, tile, taps_of, index, lanes):
        taps = [spread(taps_of[index, j : j + 1, lanes]) for j in range(3)]
        head, main = with_rims(*slabs_of(ref, tile))
        return fir3(head, taps) + fir3(main, taps)

    def body(step, _):
        for part in range(group):
            tile = step * group + part
            lanes = pl.ds(pl.multiple_of(tile * LANES, LANES), LANES)
            local = pl.ds(part * LANES, LANES)
            keys = feature(key_t, tile, short_ref, 1, lanes)
            values = feature(value_t, tile, short_ref, 2, lanes)
            for k in range(HEAD + MAIN):
                gated = keys[k] * values[k]
                if k < 2:
                    gated = jnp.where(top, 0.0, gated)
                gated_t[pl.ds(SEG * k, SEG), local] = gated
            for k, slab in enumerate(feature(query_t, tile, short_ref, 0, lanes)):
                query_all[part, pl.ds(SEG * k, SEG), :] = slab
            query_out[tile] = query_all[part, 0:HEAD_ROWS, :]
            for k, slab in enumerate(feature(key2_t, tile, second_ref, 1, lanes)):
                key2_all[part, pl.ds(SEG * k, SEG), :] = slab
            key2_out[tile] = key2_all[part, 0:HEAD_ROWS, :]
            for k, slab in enumerate(feature(query2_t, tile, second_ref, 0, lanes)):
                late[tile, pl.ds(SEG * k, SEG), :] = slab
            for k in range(HEAD):
                taps_out[tile, pl.ds(SEG * k, SEG), :] = taps_t[
                    tile, pl.ds(k, SEG, stride=HEAD), :
                ]

        filters = [taps_t[step * group + part, 0:TAPS, :] for part in range(group)]
        spectrum = matmul3(spectrum_ref[...], jnp.concatenate(filters, 1))
        high, low = halves(gated_t[...])
        first = matmul_halves(first_ref[...], high[:EARLY_ROWS], low[:EARLY_ROWS])
        second = matmul_halves(second_window_ref[...], high, low)
        medium_t[...] = matmul3(second_back_ref[...], spectral_product(second, spectrum))
        head = matmul3(first_back_ref[...], spectral_product(first, spectrum))
        medium_t[0:HEAD_ROWS, :] = medium_t[0:HEAD_ROWS, :] + head[0:HEAD_ROWS]

        for part in range(group):
            tile = step * group + part
            lanes = pl.ds(pl.multiple_of(tile * LANES, LANES), LANES)
            local = pl.ds(part * LANES, LANES)
            spectrum_out[tile] = spectrum[:, part * LANES : (part + 1) * LANES]
            medium_out[tile] = medium_t[0:HEAD_ROWS, local]
            taps = [spread(second_ref[2, j : j + 1, lanes]) for j in range(3)]
            firsts = [
                rows_of(medium_t, k, local) * query_all[part, pl.ds(SEG * k, SEG), :]
                for k in range(HEAD - 2, HEAD + MAIN)
            ]
            ends = [down(firsts[0]), down(firsts[1])]
            main = firsts[2:]
            main_all = [jnp.where(top, ends[k], down(main[MAIN - 2 + k])) for k in range(2)] + main
            values2 = fir3(main_all, taps)
            inputs = [
                key2_all[part, pl.ds(SEG * (HEAD + k), SEG), :] * values2[k] for k in range(MAIN)
            ]
            rates, gains = rate_ref[:, lanes], amplitude_ref[:, lanes]
            decays = jnp.exp(-rates)
            decay = [spread(decays[r : r + 1]) for r in range(MODES)]
            outs, ends = recurrence(
                inputs,
                decay,
                [spread(gains[r : r + 1]) for r in range(MODES)],
                spread(skip_ref[:, lanes]),
            )
            enters, leave_out[tile] = prefix(ends, rates, float(MAIN), by_segment.at[part])
            for i in range(SEG):
                by_segment[part, pl.ds(MODES * i, MODES), :] = enters[i]
            carry = [by_segment[part, pl.ds(r, SEG, stride=MODES), :] for r in range(MODES)]
            for k in range(MAIN):
                carry = [decay[r] * carry[r] for r in range(MODES)]
                late[tile, pl.ds(T + SEG * k, SEG), :] = sum(carry, outs[k])
            pltpu.make_async_copy(late.at[tile], late_hbm.at[tile], late_sem.at[tile]).start()
        return _

    lax.fori_loop(0, tiles // group, body, 0)
    for tile in range(tiles):
        pltpu.make_async_copy(late.at[tile], late_hbm.at[tile], late_sem.at[tile]).wait()


def join_kernel(
    base,
    halo_ref,
    rims_ref,
    spectrum_ref,
    medium_ref,
    taps_ref,
    query_ref,
    key2_ref,
    key_t,
    value_t,
    leave_main_ref,
    short_ref,
    second_ref,
    rate_ref,
    amplitude_ref,
    skip_ref,
    forward_ref,
    inverse_ref,
    *rest,
):
    tiles = halo_ref.shape[0]
    copies = []
    if base:
        state_ref, late_ref, state_out, late_hbm, medium_t, by_segment, late, late_sem = rest
        state_out[0:base] = state_ref[...]
        copies.append(
            pltpu.make_async_copy(late_ref, late_hbm.at[pl.ds(0, base)], late_sem.at[tiles])
        )
        copies[0].start()
    else:
        state_out, late, medium_t, by_segment = rest
    steps = medium_t.shape[0]
    top = sublane((SEG, LANES)) == 0

    def body(step):
        tile_list = list(range(base + step * tiles // steps, base + (step + 1) * tiles // steps))
        width = len(tile_list) * LANES
        halo = matmul3(
            forward_ref[...], jnp.concatenate([halo_ref[tile - base] for tile in tile_list], 1)
        )
        filters = jnp.concatenate([spectrum_ref[tile] for tile in tile_list], 1)
        medium_t[step, :, 0:width] = matmul3(inverse_ref[...], spectral_product(halo, filters))
        for part, tile in enumerate(tile_list):
            one(tile, medium_t.at[step], pl.ds(part * LANES, LANES), tile - base)

    def one(tile, medium_t, local, slot):
        lanes = pl.ds(tile * LANES, LANES)

        def rim(k):
            return rims_ref[tile, k : k + 1, :]

        def taps_of(ref, index):
            return [ref[index, j : j + 1, lanes] for j in range(3)]

        def early(ref, place, index):
            taps = taps_of(short_ref, index)
            zero, one = ref[tile, 0:1, :], ref[tile, 1:2, :]
            older, last = rim(2 * place), rim(2 * place + 1)
            return (
                taps[0] * zero + taps[1] * last + taps[2] * older,
                taps[0] * one + taps[1] * zero + taps[2] * last,
            )

        def mended(ref, place, taps):
            slabs = [ref[tile, pl.ds(SEG * k, SEG), :] for k in range(HEAD)]
            older, last = rim(2 * place), rim(2 * place + 1)
            slabs[0] = slabs[0] + jnp.where(top, spread(taps[1] * last + taps[2] * older), 0.0)
            slabs[1] = slabs[1] + jnp.where(top, spread(taps[2] * last), 0.0)
            return slabs

        def tap(j):
            row = SEG * (j % HEAD) + j // HEAD
            return taps_ref[tile, row : row + 1, :]

        keys, values = early(key_t, 0, 1), early(value_t, 1, 2)
        gated = [spread(keys[k] * values[k]) for k in range(2)]
        taps = [taps_ref[tile, pl.ds(SEG * k, SEG), :] for k in range(HEAD)]
        shifted = [jnp.where(top, 0.0, down(taps[HEAD - 1]))] + taps
        query = mended(query_ref, 2, taps_of(short_ref, 0))
        key2 = mended(key2_ref, 4, taps_of(second_ref, 1))
        mediums = [
            medium_ref[tile, pl.ds(SEG * k, SEG), :]
            + rows_of(medium_t, k, local)
            + taps[k] * gated[0]
            + shifted[k] * gated[1]
            for k in range(HEAD)
        ]
        far, farther, farthest = rim(14), rim(13), rim(12)
        mediums[0] = mediums[0] + jnp.where(top, spread(tap(127) * far), 0.0)
        older = medium_t[HEAD_ROWS : HEAD_ROWS + 1, local] + (
            tap(125) * far + tap(126) * farther + tap(127) * farthest
        )
        last = medium_t[HEAD_ROWS + 1 : HEAD_ROWS + 2, local] + (
            tap(126) * far + tap(127) * farther
        )
        firsts = [query[k] * mediums[k] for k in range(HEAD)]
        firsts_all, _ = with_rims(firsts, None, (spread(rim(10) * older), spread(rim(11) * last)))
        values2 = fir3(firsts_all, [spread(t) for t in taps_of(second_ref, 2)])
        inputs = [key2[k] * values2[k] for k in range(HEAD)]
        rates, gains = rate_ref[:, lanes], amplitude_ref[:, lanes]
        decays = jnp.exp(-rates)
        outs, ends = recurrence(
            inputs,
            [spread(decays[r : r + 1]) for r in range(MODES)],
            [spread(gains[r : r + 1]) for r in range(MODES)],
            spread(skip_ref[:, lanes]),
        )
        for k in range(HEAD):
            late[tile - base, pl.ds(SEG * k, SEG), :] = outs[k]
        enters, leave = prefix(ends, rates, float(HEAD), by_segment.at[slot])
        for i in range(SEG):
            late[tile - base, pl.ds(HEAD_ROWS + MODES * i, MODES), :] = enters[i]
        late[tile - base, pl.ds(HEAD_ROWS + MODES * SEG, MODES), :] = leave
        state_out[tile] = leave_main_ref[tile] + leave * jnp.exp(-float(MAIN_ROWS) * rates)
        if base:
            copy = pltpu.make_async_copy(
                late.at[tile - base], late_hbm.at[tile], late_sem.at[tile - base]
            )
            copy.start()
            copies.append(copy)

    for step in range(steps):
        body(step)
    for copy in copies:
        copy.wait()


def ring_kernel(states, rate_ref, out_ref):
    decay = jnp.exp(-float(T) * rate_ref[...])
    total = states[0]
    for k in range(1, states.shape[0]):
        total = decay * total + states[k]
    for k in range(out_ref.shape[0]):
        out_ref[k] = total


def scan_kernel(place_ref, states_hbm, rings_ref, rate_ref, out_ref, states, sem):
    copy = pltpu.make_async_copy(states_hbm, states, sem)
    copy.start()
    ring = place_ref[0] // RING
    rates = rate_ref[...]
    decay = jnp.exp(-float(T) * rates)
    around = jnp.exp(-float(T * RING) * rates)
    entering = jnp.zeros_like(rates)
    for k in range(rings_ref.shape[0] - 1):
        entering = jnp.where(k < ring, around * entering + rings_ref[k], entering)
    copy.wait()
    for k in range(states.shape[0]):
        out_ref[k] = entering
        entering = decay * entering + states[k]


def finish_kernel(
    state_ref,
    early_hbm,
    late_hbm,
    rims_ref,
    second_ref,
    rate_ref,
    gain_ref,
    mixed_out,
    squares_out,
    early,
    late,
    by_segment,
    squares_t,
    sems,
):
    tiles = early_hbm.shape[0]
    chunks = sems.shape[1]
    count = tiles // chunks
    copies = []
    for chunk in range(chunks):
        here = pl.ds(chunk * count, count)
        for place, (source, target) in enumerate(((early_hbm, early), (late_hbm, late))):
            copy = pltpu.make_async_copy(source.at[here], target.at[here], sems.at[place, chunk])
            copy.start()
            copies.append(copy)
    squares_t[...] = jnp.zeros_like(squares_t)
    top = sublane((SEG, LANES)) == 0

    def body(tile):
        lanes = pl.ds(tile * LANES, LANES)
        rates = rate_ref[:, lanes]
        decays = jnp.exp(-rates)
        taps = [second_ref[0, j : j + 1, lanes] for j in range(3)]
        older, last = rims_ref[tile, 6:7, :], rims_ref[tile, 7:8, :]
        mends = [spread(taps[1] * last + taps[2] * older), spread(taps[2] * last)]
        gain = spread(gain_ref[:, lanes])
        states = state_ref[tile]
        decay = [spread(decays[r : r + 1]) for r in range(MODES)]

        def half(length, entering, enters, own_ref, own_row, first_row):
            step = jnp.exp(-float(length) * rates)
            slot = 0 if first_row == 0 else 1
            for i in range(SEG):
                rows = pl.ds(MODES * i, MODES)
                by_segment[slot, rows, :] = enters[i] + entering if enters else entering
                entering = step * entering
            carry = [by_segment[slot, pl.ds(r, SEG, stride=MODES), :] for r in range(MODES)]
            for k in range(length):
                carry = [decay[r] * carry[r] for r in range(MODES)]
                total = own_ref[tile, pl.ds(own_row + SEG * k, SEG), :]
                for value in carry:
                    total = total + value
                rows = pl.ds(first_row + SEG * k, SEG)
                query = early[tile, rows, :]
                if first_row == 0 and k < 2:
                    query = query + jnp.where(top, mends[k], 0.0)
                mixed = query * total
                squares_t[rows, :] = squares_t[rows, :] + mixed * mixed
                mixed_out[tile, pl.ds(first_row + k, SEG, stride=length), :] = mixed * gain

        leave = late[tile, pl.ds(HEAD_ROWS + MODES * SEG, MODES), :]
        later = leave + states * jnp.exp(-float(HEAD_ROWS) * rates)
        enters = [late[tile, pl.ds(HEAD_ROWS + MODES * i, MODES), :] for i in range(SEG)]
        half(HEAD, states, enters, late, 0, 0)
        half(MAIN, later, None, early, T, HEAD_ROWS)

    for chunk in range(chunks):
        copies[2 * chunk].wait()
        copies[2 * chunk + 1].wait()
        for tile in range(chunk * count, (chunk + 1) * count):
            body(tile)
    sums = jnp.sum(squares_t[...], axis=1, keepdims=True)
    squares_t[...] = jnp.broadcast_to(sums, squares_t.shape)
    head = [squares_t[pl.ds(i, HEAD, stride=SEG), :] for i in range(SEG)]
    main = [squares_t[pl.ds(HEAD_ROWS + i, MAIN, stride=SEG), :] for i in range(SEG)]
    ordered = jnp.concatenate(head + main, 0)
    squares_out[...] = ordered.T[0:1, :]


def scale_kernel(divisor, mixed_ref, squares_ref, out_hbm, out_t, sems):
    scale = lax.rsqrt(squares_ref[...] / divisor + norm_eps)
    chunks = sems.shape[0]
    tiles = mixed_ref.shape[0] // chunks
    copies = []
    for chunk in range(chunks):
        for tile in range(chunk * tiles, (chunk + 1) * tiles):
            out_t[pl.ds(tile * LANES, LANES), :] = mixed_ref[tile].T * scale
        rows = pl.ds(chunk * tiles * LANES, tiles * LANES)
        copy = pltpu.make_async_copy(out_t.at[rows, :], out_hbm.at[rows, :], sems.at[chunk])
        copy.start()
        copies.append(copy)
    for copy in copies:
        copy.wait()


def from_behind(block):
    count = lax.axis_size("seq")
    return lax.ppermute(block, "seq", [(i, i + 1) for i in range(count - 1)])


def in_hbm(x):
    return pltpu.with_memory_space_constraint(x, pltpu.HBM)


def call(kernel, in_specs, out_specs, out_shape, scratch, flops, size, name):
    return pl.pallas_call(
        kernel,
        in_specs=in_specs,
        out_specs=out_specs,
        out_shape=out_shape,
        scratch_shapes=scratch,
        compiler_params=pltpu.CompilerParams(vmem_limit_bytes=LIMIT),
        cost_estimate=pl.CostEstimate(flops=flops, bytes_accessed=size, transcendentals=0),
        name=name,
    )


def exchange(rows, groups):
    return lax.all_to_all(
        rows, "seq", split_axis=0, concat_axis=0, axis_index_groups=groups, tiled=True
    )


def local(
    query_proj,
    key_proj,
    value_proj,
    second_query,
    second_key,
    short_filter,
    second_short,
    medium_filter,
    decay_rate,
    residue,
    skip_gain,
    norm_gain,
):
    channels = query_proj.shape[0]
    count = lax.axis_size("seq")
    tiles = channels // LANES
    group = min(8, tiles)
    chunks = min(4, tiles)
    second = max(1, tiles * 3 // 16)
    parts = (tiles - second, second)
    short_t = jnp.transpose(short_filter, (0, 2, 1))
    second_t = jnp.transpose(second_short, (0, 2, 1))
    rate_t = decay_rate.T
    amplitude = residue.T * jnp.sqrt(-jnp.expm1(-2.0 * rate_t))
    skip = skip_gain[None, :]
    gain = norm_gain[None, :]
    *windows, halo_forward, halo_inverse = tables()
    held = pl.BlockSpec(memory_space=pltpu.VMEM)
    outside = pl.BlockSpec(memory_space=pl.ANY)
    words = channels * T

    def struct(*shape):
        return jax.ShapeDtypeStruct(shape, F32)

    def hbm(*shape):
        return pltpu.HBM(shape, F32)

    fields = [
        in_hbm(x) for x in (key_proj, value_proj, query_proj, second_query, second_key, medium_filter)
    ]
    rings = count // RING
    share = tiles // RING
    ring_groups = [[ring * RING + k for k in range(RING)] for ring in range(rings)]
    across_groups = [[ring * RING + k for ring in range(rings)] for k in range(RING)]
    place = lax.axis_index("seq").astype(jnp.int32).reshape(1)
    tail, own_rate = call(
        tail_kernel,
        [pl.BlockSpec(memory_space=pltpu.SMEM)] + [outside] * 4,
        [held] * 2,
        [struct(parts[0], TAPS, LANES), struct(share, MODES, LANES)],
        [pltpu.VMEM((parts[0] * LANES, LANES), F32)] * 2
        + [pltpu.VMEM((3, 3, channels), F32), pltpu.VMEM((share, MODES, LANES), F32)]
        + [pltpu.SemaphoreType.DMA((2,))] * 2
        + [pltpu.SemaphoreType.DMA, pltpu.SemaphoreType.DMA((share,))],
        words * 8,
        words * 6,
        "tail",
    )(place, fields[0], fields[1], in_hbm(short_t), in_hbm(rate_t))
    halo = from_behind(tail)

    *turned_fields, taps_t, rims, tail_two = call(
        prep_kernel,
        [outside] * 6 + [held] * 2,
        [held] * 8,
        [struct(tiles, T, LANES)] * 5
        + [struct(tiles, HEAD_ROWS, LANES), struct(tiles, RIMS, LANES)]
        + [struct(parts[1], TAPS, LANES)],
        [pltpu.VMEM((channels, T), F32)] * 5
        + [pltpu.VMEM((channels, TAPS), F32), pltpu.SemaphoreType.DMA((6, chunks))],
        words * 20,
        words * 40,
        "prep",
    )(*fields, short_t, own_rate)
    border = from_behind(rims)
    halo_two = from_behind(tail_two)

    early_rows = T + MAIN_ROWS
    (
        taps,
        tap_spectrum,
        medium,
        query,
        key2,
        leave_main,
        early,
    ) = call(
        local_kernel,
        [held] * (11 + len(windows)),
        [held] * 6 + [outside],
        [
            struct(tiles, HEAD_ROWS, LANES),
            struct(tiles, 384, LANES),
            struct(tiles, HEAD_ROWS, LANES),
            struct(tiles, HEAD_ROWS, LANES),
            struct(tiles, HEAD_ROWS, LANES),
            struct(tiles, MODES, LANES),
            hbm(tiles, early_rows, LANES),
        ],
        [pltpu.VMEM((T, group * LANES), F32)] * 2
        + [pltpu.VMEM((group, T, LANES), F32)] * 2
        + [pltpu.VMEM((group, MODES * SEG, LANES), F32)]
        + [pltpu.VMEM((tiles, early_rows, LANES), F32), pltpu.SemaphoreType.DMA((tiles,))],
        words * 8000,
        words * 60,
        "local",
    )(
        *turned_fields,
        taps_t,
        short_t,
        second_t,
        rate_t,
        amplitude,
        skip,
        *windows,
    )

    late_rows = HEAD_ROWS + MODES * SEG + MODES
    joined = ()
    for base, part in zip((0, parts[0]), (halo, halo_two)):
        here = part.shape[0]
        join_steps = min(here, 1 if base else 2)
        late_shape = (base + here, late_rows, LANES)
        scratch = [
            pltpu.VMEM((join_steps, HEAD_ROWS + 8, -(-here // join_steps) * LANES), F32),
            pltpu.VMEM((here, MODES * SEG, LANES), F32),
        ]
        if base:
            scratch.append(pltpu.VMEM((here, late_rows, LANES), F32))
            scratch.append(pltpu.SemaphoreType.DMA((here + 1,)))
        joined = call(
            functools.partial(join_kernel, base),
            [held] * (17 + len(joined)),
            [held, outside if base else held],
            [struct(base + here, MODES, LANES), (hbm if base else struct)(*late_shape)],
            scratch,
            here * 500 * T * LANES,
            here * 20 * T * LANES,
            "join",
        )(
            part,
            border,
            tap_spectrum,
            medium,
            taps,
            query,
            key2,
            turned_fields[0],
            turned_fields[1],
            leave_main,
            short_t,
            second_t,
            rate_t,
            amplitude,
            skip,
            halo_forward,
            halo_inverse,
            *joined,
        )
    state, late = joined

    share_shape = (RING, share, MODES, LANES)
    ring_states = exchange(state.reshape(share_shape), ring_groups)
    totals = call(
        ring_kernel,
        [held, held],
        held,
        struct(rings, share, MODES, LANES),
        [],
        count * LANES * 30,
        count * LANES * 8,
        "ring",
    )(ring_states, own_rate)
    scanned = call(
        scan_kernel,
        [pl.BlockSpec(memory_space=pltpu.SMEM), outside, held, held],
        held,
        struct(*share_shape),
        [pltpu.VMEM(share_shape, F32), pltpu.SemaphoreType.DMA],
        count * LANES * 30,
        count * LANES * 8,
        "scan",
    )(place, in_hbm(ring_states), exchange(totals, across_groups), own_rate)
    incoming = exchange(scanned, ring_groups).reshape(tiles, MODES, LANES)

    mixed, squares = call(
        finish_kernel,
        [held] + [outside] * 2 + [held] * 4,
        [held] * 2,
        [struct(tiles, T, LANES), struct(1, T)],
        [
            pltpu.VMEM((tiles, early_rows, LANES), F32),
            pltpu.VMEM((tiles, late_rows, LANES), F32),
            pltpu.VMEM((2, MODES * SEG, LANES), F32),
            pltpu.VMEM((T, LANES), F32),
            pltpu.SemaphoreType.DMA((2, 2 * chunks)),
        ],
        words * 40,
        words * 16,
        "finish",
    )(incoming, in_hbm(early), in_hbm(late), border, second_t, rate_t, gain)
    total = lax.psum(squares, "chan")
    return call(
        functools.partial(scale_kernel, float(channels * lax.axis_size("chan"))),
        [held, held],
        outside,
        struct(channels, T),
        [pltpu.VMEM((channels, T), F32), pltpu.SemaphoreType.DMA((chunks,))],
        words,
        words * 8,
        "scale",
    )(mixed, total)


def solution(mesh):
    return jax.shard_map(
        local,
        mesh=mesh,
        in_specs=(
            P("chan", "seq"),
            P("chan", "seq"),
            P("chan", "seq"),
            P("chan", "seq"),
            P("chan", "seq"),
            P(None, "chan", None),
            P(None, "chan", None),
            P("chan", None),
            P("chan", None),
            P("chan", None),
            P("chan"),
            P("chan"),
        ),
        out_specs=P("chan", "seq"),
        check_vma=False,
    )
```

```python
import functools

import jax
import jax.numpy as jnp
import ml_dtypes
import numpy as np
from jax import lax
from jax.experimental import pallas as pl
from jax.experimental.pallas import tpu as pltpu
from jax.sharding import PartitionSpec as P

norm_eps = 1e-06

T = 256
TAPS = 128
MODES = 8
LANES = 128
SEG = 8
HEAD = 17
MAIN = 15
HEAD_ROWS = HEAD * SEG
MAIN_ROWS = MAIN * SEG
EARLY_ROWS = 144
RIMS = 13
RING = 8
LIMIT = 24 * 1024 * 1024

F32 = jnp.float32
BF16 = jnp.bfloat16


def row_times():
    head = [HEAD * i + k for k in range(HEAD) for i in range(SEG)]
    main = [HEAD_ROWS + MAIN * i + k for k in range(MAIN) for i in range(SEG)]
    return np.array(head + main)


def packed_forward(slots):
    k = np.arange(128)[:, None]
    angle = 2.0 * np.pi * k * np.asarray(slots)[None, :] / 256.0
    imag = -np.sin(angle)
    imag[0] = np.cos(np.pi * np.asarray(slots))
    return np.concatenate([np.cos(angle), imag], 0)


def packed_inverse(slots):
    k = np.arange(128)[None, :]
    angle = 2.0 * np.pi * k * np.asarray(slots)[:, None] / 256.0
    real = 2.0 * np.cos(angle)
    real[:, 0] = 1.0
    imag = -2.0 * np.sin(angle)
    imag[:, 0] = np.cos(np.pi * np.asarray(slots))
    return np.concatenate([real, imag], 1) / 256.0


def three_pass(matrix):
    high = matrix.astype(ml_dtypes.bfloat16)
    low = (matrix - high.astype(np.float64)).astype(ml_dtypes.bfloat16)
    return np.concatenate([high, low, high], 1)


def tables():
    times = row_times()
    early = times[:EARLY_ROWS]
    first = packed_forward(early + 128) * (early < 128)[None, :]
    second = packed_forward(times)
    taps = packed_forward(np.arange(TAPS))
    real, imag = taps[:128], taps[128:].copy()
    cross = real.copy()
    cross[0] = imag[0]
    imag[0] = 0.0
    spectrum = np.concatenate([real, imag, cross], 0)
    first_back = packed_inverse(early + 128) * (early < 128)[:, None]
    second_back = packed_inverse(times) * (times >= 128)[:, None]
    halo = packed_forward(np.arange(128))
    halo[:, :2] = 0.0
    head_times = np.concatenate([times[:HEAD_ROWS], [-2, -1], np.full(6, 255)])
    halo_back = packed_inverse(head_times + 128) * (head_times < 128)[:, None]
    matrices = (first, second, spectrum, first_back, second_back, halo, halo_back)
    return [three_pass(m) for m in matrices]


def halves(x):
    high = x.astype(BF16)
    low = (x - high.astype(F32)).astype(BF16)
    return high, low


def matmul_halves(matrix, high, low):
    stacked = jnp.concatenate([high, high, low], 0)
    return jnp.dot(matrix, stacked, preferred_element_type=F32)


def matmul3(matrix, x):
    return matmul_halves(matrix, *halves(x))


def spectral_product(x, taps):
    real, imag = x[:128], x[128:]
    tap_real, tap_imag, tap_cross = taps[:128], taps[128:256], taps[256:]
    return jnp.concatenate(
        [real * tap_real - imag * tap_imag, real * tap_imag + imag * tap_cross], 0
    )


def sublane(shape):
    return lax.broadcasted_iota(jnp.int32, shape, 0)


def down(x, distance=1):
    return pltpu.roll(x, distance, axis=0)


def fir3(slabs, taps):
    return [
        taps[0] * slabs[k + 2] + taps[1] * slabs[k + 1] + taps[2] * slabs[k]
        for k in range(len(slabs) - 2)
    ]


def with_rims(head, main, rims=None):
    top = sublane(head[0].shape) == 0
    zero = jnp.zeros_like(head[0])
    before = (zero, zero) if rims is None else rims
    ends = [down(head[HEAD - 2]), down(head[HEAD - 1])]
    head_all = [jnp.where(top, before[k], ends[k]) for k in range(2)] + head
    if main is None:
        return head_all, None
    main_all = [jnp.where(top, ends[k], down(main[MAIN - 2 + k])) for k in range(2)] + main
    return head_all, main_all


def rows_of(ref, k, lanes):
    return ref[pl.ds(SEG * k, SEG), lanes]


def spread(row):
    return jnp.broadcast_to(row, (SEG, row.shape[1]))


def recurrence(inputs, decays, gains, skip):
    states = [gains[r] * inputs[0] for r in range(MODES)]
    outs = []
    for k, value in enumerate(inputs):
        if k:
            states = [decays[r] * states[r] + gains[r] * value for r in range(MODES)]
        total = skip * value
        for state in states:
            total = total + state
        outs.append(total)
    return outs, states


def prefix(ends, rates, step, by_segment):
    for r in range(MODES):
        by_segment[pl.ds(r, SEG, stride=MODES), :] = ends[r]
    power = jnp.exp(-step * rates)
    enters = [jnp.zeros_like(rates)]
    for i in range(SEG):
        enters.append(power * enters[i] + by_segment[pl.ds(MODES * i, MODES), :])
    return enters[:SEG], enters[SEG]


def turned(block):
    return block.T


def tail_kernel(
    place_ref,
    key_hbm,
    value_hbm,
    short_hbm,
    rate_hbm,
    tail_ref,
    own_rate_out,
    key_in,
    value_in,
    short_ref,
    rates_in,
    key_sem,
    value_sem,
    short_sem,
    rate_sem,
):
    chunks = key_sem.shape[0]
    tiles = tail_ref.shape[0]
    bounds = [chunk * tiles // chunks for chunk in range(chunks + 1)]
    copies = []
    filters = pltpu.make_async_copy(short_hbm, short_ref, short_sem)
    filters.start()
    index = place_ref[0]
    share = rates_in.shape[0]
    first = lax.rem(index, RING) * (share * LANES)
    rates = []
    for part in range(share):
        mine = pl.ds(pl.multiple_of(first + part * LANES, LANES), LANES)
        copy = pltpu.make_async_copy(rate_hbm.at[:, mine], rates_in.at[part], rate_sem.at[part])
        copy.start()
        rates.append(copy)
    for chunk in range(chunks):
        here = pl.ds(bounds[chunk] * LANES, (bounds[chunk + 1] - bounds[chunk]) * LANES)
        for source, target, sem in (
            (key_hbm, key_in, key_sem),
            (value_hbm, value_in, value_sem),
        ):
            copy = pltpu.make_async_copy(
                source.at[here, pl.ds(LANES, LANES)], target.at[here, :], sem.at[chunk]
            )
            copy.start()
            copies.append(copy)
    filters.wait()
    for chunk in range(chunks):
        copies[2 * chunk].wait()
        copies[2 * chunk + 1].wait()
        for tile in range(bounds[chunk], bounds[chunk + 1]):
            lanes = pl.ds(tile * LANES, LANES)

            def feature(ref, index):
                here = turned(ref[lanes, :])
                taps = [short_ref[index, j : j + 1, lanes] for j in range(3)]
                return taps[0] * here + taps[1] * down(here) + taps[2] * down(here, 2)

            tail_ref[tile] = feature(key_in, 1) * feature(value_in, 2)
            tail_ref[tile, 0:2, :] = turned(key_in[lanes, :])[LANES - 2 :]
    for copy in rates:
        copy.wait()
    own_rate_out[...] = rates_in[...]


def prep_kernel(
    key_hbm,
    value_hbm,
    query_hbm,
    query2_hbm,
    key2_hbm,
    medium_hbm,
    short_ref,
    _,
    key_t,
    value_t,
    query_t,
    query2_t,
    key2_t,
    taps_t,
    rims_out,
    tail_out,
    key_in,
    value_in,
    query_in,
    query2_in,
    key2_in,
    medium_in,
    sems,
):
    chunks = sems.shape[1]
    rows = key_hbm.shape[0] // chunks
    fields = (
        (key_hbm, key_in, key_t),
        (value_hbm, value_in, value_t),
        (query_hbm, query_in, query_t),
        (query2_hbm, query2_in, query2_t),
        (key2_hbm, key2_in, key2_t),
        (medium_hbm, medium_in, taps_t),
    )
    copies = []
    for chunk in range(chunks):
        here = pl.ds(chunk * rows, rows)
        for place, (source, target, _) in enumerate(fields):
            copy = pltpu.make_async_copy(
                source.at[here, :], target.at[here, :], sems.at[place, chunk]
            )
            copy.start()
            copies.append(copy)
    for chunk in range(chunks):
        for place in range(len(fields)):
            copies[chunk * len(fields) + place].wait()
        for tile in range(chunk * rows // LANES, (chunk + 1) * rows // LANES):
            lanes = pl.ds(tile * LANES, LANES)
            for place, (_, source, target) in enumerate(fields):
                if place < 5:
                    target[tile] = turned(source[lanes, :])
                    for k in range(2 if place else 0):
                        rims_out[2 * place - 2 + k, tile : tile + 1, :] = target[
                            tile, T - 2 + k : T - 1 + k, :
                        ]
                else:
                    target[tile, 0:TAPS, :] = turned(source[lanes, :])
                    target[tile, TAPS:HEAD_ROWS, :] = jnp.zeros((HEAD_ROWS - TAPS, LANES), F32)

            def feature(ref, index, time):
                return sum(
                    short_ref[index, j : j + 1, lanes] * ref[tile, time - j : time - j + 1, :]
                    for j in range(3)
                )

            late = tile - (key_t.shape[0] - tail_out.shape[0])
            if late >= 0:
                gated = 1.0
                for ref, index in ((key_t, 1), (value_t, 2)):
                    here = ref[tile, T // 2 : T, :]
                    taps = [short_ref[index, j : j + 1, lanes] for j in range(3)]
                    gated = gated * (taps[0] * here + taps[1] * down(here) + taps[2] * down(here, 2))
                tail_out[late] = gated
                tail_out[late, 0:2, :] = key_t[tile, T - 2 : T, :]
            for k in range(2):
                rims_out[8 + k, tile : tile + 1, :] = feature(query_t, 0, T - 2 + k)
            for k in range(3):
                rims_out[10 + k, tile : tile + 1, :] = feature(key_t, 1, T // 2 - 1 + k) * feature(
                    value_t, 2, T // 2 - 1 + k
                )


def local_kernel(
    key_t,
    value_t,
    query_t,
    query2_t,
    key2_t,
    taps_t,
    short_ref,
    second_ref,
    rate_ref,
    amplitude_ref,
    skip_ref,
    first_ref,
    second_window_ref,
    spectrum_ref,
    first_back_ref,
    second_back_ref,
    taps_out,
    spectrum_out,
    medium_out,
    query_out,
    key2_out,
    leave_out,
    late_hbm,
    gated_t,
    medium_t,
    query_all,
    key2_all,
    by_segment,
    late,
    late_sem,
):

    tiles = key_t.shape[0]
    group = gated_t.shape[1] // LANES
    top = sublane((SEG, LANES)) == 0

    def slabs_of(ref, tile):
        head = [ref[tile, pl.ds(k, SEG, stride=HEAD), :] for k in range(HEAD)]
        main = [ref[tile, pl.ds(HEAD_ROWS + k, SEG, stride=MAIN), :] for k in range(MAIN)]
        return head, main

    def feature(ref, tile, taps_of, index, lanes):
        taps = [spread(taps_of[index, j : j + 1, lanes]) for j in range(3)]
        head, main = with_rims(*slabs_of(ref, tile))
        return fir3(head, taps) + fir3(main, taps)

    def body(step, _):
        for part in range(group):
            tile = step * group + part
            lanes = pl.ds(pl.multiple_of(tile * LANES, LANES), LANES)
            local = pl.ds(part * LANES, LANES)
            keys = feature(key_t, tile, short_ref, 1, lanes)
            values = feature(value_t, tile, short_ref, 2, lanes)
            for k in range(HEAD + MAIN):
                gated = keys[k] * values[k]
                if k < 2:
                    gated = jnp.where(top, 0.0, gated)
                gated_t[pl.ds(SEG * k, SEG), local] = gated
            for k, slab in enumerate(feature(query_t, tile, short_ref, 0, lanes)):
                query_all[part, pl.ds(SEG * k, SEG), :] = slab
            query_out[tile] = query_all[part, 0:HEAD_ROWS, :]
            for k, slab in enumerate(feature(key2_t, tile, second_ref, 1, lanes)):
                key2_all[part, pl.ds(SEG * k, SEG), :] = slab
            key2_out[tile] = key2_all[part, 0:HEAD_ROWS, :]
            for k, slab in enumerate(feature(query2_t, tile, second_ref, 0, lanes)):
                late[tile, pl.ds(SEG * k, SEG), :] = slab
            for k in range(HEAD):
                taps_out[tile, pl.ds(SEG * k, SEG), :] = taps_t[
                    tile, pl.ds(k, SEG, stride=HEAD), :
                ]

        filters = [taps_t[step * group + part, 0:TAPS, :] for part in range(group)]
        spectrum = matmul3(spectrum_ref[...], jnp.concatenate(filters, 1))
        high, low = halves(gated_t[...])
        first = matmul_halves(first_ref[...], high[:EARLY_ROWS], low[:EARLY_ROWS])
        second = matmul_halves(second_window_ref[...], high, low)
        medium_t[...] = matmul3(second_back_ref[...], spectral_product(second, spectrum))
        head = matmul3(first_back_ref[...], spectral_product(first, spectrum))
        medium_t[0:HEAD_ROWS, :] = medium_t[0:HEAD_ROWS, :] + head[0:HEAD_ROWS]

        for part in range(group):
            tile = step * group + part
            lanes = pl.ds(pl.multiple_of(tile * LANES, LANES), LANES)
            local = pl.ds(part * LANES, LANES)
            spectrum_out[tile] = spectrum[:, part * LANES : (part + 1) * LANES]
            medium_out[tile] = medium_t[0:HEAD_ROWS, local]
            taps = [spread(second_ref[2, j : j + 1, lanes]) for j in range(3)]
            firsts = [
                rows_of(medium_t, k, local) * query_all[part, pl.ds(SEG * k, SEG), :]
                for k in range(HEAD - 2, HEAD + MAIN)
            ]
            ends = [down(firsts[0]), down(firsts[1])]
            main = firsts[2:]
            main_all = [jnp.where(top, ends[k], down(main[MAIN - 2 + k])) for k in range(2)] + main
            values2 = fir3(main_all, taps)
            inputs = [
                key2_all[part, pl.ds(SEG * (HEAD + k), SEG), :] * values2[k] for k in range(MAIN)
            ]
            rates, gains = rate_ref[:, lanes], amplitude_ref[:, lanes]
            decays = jnp.exp(-rates)
            decay = [spread(decays[r : r + 1]) for r in range(MODES)]
            outs, ends = recurrence(
                inputs,
                decay,
                [spread(gains[r : r + 1]) for r in range(MODES)],
                spread(skip_ref[:, lanes]),
            )
            enters, leave_out[tile] = prefix(ends, rates, float(MAIN), by_segment.at[part])
            for i in range(SEG):
                by_segment[part, pl.ds(MODES * i, MODES), :] = enters[i]
            carry = [by_segment[part, pl.ds(r, SEG, stride=MODES), :] for r in range(MODES)]
            for k in range(MAIN):
                carry = [decay[r] * carry[r] for r in range(MODES)]
                late[tile, pl.ds(T + SEG * k, SEG), :] = sum(carry, outs[k])
            pltpu.make_async_copy(late.at[tile], late_hbm.at[tile], late_sem.at[tile]).start()
        return _

    lax.fori_loop(0, tiles // group, body, 0)
    for tile in range(tiles):
        pltpu.make_async_copy(late.at[tile], late_hbm.at[tile], late_sem.at[tile]).wait()


def join_kernel(
    base,
    halo_ref,
    rims_ref,
    spectrum_ref,
    medium_ref,
    taps_ref,
    query_ref,
    key2_ref,
    key_t,
    value_t,
    leave_main_ref,
    short_ref,
    second_ref,
    rate_ref,
    amplitude_ref,
    skip_ref,
    forward_ref,
    inverse_ref,
    *rest,
):
    tiles = halo_ref.shape[0]
    copies = []
    if base:
        state_ref, late_ref, state_out, late_hbm, medium_t, by_segment, late, late_sem = rest
        state_out[0:base] = state_ref[...]
        copies.append(
            pltpu.make_async_copy(late_ref, late_hbm.at[pl.ds(0, base)], late_sem.at[tiles])
        )
        copies[0].start()
    else:
        state_out, late, medium_t, by_segment = rest
    steps = medium_t.shape[0]
    top = sublane((SEG, LANES)) == 0

    def body(step):
        tile_list = list(range(base + step * tiles // steps, base + (step + 1) * tiles // steps))
        width = len(tile_list) * LANES
        halo = matmul3(
            forward_ref[...], jnp.concatenate([halo_ref[tile - base] for tile in tile_list], 1)
        )
        filters = jnp.concatenate([spectrum_ref[tile] for tile in tile_list], 1)
        medium_t[step, :, 0:width] = matmul3(inverse_ref[...], spectral_product(halo, filters))
        for part, tile in enumerate(tile_list):
            one(tile, medium_t.at[step], pl.ds(part * LANES, LANES), tile - base)

    def one(tile, medium_t, local, slot):
        lanes = pl.ds(tile * LANES, LANES)

        def rim(k):
            if k < 2:
                return halo_ref[tile - base, k : k + 1, :]
            return rims_ref[k - 2, tile : tile + 1, :]

        def taps_of(ref, index):
            return [ref[index, j : j + 1, lanes] for j in range(3)]

        def early(ref, place, index):
            taps = taps_of(short_ref, index)
            zero, one = ref[tile, 0:1, :], ref[tile, 1:2, :]
            older, last = rim(2 * place), rim(2 * place + 1)
            return (
                taps[0] * zero + taps[1] * last + taps[2] * older,
                taps[0] * one + taps[1] * zero + taps[2] * last,
            )

        def mended(ref, place, taps):
            slabs = [ref[tile, pl.ds(SEG * k, SEG), :] for k in range(HEAD)]
            older, last = rim(2 * place), rim(2 * place + 1)
            slabs[0] = slabs[0] + jnp.where(top, spread(taps[1] * last + taps[2] * older), 0.0)
            slabs[1] = slabs[1] + jnp.where(top, spread(taps[2] * last), 0.0)
            return slabs

        def tap(j):
            row = SEG * (j % HEAD) + j // HEAD
            return taps_ref[tile, row : row + 1, :]

        keys, values = early(key_t, 0, 1), early(value_t, 1, 2)
        gated = [spread(keys[k] * values[k]) for k in range(2)]
        taps = [taps_ref[tile, pl.ds(SEG * k, SEG), :] for k in range(HEAD)]
        shifted = [jnp.where(top, 0.0, down(taps[HEAD - 1]))] + taps
        query = mended(query_ref, 2, taps_of(short_ref, 0))
        key2 = mended(key2_ref, 4, taps_of(second_ref, 1))
        mediums = [
            medium_ref[tile, pl.ds(SEG * k, SEG), :]
            + rows_of(medium_t, k, local)
            + taps[k] * gated[0]
            + shifted[k] * gated[1]
            for k in range(HEAD)
        ]
        far, farther, farthest = rim(14), rim(13), rim(12)
        mediums[0] = mediums[0] + jnp.where(top, spread(tap(127) * far), 0.0)
        older = medium_t[HEAD_ROWS : HEAD_ROWS + 1, local] + (
            tap(125) * far + tap(126) * farther + tap(127) * farthest
        )
        last = medium_t[HEAD_ROWS + 1 : HEAD_ROWS + 2, local] + (
            tap(126) * far + tap(127) * farther
        )
        firsts = [query[k] * mediums[k] for k in range(HEAD)]
        firsts_all, _ = with_rims(firsts, None, (spread(rim(10) * older), spread(rim(11) * last)))
        values2 = fir3(firsts_all, [spread(t) for t in taps_of(second_ref, 2)])
        inputs = [key2[k] * values2[k] for k in range(HEAD)]
        rates, gains = rate_ref[:, lanes], amplitude_ref[:, lanes]
        decays = jnp.exp(-rates)
        outs, ends = recurrence(
            inputs,
            [spread(decays[r : r + 1]) for r in range(MODES)],
            [spread(gains[r : r + 1]) for r in range(MODES)],
            spread(skip_ref[:, lanes]),
        )
        for k in range(HEAD):
            late[tile - base, pl.ds(SEG * k, SEG), :] = outs[k]
        enters, leave = prefix(ends, rates, float(HEAD), by_segment.at[slot])
        for i in range(SEG):
            late[tile - base, pl.ds(HEAD_ROWS + MODES * i, MODES), :] = enters[i]
        late[tile - base, pl.ds(HEAD_ROWS + MODES * SEG, MODES), :] = leave
        state_out[tile] = leave_main_ref[tile] + leave * jnp.exp(-float(MAIN_ROWS) * rates)
        if base:
            copy = pltpu.make_async_copy(
                late.at[tile - base], late_hbm.at[tile], late_sem.at[tile - base]
            )
            copy.start()
            copies.append(copy)

    for step in range(steps):
        body(step)
    for copy in copies:
        copy.wait()


def ring_kernel(states, rate_ref, out_ref):
    decay = jnp.exp(-float(T) * rate_ref[...])
    total = states[0]
    for k in range(1, states.shape[0]):
        total = decay * total + states[k]
    for k in range(out_ref.shape[0]):
        out_ref[k] = total


def scan_kernel(place_ref, states_hbm, rings_ref, rate_ref, out_ref, states, sem):
    copy = pltpu.make_async_copy(states_hbm, states, sem)
    copy.start()
    ring = place_ref[0] // RING
    rates = rate_ref[...]
    decay = jnp.exp(-float(T) * rates)
    around = jnp.exp(-float(T * RING) * rates)
    entering = jnp.zeros_like(rates)
    for k in range(rings_ref.shape[0] - 1):
        entering = jnp.where(k < ring, around * entering + rings_ref[k], entering)
    copy.wait()
    for k in range(states.shape[0]):
        out_ref[k] = entering
        entering = decay * entering + states[k]


def finish_kernel(
    state_ref,
    early_hbm,
    late_hbm,
    rims_ref,
    second_ref,
    rate_ref,
    gain_ref,
    mixed_out,
    squares_out,
    early,
    late,
    by_segment,
    squares_t,
    sems,
):
    tiles = early_hbm.shape[0]
    chunks = sems.shape[1]
    count = tiles // chunks
    copies = []
    for chunk in range(chunks):
        here = pl.ds(chunk * count, count)
        for place, (source, target) in enumerate(((early_hbm, early), (late_hbm, late))):
            copy = pltpu.make_async_copy(source.at[here], target.at[here], sems.at[place, chunk])
            copy.start()
            copies.append(copy)
    squares_t[...] = jnp.zeros_like(squares_t)
    top = sublane((SEG, LANES)) == 0

    def body(tile):
        lanes = pl.ds(tile * LANES, LANES)
        rates = rate_ref[:, lanes]
        decays = jnp.exp(-rates)
        taps = [second_ref[0, j : j + 1, lanes] for j in range(3)]
        older, last = rims_ref[4, tile : tile + 1, :], rims_ref[5, tile : tile + 1, :]
        mends = [spread(taps[1] * last + taps[2] * older), spread(taps[2] * last)]
        gain = spread(gain_ref[:, lanes])
        states = state_ref[tile]
        decay = [spread(decays[r : r + 1]) for r in range(MODES)]

        def half(length, entering, enters, own_ref, own_row, first_row):
            step = jnp.exp(-float(length) * rates)
            slot = 0 if first_row == 0 else 1
            for i in range(SEG):
                rows = pl.ds(MODES * i, MODES)
                by_segment[slot, rows, :] = enters[i] + entering if enters else entering
                entering = step * entering
            carry = [by_segment[slot, pl.ds(r, SEG, stride=MODES), :] for r in range(MODES)]
            for k in range(length):
                carry = [decay[r] * carry[r] for r in range(MODES)]
                total = own_ref[tile, pl.ds(own_row + SEG * k, SEG), :]
                for value in carry:
                    total = total + value
                rows = pl.ds(first_row + SEG * k, SEG)
                query = early[tile, rows, :]
                if first_row == 0 and k < 2:
                    query = query + jnp.where(top, mends[k], 0.0)
                mixed = query * total
                squares_t[rows, :] = squares_t[rows, :] + mixed * mixed
                mixed_out[tile, pl.ds(first_row + k, SEG, stride=length), :] = mixed * gain

        leave = late[tile, pl.ds(HEAD_ROWS + MODES * SEG, MODES), :]
        later = leave + states * jnp.exp(-float(HEAD_ROWS) * rates)
        enters = [late[tile, pl.ds(HEAD_ROWS + MODES * i, MODES), :] for i in range(SEG)]
        half(HEAD, states, enters, late, 0, 0)
        half(MAIN, later, None, early, T, HEAD_ROWS)

    for chunk in range(chunks):
        copies[2 * chunk].wait()
        copies[2 * chunk + 1].wait()
        for tile in range(chunk * count, (chunk + 1) * count):
            body(tile)
    sums = jnp.sum(squares_t[...], axis=1, keepdims=True)
    squares_t[...] = jnp.broadcast_to(sums, squares_t.shape)
    head = [squares_t[pl.ds(i, HEAD, stride=SEG), :] for i in range(SEG)]
    main = [squares_t[pl.ds(HEAD_ROWS + i, MAIN, stride=SEG), :] for i in range(SEG)]
    ordered = jnp.concatenate(head + main, 0)
    squares_out[...] = ordered.T[0:1, :]


def scale_kernel(divisor, mixed_ref, squares_ref, out_hbm, out_t, sems):
    scale = lax.rsqrt(squares_ref[...] / divisor + norm_eps)
    chunks = sems.shape[0]
    tiles = mixed_ref.shape[0] // chunks
    copies = []
    for chunk in range(chunks):
        for tile in range(chunk * tiles, (chunk + 1) * tiles):
            out_t[pl.ds(tile * LANES, LANES), :] = mixed_ref[tile].T * scale
        rows = pl.ds(chunk * tiles * LANES, tiles * LANES)
        copy = pltpu.make_async_copy(out_t.at[rows, :], out_hbm.at[rows, :], sems.at[chunk])
        copy.start()
        copies.append(copy)
    for copy in copies:
        copy.wait()


def from_behind(block):
    count = lax.axis_size("seq")
    return lax.ppermute(block, "seq", [(i, i + 1) for i in range(count - 1)])


def in_hbm(x):
    return pltpu.with_memory_space_constraint(x, pltpu.HBM)


def call(kernel, in_specs, out_specs, out_shape, scratch, flops, size, name):
    return pl.pallas_call(
        kernel,
        in_specs=in_specs,
        out_specs=out_specs,
        out_shape=out_shape,
        scratch_shapes=scratch,
        compiler_params=pltpu.CompilerParams(vmem_limit_bytes=LIMIT),
        cost_estimate=pl.CostEstimate(flops=flops, bytes_accessed=size, transcendentals=0),
        name=name,
    )


def exchange(rows, groups):
    return lax.all_to_all(
        rows, "seq", split_axis=0, concat_axis=0, axis_index_groups=groups, tiled=True
    )


def local(
    query_proj,
    key_proj,
    value_proj,
    second_query,
    second_key,
    short_filter,
    second_short,
    medium_filter,
    decay_rate,
    residue,
    skip_gain,
    norm_gain,
):
    channels = query_proj.shape[0]
    count = lax.axis_size("seq")
    tiles = channels // LANES
    group = min(8, tiles)
    chunks = min(4, tiles)
    second = max(1, tiles * 3 // 16)
    parts = (tiles - second, second)
    short_t = jnp.transpose(short_filter, (0, 2, 1))
    second_t = jnp.transpose(second_short, (0, 2, 1))
    rate_t = decay_rate.T
    amplitude = residue.T * jnp.sqrt(-jnp.expm1(-2.0 * rate_t))
    skip = skip_gain[None, :]
    gain = norm_gain[None, :]
    *windows, halo_forward, halo_inverse = tables()
    held = pl.BlockSpec(memory_space=pltpu.VMEM)
    outside = pl.BlockSpec(memory_space=pl.ANY)
    words = channels * T

    def struct(*shape):
        return jax.ShapeDtypeStruct(shape, F32)

    def hbm(*shape):
        return pltpu.HBM(shape, F32)

    fields = [
        in_hbm(x) for x in (key_proj, value_proj, query_proj, second_query, second_key, medium_filter)
    ]
    rings = count // RING
    share = tiles // RING
    ring_groups = [[ring * RING + k for k in range(RING)] for ring in range(rings)]
    across_groups = [[ring * RING + k for ring in range(rings)] for k in range(RING)]
    place = lax.axis_index("seq").astype(jnp.int32).reshape(1)
    tail, own_rate = call(
        tail_kernel,
        [pl.BlockSpec(memory_space=pltpu.SMEM)] + [outside] * 4,
        [held] * 2,
        [struct(parts[0], TAPS, LANES), struct(share, MODES, LANES)],
        [pltpu.VMEM((parts[0] * LANES, LANES), F32)] * 2
        + [pltpu.VMEM((3, 3, channels), F32), pltpu.VMEM((share, MODES, LANES), F32)]
        + [pltpu.SemaphoreType.DMA((2,))] * 2
        + [pltpu.SemaphoreType.DMA, pltpu.SemaphoreType.DMA((share,))],
        words * 8,
        words * 6,
        "tail",
    )(place, fields[0], fields[1], in_hbm(short_t), in_hbm(rate_t))
    halo = from_behind(tail)

    *turned_fields, taps_t, rims, tail_two = call(
        prep_kernel,
        [outside] * 6 + [held] * 2,
        [held] * 8,
        [struct(tiles, T, LANES)] * 5
        + [struct(tiles, HEAD_ROWS, LANES), struct(RIMS, tiles, LANES)]
        + [struct(parts[1], TAPS, LANES)],
        [pltpu.VMEM((channels, T), F32)] * 5
        + [pltpu.VMEM((channels, TAPS), F32), pltpu.SemaphoreType.DMA((6, chunks))],
        words * 20,
        words * 40,
        "prep",
    )(*fields, short_t, own_rate)
    border = from_behind(rims)
    halo_two = from_behind(tail_two)

    early_rows = T + MAIN_ROWS
    (
        taps,
        tap_spectrum,
        medium,
        query,
        key2,
        leave_main,
        early,
    ) = call(
        local_kernel,
        [held] * (11 + len(windows)),
        [held] * 6 + [outside],
        [
            struct(tiles, HEAD_ROWS, LANES),
            struct(tiles, 384, LANES),
            struct(tiles, HEAD_ROWS, LANES),
            struct(tiles, HEAD_ROWS, LANES),
            struct(tiles, HEAD_ROWS, LANES),
            struct(tiles, MODES, LANES),
            hbm(tiles, early_rows, LANES),
        ],
        [pltpu.VMEM((T, group * LANES), F32)] * 2
        + [pltpu.VMEM((group, T, LANES), F32)] * 2
        + [pltpu.VMEM((group, MODES * SEG, LANES), F32)]
        + [pltpu.VMEM((tiles, early_rows, LANES), F32), pltpu.SemaphoreType.DMA((tiles,))],
        words * 8000,
        words * 60,
        "local",
    )(
        *turned_fields,
        taps_t,
        short_t,
        second_t,
        rate_t,
        amplitude,
        skip,
        *windows,
    )

    late_rows = HEAD_ROWS + MODES * SEG + MODES
    joined = ()
    for base, part in zip((0, parts[0]), (halo, halo_two)):
        here = part.shape[0]
        join_steps = min(here, 1 if base else 2)
        late_shape = (base + here, late_rows, LANES)
        scratch = [
            pltpu.VMEM((join_steps, HEAD_ROWS + 8, -(-here // join_steps) * LANES), F32),
            pltpu.VMEM((here, MODES * SEG, LANES), F32),
        ]
        if base:
            scratch.append(pltpu.VMEM((here, late_rows, LANES), F32))
            scratch.append(pltpu.SemaphoreType.DMA((here + 1,)))
        joined = call(
            functools.partial(join_kernel, base),
            [held] * (17 + len(joined)),
            [held, outside if base else held],
            [struct(base + here, MODES, LANES), (hbm if base else struct)(*late_shape)],
            scratch,
            here * 500 * T * LANES,
            here * 20 * T * LANES,
            "join",
        )(
            part,
            border,
            tap_spectrum,
            medium,
            taps,
            query,
            key2,
            turned_fields[0],
            turned_fields[1],
            leave_main,
            short_t,
            second_t,
            rate_t,
            amplitude,
            skip,
            halo_forward,
            halo_inverse,
            *joined,
        )
    state, late = joined

    share_shape = (RING, share, MODES, LANES)
    ring_states = exchange(state.reshape(share_shape), ring_groups)
    totals = call(
        ring_kernel,
        [held, held],
        held,
        struct(rings, share, MODES, LANES),
        [],
        count * LANES * 30,
        count * LANES * 8,
        "ring",
    )(ring_states, own_rate)
    scanned = call(
        scan_kernel,
        [pl.BlockSpec(memory_space=pltpu.SMEM), outside, held, held],
        held,
        struct(*share_shape),
        [pltpu.VMEM(share_shape, F32), pltpu.SemaphoreType.DMA],
        count * LANES * 30,
        count * LANES * 8,
        "scan",
    )(place, in_hbm(ring_states), exchange(totals, across_groups), own_rate)
    incoming = exchange(scanned, ring_groups).reshape(tiles, MODES, LANES)

    mixed, squares = call(
        finish_kernel,
        [held] + [outside] * 2 + [held] * 4,
        [held] * 2,
        [struct(tiles, T, LANES), struct(1, T)],
        [
            pltpu.VMEM((tiles, early_rows, LANES), F32),
            pltpu.VMEM((tiles, late_rows, LANES), F32),
            pltpu.VMEM((2, MODES * SEG, LANES), F32),
            pltpu.VMEM((T, LANES), F32),
            pltpu.SemaphoreType.DMA((2, 2 * chunks)),
        ],
        words * 40,
        words * 16,
        "finish",
    )(incoming, in_hbm(early), in_hbm(late), border, second_t, rate_t, gain)
    total = lax.psum(squares, "chan")
    return call(
        functools.partial(scale_kernel, float(channels * lax.axis_size("chan"))),
        [held, held],
        outside,
        struct(channels, T),
        [pltpu.VMEM((channels, T), F32), pltpu.SemaphoreType.DMA((chunks,))],
        words,
        words * 8,
        "scale",
    )(mixed, total)


def solution(mesh):
    return jax.shard_map(
        local,
        mesh=mesh,
        in_specs=(
            P("chan", "seq"),
            P("chan", "seq"),
            P("chan", "seq"),
            P("chan", "seq"),
            P("chan", "seq"),
            P(None, "chan", None),
            P(None, "chan", None),
            P("chan", None),
            P("chan", None),
            P("chan", None),
            P("chan"),
            P("chan"),
        ),
        out_specs=P("chan", "seq"),
        check_vma=False,
    )
```
